32 devices in a mesh: dp: 4 (over y, x), cp: 8 (over z, core).
Axes of the slice: x: 2, y: 2, z: 4, core: 2. Of those that a mesh axis runs over, the one named last changes fastest.
Arguments:
- tokens: bfloat16 [4096, 1536], P(('dp', 'cp')), may hold values from -6 to 6
- cotangent: bfloat16 [4096, 1536], P(('dp', 'cp')), may hold values from -6 to 6
- doc_lengths: int32 [4, 4], P('dp'), may hold values from 1 to 1021, as said below
- routes: int32 [2, 4096, 4], P(None, ('dp', 'cp')), may hold values from 0 to 15, all different within a row; in each aligned block of 128 rows (0 to 127, 128 to 255, ..., all dimensions but the last counted through in order) at most 64 rows name the same one
- w_qkv: bfloat16 [2, 2048, 1536], P(None, ('dp', 'cp')), may hold values from -0.15625 to 0.15625
- w_out: bfloat16 [2, 1536, 1536], P(None, ('dp', 'cp')), may hold values from -1.25 to 1.25
- router: bfloat16 [2, 1536, 16], P(None, ('dp', 'cp')), may hold values from -0.078125 to 0.078125
- gains: bfloat16 [2, 1536, 2], P(None, ('dp', 'cp')), may hold values from 0.5 to 1.5
- w_gate_up: bfloat16 [2, 16, 1536, 1536], P(None, 'cp', 'dp'), may hold values from -0.15625 to 0.15625
- w_down: bfloat16 [2, 16, 768, 1536], P(None, 'cp', 'dp'), may hold values from -0.625 to 0.625
Outputs:
- output: float32 [4096, 1536], P(('dp', 'cp'))
- token_grad: float32 [4096, 1536], P(('dp', 'cp'))
- qkv_grad: float32 [2, 2048, 1536], P(None, ('dp', 'cp'))
- out_proj_grad: float32 [2, 1536, 1536], P(None, ('dp', 'cp'))
- router_grad: float32 [2, 1536, 16], P(None, ('dp', 'cp'))
- gains_grad: float32 [2, 1536, 2], P(None, ('dp', 'cp'))
- gate_up_grad: float32 [2, 16, 1536, 1536], P(None, 'cp', 'dp')
- down_grad: float32 [2, 16, 768, 1536], P(None, 'cp', 'dp')
The draws below stay inside these ranges and needn't reach their ends.
Inputs may be any that keep to these rules, and one draw needn't show every extreme that they name: `routes`: in every layer each token names 4 different experts; among the rows of one device no expert is named by more than 64 tokens, and some device's rows reach that bound. `doc_lengths`: row b lists in order the lengths of the 4 documents packed into group b; they sum to 1024. Document 1 begins within the group's first 128 tokens and ends within its last 128; documents 0, 2 and 3 are shorter than 128. In one group documents 0, 2 and 3 have one token each.
All inputs are finite; a program needn't handle non-finite values.
Results may differ from the reference program's by a relative error of at most 0.033.
Values may be sent and summed in bfloat16 or wider, within the bound.
No kernel may reach another device: no remote copies, remote signals or barrier semaphores. Data moves between devices by JAX's collectives and lax.ppermute only.
A program may use at most 256 MiB of HBM per device.

```python
import math
import jax
import jax.numpy as jnp
import numpy as np
from jax import lax

D = 1536
HEADS = 12
KV_HEADS = 2
HEAD = 128
FF = 768
TOP = 4
LAYERS = 2
DOCS = 4
TOK_DEV = 128
HQ = 1536
KVW = 256
QKV = 2048
Q_PER_KV = 6
EXPERTS = 16
CAP = 64
GROUP_TOKENS = 1024
GROUPS = 4
TOKENS = 4096


def draw_doc_lengths(key, part):
    key = jax.random.fold_in(key, 7)
    opening_key, middle_key, closing_key, group_key = jax.random.split(key, 4)
    opening = jax.random.randint(opening_key, (GROUPS, 1), 1, TOK_DEV // 2 + 1)
    third_length = jax.random.randint(middle_key, (GROUPS, 1), 1, TOK_DEV // 4 + 1)
    fourth = jax.random.randint(closing_key, (GROUPS, 1), 1, TOK_DEV // 4 + 1)
    single_group = jax.random.randint(group_key, (), 0, GROUPS)
    is_single = (jnp.arange(GROUPS, dtype=jnp.int32) == single_group)[:, None]
    opening = jnp.where(is_single, 1, opening)
    third_length = jnp.where(is_single, 1, third_length)
    fourth = jnp.where(is_single, 1, fourth)
    longest = GROUP_TOKENS - opening - third_length - fourth
    return jnp.concatenate([opening, longest, third_length, fourth], axis=1).astype(jnp.int32)


def steps_of(own_key, dims, cuts, smallest, high):
    level, own = 1.0, jax.random.fold_in(own_key, 6)
    for axis_at, blocks in cuts:
        steps = jnp.exp(jax.random.uniform(jax.random.fold_in(own, axis_at), (blocks,), jnp.float32, smallest / len(cuts), high / len(cuts)))
        level = level * jnp.repeat(steps, dims[axis_at] // blocks).reshape([-1 if axis == axis_at else 1 for axis in range(len(dims))])
    return level


def shared_out(key, own, number, rows, number_of, top, limit, skew):
    sequence = jax.random.permutation(key, number_of)
    heavy_load, common = load_shares(number_of, rows * top, limit, skew, True), load_shares(number_of, rows * top, limit, skew, False)
    places = jnp.arange(number_of)

    def named(lengths, rotation):
        used = int((lengths > 0).sum())
        fixed = max(1, used // 4)
        shifted = fixed + (places - fixed + rotation * (used - fixed)) % max(1, number_of - fixed)
        return jnp.zeros((number_of,), jnp.int32).at[sequence[jnp.where(places < fixed, places, shifted)]].set(jnp.asarray(lengths, jnp.int32))

    lengths = jnp.where(number % 4 == 0, named(heavy_load, number // 4), named(common, number - number // 4 - 1))
    mixed = jax.random.permutation(jax.random.fold_in(own, 3), number_of)
    giver, taker = mixed[0:number_of // 2 * 2:2], mixed[1:number_of // 2 * 2:2]
    slack = jnp.minimum(lengths[giver] - 1, limit - lengths[taker]) // 2
    slack = jnp.where((giver == sequence[0]) | (taker == sequence[0]) | (lengths[taker] == 0), 0, jnp.maximum(slack, 0))
    shifted = jax.random.randint(jax.random.fold_in(own, 4), (number_of // 2,), 0, 1 << 20) % (slack + 1)
    lengths = lengths.at[giver].add(-shifted).at[taker].add(shifted)
    labels = jnp.searchsorted(jnp.cumsum(lengths), jnp.arange(rows * top), side="right").astype(jnp.int32)
    grid = labels.reshape(top, rows).T
    grid = grid[jax.random.permutation(jax.random.fold_in(own, 1), rows)]
    rotation = jax.random.randint(jax.random.fold_in(own, 2), (rows, 1), 0, top)
    return jnp.take_along_axis(grid, (jnp.arange(top)[None, :] + rotation) % top, axis=1)


def load_shares(number_of, total, reach, lean, full):
    weights = [(1 << 20) // math.isqrt(grade ** lean) + 1 for grade in range(1, number_of + 1)]
    largest = reach if full else min(reach, max(-(-total // number_of), total * weights[0] // sum(weights)))
    least = 1 if total - largest >= number_of - 1 else 0
    holding, spare = [largest] + [least] * (number_of - 1), total - largest - least * (number_of - 1)
    while spare > 0:
        candidates = [i for i in range(1, number_of) if holding[i] < largest] or [i for i in range(1, number_of) if holding[i] < reach]
        mass, remaining = sum([weights[i] for i in candidates]), spare
        for i in candidates:
            extra = min(reach - holding[i], max(1, remaining * weights[i] // mass), spare)
            holding[i] = holding[i] + extra
            spare = spare - extra
    return np.array(holding)


def bell_draw(key, shape, width, limit, shards=(), held_as=jnp.bfloat16):
    result = jax.random.normal(key, shape, jnp.float32) * width
    if len(shards) > 0:
        result = steps_of(key, shape, shards, -0.22, 0.18) * result
    return jnp.clip(result, min=-limit, max=limit).astype(held_as)


def setup_inputs(seed: int = 0) -> dict:
    streams_of = jax.random.split(jax.random.key(seed), 11)
    tokens = bell_draw(streams_of[0], (TOKENS, D), 1.0, 6.0, ((0, 32),))
    cotangent = bell_draw(streams_of[1], (TOKENS, D), 1.0, 6.0, ((0, 32),))
    doc_lengths = draw_doc_lengths(jax.random.fold_in(streams_of[10], 71), 0)
    routes_keys = jax.random.split(jax.random.fold_in(streams_of[3], 1), LAYERS * TOKENS // TOK_DEV)
    routes_turns = jax.random.permutation(jax.random.fold_in(streams_of[3], 3), LAYERS * TOKENS // TOK_DEV)
    routes = jax.vmap(lambda own, number: shared_out(jax.random.fold_in(streams_of[3], 2), own, number, TOK_DEV, EXPERTS, TOP, CAP, 2))(routes_keys, routes_turns).reshape((LAYERS, TOKENS, TOP))
    w_qkv = bell_draw(streams_of[4], (LAYERS, QKV, D), D ** -0.5, 0.15625, ((1, 32),))
    w_out = bell_draw(streams_of[5], (LAYERS, HQ, D), (HQ // 64) ** -0.5, 1.25, ((1, 32),))
    router = bell_draw(streams_of[6], (LAYERS, D, EXPERTS), (4 * D) ** -0.5, 0.078125, ((1, 32),))
    gains = jnp.clip(1.0 + 0.1 * jax.random.normal(streams_of[7], (LAYERS, D, 2), jnp.float32), 0.5, 1.5).astype(jnp.bfloat16)
    w_gate_up = bell_draw(streams_of[8], (LAYERS, EXPERTS, D, 2 * FF), D ** -0.5, 0.15625, ((1, 8), (2, 4)))
    w_down = bell_draw(streams_of[9], (LAYERS, EXPERTS, FF, D), (FF // 8) ** -0.5, 0.625, ((1, 8), (2, 4)))
    return dict(tokens=tokens, cotangent=cotangent, doc_lengths=doc_lengths, routes=routes, w_qkv=w_qkv, w_out=w_out, router=router, gains=gains, w_gate_up=w_gate_up, w_down=w_down)


@jax.custom_vjp
def low(v):
    return lax.optimization_barrier(v.astype(jnp.bfloat16)).astype(jnp.float32)

@jax.custom_vjp
def low_back(v):
    return v

def low_keep(v):
    return (low(v), None)

def low_pass(kept, grad):
    return (grad,)

def back_keep(v):
    return (v, None)

def back_low(kept, grad):
    return (low(grad),)
low.defvjp(low_keep, low_pass)
low_back.defvjp(back_keep, back_low)
EPSILON = 1e-06
MASKED = -1e+30
HIGHEST = lax.Precision.HIGHEST

def inverse_rms(values):
    return lax.rsqrt(lax.optimization_barrier(jnp.mean(values * values, axis=-1, keepdims=True)) + EPSILON)

def doc_places(token_index, lengths_row):
    starts = (jnp.cumsum(lengths_row) - lengths_row).astype(jnp.int32)
    segment = lax.optimization_barrier(jnp.sum((token_index[:, None] >= starts[None, 1:]).astype(jnp.int32), axis=1)).astype(jnp.int32)
    picked = segment[:, None] == jnp.arange(DOCS, dtype=jnp.int32)[None, :]
    offset = lax.optimization_barrier(jnp.sum(jnp.where(picked, starts[None, :], 0), axis=1)).astype(jnp.int32)
    return (segment, (token_index - offset).astype(jnp.int32))

def rope_tables(positions):
    half_width = HEAD // 2
    frequency = jnp.exp(-jnp.log(10000.0) * 2.0 * jnp.arange(half_width, dtype=jnp.float32) / HEAD)
    angles = positions.astype(jnp.float32)[:, None] * frequency[None, :]
    return (jnp.cos(angles)[:, None, :], jnp.sin(angles)[:, None, :])

def rotate(values, cosine, sine_table):
    half_width = values.shape[-1] // 2
    former = values[..., :half_width]
    latter = values[..., half_width:]
    return jnp.concatenate([former * cosine - latter * sine_table, latter * cosine + former * sine_table], axis=-1)

def group_attention(inputs_group):
    queries, key_heads, value_heads, segment = inputs_group
    token_order = jnp.arange(GROUP_TOKENS, dtype=jnp.int32)
    allowed = (segment[:, None] == segment[None, :]) & (token_order[None, :] <= token_order[:, None])
    scores = low_back(jnp.einsum('tkgh,ukh->kgtu', queries, key_heads, precision=HIGHEST) * HEAD ** (-0.5))
    scores = jnp.where(allowed[None, None], scores, MASKED)
    top_score = lax.optimization_barrier(jnp.max(scores, axis=-1, keepdims=True))
    log_total = top_score + jnp.log(lax.optimization_barrier(jnp.sum(jnp.exp(scores - top_score), axis=-1, keepdims=True)))
    weights = low(jnp.exp(scores - log_total))
    mixed = jnp.einsum('kgtu,ukh->tkgh', weights, value_heads, precision=HIGHEST)
    return mixed.reshape(GROUP_TOKENS, HQ)

def route_tables(route_layer):
    block_count = TOKENS // TOK_DEV
    flat_routes = route_layer.reshape(block_count, TOK_DEV * TOP)
    matches = (flat_routes[:, :, None] == jnp.arange(EXPERTS, dtype=jnp.int32)[None, None, :]).astype(jnp.int32)
    earlier = jnp.cumsum(matches, axis=1).astype(jnp.int32) - matches
    position = lax.optimization_barrier(jnp.sum(earlier * matches, axis=2)).astype(jnp.int32)
    block_base = (jnp.arange(block_count, dtype=jnp.int32) * CAP)[:, None]
    slot_index = (flat_routes * (block_count * CAP) + block_base + position).astype(jnp.int32)
    route_token = (jnp.arange(TOKENS * TOP, dtype=jnp.int32) // TOP).astype(jnp.int32)
    expert_source = jnp.full((EXPERTS * block_count * CAP,), TOKENS, jnp.int32)
    expert_source = expert_source.at[slot_index.reshape(-1)].set(route_token)
    chosen = matches.reshape(TOKENS, TOP, EXPERTS).astype(jnp.float32)
    return (slot_index.reshape(TOKENS, TOP), expert_source.reshape(EXPERTS, block_count * CAP), chosen)

def block_layer(layer_input, query_weight, output_weight, router_weight, gain_pair, gate_up_all, down_all, segment, cosine, sine_table, tables):
    slot_index, expert_source, chosen = tables
    normed = low(layer_input * inverse_rms(layer_input) * gain_pair[:, 0])
    joined = low_back(jnp.dot(normed, query_weight.T, precision=HIGHEST))
    queries = low(rotate(joined[:, :HQ].reshape(TOKENS, HEADS, HEAD), cosine, sine_table))
    key_heads = low(rotate(joined[:, HQ:HQ + KVW].reshape(TOKENS, KV_HEADS, HEAD), cosine, sine_table))
    value_heads = low(joined[:, HQ + KVW:].reshape(TOKENS, KV_HEADS, HEAD))
    attended = lax.map(jax.checkpoint(group_attention), (queries.reshape(GROUPS, GROUP_TOKENS, KV_HEADS, Q_PER_KV, HEAD), key_heads.reshape(GROUPS, GROUP_TOKENS, KV_HEADS, HEAD), value_heads.reshape(GROUPS, GROUP_TOKENS, KV_HEADS, HEAD), segment.reshape(GROUPS, GROUP_TOKENS)))
    attended = low(low_back(attended.reshape(TOKENS, HQ)))
    middle = layer_input + low_back(jnp.dot(attended, output_weight, precision=HIGHEST))
    mixed = low(middle * inverse_rms(middle) * gain_pair[:, 1])
    logits = jnp.dot(mixed, router_weight, precision=HIGHEST)
    picked = lax.optimization_barrier(jnp.sum(logits[:, None, :] * chosen, axis=-1))
    gate_values = jax.nn.softmax(picked, axis=-1)
    padded = jnp.concatenate([mixed, jnp.zeros((1, D), jnp.float32)], axis=0)

    def one_expert(expert_inputs):
        source_rows, gate_up_weight, down_weight = expert_inputs
        arrived = low_back(padded[source_rows])
        gate_up = low_back(jnp.dot(arrived, gate_up_weight, precision=HIGHEST))
        hidden = low(jax.nn.silu(gate_up[:, :FF]) * gate_up[:, FF:])
        return low(low_back(jnp.dot(hidden, down_weight, precision=HIGHEST)))
    produced = lax.map(jax.checkpoint(one_expert), (expert_source, gate_up_all, down_all))
    expert_rows = produced.reshape(-1, D)[slot_index]
    return middle + lax.optimization_barrier(jnp.sum(gate_values[:, :, None] * expert_rows, axis=1))

def reference(tokens, cotangent, doc_lengths, routes, w_qkv, w_out, router, gains, w_gate_up, w_down):
    local_index = (jnp.arange(TOKENS, dtype=jnp.int32) % GROUP_TOKENS).astype(jnp.int32).reshape(GROUPS, GROUP_TOKENS)
    segment, position = jax.vmap(doc_places)(local_index, doc_lengths)
    cosine, sine_table = rope_tables(position.reshape(TOKENS))
    segment = segment.reshape(TOKENS)
    tables = [route_tables(routes[layer_index]) for layer_index in range(LAYERS)]

    def forward(layer_value, qkv_all, out_all, router_all, gains_all, gate_up_all, down_all):
        for layer_index in range(LAYERS):
            layer_value = block_layer(layer_value, qkv_all[layer_index], out_all[layer_index], router_all[layer_index], gains_all[layer_index], gate_up_all[layer_index], down_all[layer_index], segment, cosine, sine_table, tables[layer_index])
        return layer_value
    floats = (tokens.astype(jnp.float32), w_qkv.astype(jnp.float32), w_out.astype(jnp.float32), router.astype(jnp.float32), gains.astype(jnp.float32), w_gate_up.astype(jnp.float32), w_down.astype(jnp.float32))
    output, pull_back = jax.vjp(forward, *floats)
    gradients = pull_back(cotangent.astype(jnp.float32))
    return (output, gradients[0], gradients[1], gradients[2], gradients[3], gradients[4], gradients[5], gradients[6])
```

```python
import jax
import jax.numpy as jnp
from jax import lax
from jax.sharding import PartitionSpec as P

D = 1536
HEADS = 12
KV_HEADS = 2
HEAD = 128
FF = 768
TOP = 4
EXP_DEV = 2
LAYERS = 2
DOCS = 4
HQ = 1536
KVW = 256
QKV = 2048
Q_PER_KV = 6

EPSILON = 1e-06
MASKED = -1e30
LOW = jnp.bfloat16
WIDE = jnp.float32


def inverse_rms(values):
    return lax.rsqrt(jnp.mean(values * values, axis=-1, keepdims=True) + EPSILON)


def norm_backward(values, gain, upstream):
    scale_rows = inverse_rms(values)
    weighted = gain * upstream
    inner_mean = jnp.mean(values * weighted, axis=-1, keepdims=True)
    grad_values = scale_rows * weighted - values * scale_rows * scale_rows * scale_rows * inner_mean
    grad_gain = jnp.sum(values * scale_rows * upstream, axis=0)
    return (grad_values, grad_gain)


def doc_places(token_index, lengths_row):
    starts = jnp.cumsum(lengths_row) - lengths_row
    segment = jnp.sum((token_index[:, None] >= starts[None, 1:]).astype(jnp.int32), axis=1)
    picked = segment[:, None] == jnp.arange(DOCS, dtype=jnp.int32)[None, :]
    offset = jnp.sum(jnp.where(picked, starts[None, :], 0), axis=1)
    return (segment, token_index - offset)


def rope_tables(positions):
    half_width = HEAD // 2
    frequency = jnp.exp(-jnp.log(10000.0) * 2.0 * jnp.arange(half_width, dtype=WIDE) / HEAD)
    angles = positions.astype(WIDE)[:, None] * frequency[None, :]
    return (jnp.cos(angles)[:, None, :], jnp.sin(angles)[:, None, :])


def rotate(values, cosine, sine_table):
    half_width = values.shape[-1] // 2
    former = values[..., :half_width]
    latter = values[..., half_width:]
    return jnp.concatenate(
        [former * cosine - latter * sine_table, latter * cosine + former * sine_table], axis=-1
    )


def heads_first(values):
    token_rows = values.shape[0]
    shaped = values.reshape(token_rows, KV_HEADS, Q_PER_KV, HEAD).transpose(1, 2, 0, 3)
    return shaped.reshape(KV_HEADS, Q_PER_KV * token_rows, HEAD)


def heads_last(values):
    token_rows = values.shape[1] // Q_PER_KV
    shaped = values.reshape(KV_HEADS, Q_PER_KV, token_rows, HEAD).transpose(2, 0, 1, 3)
    return shaped.reshape(token_rows, HQ)


def dot(left, right):
    return jnp.dot(left, right, preferred_element_type=WIDE)


def dot_t(left, right):
    return lax.dot_general(left, right, (((1,), (1,)), ((), ())), preferred_element_type=WIDE)


def t_dot(left, right):
    return lax.dot_general(left, right, (((0,), (0,)), ((), ())), preferred_element_type=WIDE)


def after(value, *earlier):
    return lax.optimization_barrier((value, *earlier))[0]


LINE = 4


def swap_core(value):
    return lax.ppermute(value, "cp", [(i, i ^ 1) for i in range(2 * LINE)])


def hop(value, upward, sources):
    step = 1 if upward else -1
    pairs = [(2 * z + core, 2 * (z + step) + core) for z in sources for core in range(2)]
    return lax.ppermute(value, "cp", pairs)


def across(value, flip):
    return lax.ppermute(value, "dp", [(i, i ^ flip) for i in range(4)])


def line_gather(value):
    place = lax.axis_index("cp") // 2
    rising, falling = value, value
    risen, fallen = [], []
    for step in range(1, LINE):
        rising = hop(rising, True, range(step - 1, LINE - 1))
        falling = hop(falling, False, range(1, LINE - step + 1))
        risen.insert(0, rising)
        fallen.append(falling)
    every = jnp.stack(risen + [value] + fallen)
    return lax.dynamic_slice_in_dim(every, LINE - 1 - place, LINE, 0)


def line_scatter(parts):
    place = lax.axis_index("cp") // 2

    def pick(index):
        return lax.dynamic_index_in_dim(parts, jnp.clip(index, 0, LINE - 1), 0, keepdims=False)

    rising = falling = None
    for step in range(1, LINE):
        up = pick(LINE + place - step)
        down = pick(place - LINE + step)
        if step > 1:
            up = (up.astype(WIDE) + rising.astype(WIDE)).astype(LOW)
            down = (down.astype(WIDE) + falling.astype(WIDE)).astype(LOW)
        rising = hop(up, True, range(step))
        falling = hop(down, False, range(LINE - step, LINE))
    return pick(place).astype(WIDE) + rising.astype(WIDE) + falling.astype(WIDE)


def square_gather(value):
    half = value.shape[0] // 2
    by_x = across(value, 1)
    by_y = across(value, 2)
    far = jnp.concatenate([across(by_x[:half], 2), across(by_y[half:], 1)], axis=0)
    return (value, by_x, by_y, far)


def square_scatter(piece):
    far = piece(3)
    half = far.shape[0] // 2
    from_x = across(far[:half], 1)
    from_y = across(far[half:], 2)
    to_x, to_y = piece(1), piece(2)
    to_x = jnp.concatenate(
        [to_x[:half], (to_x[half:].astype(WIDE) + from_y.astype(WIDE)).astype(LOW)], axis=0
    )
    to_y = jnp.concatenate(
        [(to_y[:half].astype(WIDE) + from_x.astype(WIDE)).astype(LOW), to_y[half:]], axis=0
    )
    got_x = across(to_x, 1)
    got_y = across(to_y, 2)
    return piece(0).astype(WIDE) + got_x.astype(WIDE) + got_y.astype(WIDE)


class SquareLine:
    def order(self, rows):
        core = lax.axis_index("cp") % 2
        blocks = jnp.concatenate(
            [2 * jnp.arange(LINE) + core, 2 * jnp.arange(LINE) + 1 - core]
        ).astype(jnp.int32)
        return (blocks[:, None] * rows + jnp.arange(rows, dtype=jnp.int32)[None, :]).reshape(-1)

    def group_gather(self, value):
        mine = line_gather(value)
        other = swap_core(mine)
        return jnp.concatenate([mine, other], axis=0).reshape(-1, *value.shape[1:])

    def group_scatter(self, terms):
        parts = terms.astype(LOW).reshape(2, LINE, -1, *terms.shape[1:])
        other = swap_core(parts[1])
        return line_scatter((parts[0].astype(WIDE) + other.astype(WIDE)).astype(LOW))

    def expert_gather(self, block):
        place = lax.axis_index("dp")
        pieces = square_gather(block)
        whole = jnp.zeros((block.shape[0], 4, *block.shape[1:]), block.dtype)
        for flip, part in enumerate(pieces):
            whole = lax.dynamic_update_slice_in_dim(whole, part[:, None], place ^ flip, 1)
        return whole.reshape(block.shape[0], 4 * block.shape[1], *block.shape[2:])

    def expert_scatter(self, terms):
        place = lax.axis_index("dp")
        parts = terms.reshape(terms.shape[0], 4, -1, *terms.shape[2:])
        return square_scatter(
            lambda flip: lax.dynamic_index_in_dim(parts, place ^ flip, 1, keepdims=False)
        )

    def dense_gather(self, block):
        place = lax.axis_index("dp")
        core = lax.axis_index("cp") % 2
        rows = block.shape[0]
        whole = jnp.zeros((4, LINE, 2, *block.shape), block.dtype)
        for flip, part in enumerate(square_gather(line_gather(block))):
            other = swap_core(part)
            for held, side in ((part, core), (other, 1 - core)):
                whole = lax.dynamic_update_slice(
                    whole, held[None, :, None], (place ^ flip, 0, side, 0, 0)
                )
        return whole.reshape(8 * LINE * rows, *block.shape[1:])

    def dense_scatter(self, terms):
        place = lax.axis_index("dp")
        core = lax.axis_index("cp") % 2
        parts = terms.astype(LOW).reshape(4, LINE, 2, -1, *terms.shape[1:])
        mine = lax.dynamic_index_in_dim(parts, core, 2, keepdims=False)
        other = swap_core(lax.dynamic_index_in_dim(parts, 1 - core, 2, keepdims=False))
        both = (mine.astype(WIDE) + other.astype(WIDE)).astype(LOW)
        plane = square_scatter(
            lambda flip: lax.dynamic_index_in_dim(both, place ^ flip, 0, keepdims=False)
        )
        return line_scatter(plane.astype(LOW))


class AnyMesh:
    def order(self, rows):
        return jnp.arange(lax.axis_size("cp") * rows, dtype=jnp.int32)

    def group_gather(self, value):
        return lax.all_gather(value, "cp", axis=0, tiled=True)

    def group_scatter(self, terms):
        return lax.psum_scatter(
            terms.astype(LOW), "cp", scatter_dimension=0, tiled=True
        ).astype(WIDE)

    def expert_gather(self, block):
        return lax.all_gather(block, "dp", axis=1, tiled=True)

    def expert_scatter(self, terms):
        return lax.psum_scatter(terms, "dp", scatter_dimension=1, tiled=True).astype(WIDE)

    def dense_gather(self, block):
        return lax.all_gather(block, ("dp", "cp"), axis=0, tiled=True)

    def dense_scatter(self, terms):
        return lax.psum_scatter(
            terms.astype(LOW), ("dp", "cp"), scatter_dimension=0, tiled=True
        ).astype(WIDE)


def shards(tokens, cotangent, doc_lengths, routes, w_qkv, w_out, router, gains, w_gate_up, w_down):
    dp_size = lax.axis_size("dp")
    cp_size = lax.axis_size("cp")
    device_count = dp_size * cp_size
    move = SquareLine() if (dp_size, cp_size) == (4, 2 * LINE) else AnyMesh()
    row_count = tokens.shape[0]
    group_rows = row_count * cp_size
    cycle_place = lax.axis_index("cp")
    expert_count = EXP_DEV * cp_size
    lengths_row = doc_lengths[0]
    my_index = cycle_place * row_count + jnp.arange(row_count, dtype=jnp.int32)
    my_segment, my_position = doc_places(my_index, lengths_row)
    cosine, sine_table = rope_tables(my_position)
    score_scale = HEAD ** (-0.5)
    key_index = move.order(row_count)
    key_segment, unused_position = doc_places(key_index, lengths_row)
    allowed = (my_segment[:, None] == key_segment[None, :]) & (
        key_index[None, :] <= my_index[:, None]
    )
    allowed = jnp.tile(allowed, (Q_PER_KV, 1))[None]

    part_rows = router.shape[1]
    small_width = expert_count + 2
    small = jnp.concatenate([router, gains], axis=2).reshape(-1)
    small_size = small.shape[0]
    small = jnp.pad(small, (0, -small_size % 2048)).reshape(-1, 128)
    small = lax.all_gather(small, ("dp", "cp"), axis=0, tiled=False).reshape(device_count, -1)
    small = small[:, :small_size].reshape(device_count, LAYERS, part_rows, small_width)
    small = small.transpose(1, 0, 2, 3).reshape(LAYERS, D, small_width)
    router_all = small[:, :, :expert_count]
    gains_all = small[:, :, expert_count:].astype(WIDE)
    route_block = routes.reshape(-1, 128)
    route_blocks = lax.all_gather(route_block, "cp", axis=0, tiled=False)
    route_blocks = route_blocks.reshape(cp_size, LAYERS, row_count, TOP)
    route_rows = route_blocks.transpose(1, 0, 2, 3).reshape(LAYERS, group_rows, TOP)
    expert_ids = jnp.arange(expert_count, dtype=jnp.int32)

    weights = []
    for layer in range(LAYERS):
        query_weight = move.dense_gather(w_qkv[layer])
        output_weight = move.dense_gather(w_out[layer])
        gate_up_weight = move.expert_gather(w_gate_up[layer])
        down_weight = move.expert_gather(w_down[layer])
        weights.append((query_weight, output_weight, gate_up_weight, down_weight))
    cotangent_group = move.group_gather(cotangent)

    def norm_rows(values, gain):
        return (values * inverse_rms(values) * gain).astype(LOW)

    def forward_layer(layer, layer_value):
        query_weight, output_weight, gate_up_weight, down_weight = weights[layer]
        normed = norm_rows(layer_value, gains_all[layer, :, 0])
        joined = dot_t(normed, query_weight)
        queries = rotate(joined[:, :HQ].reshape(row_count, HEADS, HEAD), cosine, sine_table)
        keys = rotate(
            joined[:, HQ : HQ + KVW].reshape(row_count, KV_HEADS, HEAD), cosine, sine_table
        )
        queries = heads_first(queries.reshape(row_count, HQ).astype(LOW))
        keys_values = jnp.concatenate(
            [keys.reshape(row_count, KVW), joined[:, HQ + KVW :]], axis=1
        ).astype(LOW)
        keys_values = move.group_gather(keys_values)
        key_heads = keys_values[:, :KVW].reshape(group_rows, KV_HEADS, HEAD)
        value_heads = keys_values[:, KVW:].reshape(group_rows, KV_HEADS, HEAD)
        scores = (
            jnp.einsum("kqh,nkh->kqn", queries, key_heads, preferred_element_type=WIDE)
            * score_scale
        )
        scores = jnp.where(allowed, scores, MASKED)
        top_score = jnp.max(scores, axis=-1, keepdims=True)
        shares = jnp.exp(scores - top_score)
        total = jnp.sum(shares, axis=-1, keepdims=True)
        probs = (shares / total).astype(LOW)
        attended = jnp.einsum("kqn,nkh->kqh", probs, value_heads, preferred_element_type=WIDE)
        attended = heads_last(attended)
        attended_low = attended.astype(LOW)
        middle = layer_value + dot(attended_low, output_weight)
        mixed = norm_rows(middle, gains_all[layer, :, 1])
        mixed_group = move.group_gather(mixed)
        route_group = jnp.take(
            route_rows[layer].reshape(cp_size, row_count, TOP),
            key_index[::row_count] // row_count,
            axis=0,
        ).reshape(group_rows, TOP)
        chosen = jnp.any(route_group[:, :, None] == expert_ids[None, None, :], axis=1)
        logits = jnp.where(chosen, dot(mixed_group, router_all[layer]), MASKED)
        gates = jax.nn.softmax(logits, axis=-1)
        own_gates = lax.dynamic_slice_in_dim(gates, EXP_DEV * cycle_place, EXP_DEV, 1)
        gate_up = [dot(mixed_group, gate_up_weight[e]).astype(LOW) for e in range(EXP_DEV)]
        hidden = []
        for e in range(EXP_DEV):
            gate_part = gate_up[e][:, :FF].astype(WIDE)
            up_part = gate_up[e][:, FF:].astype(WIDE)
            hidden.append(jax.nn.silu(gate_part) * up_part * own_gates[:, e : e + 1])
        hidden = jnp.concatenate(hidden, axis=1).astype(LOW)
        terms = dot(hidden, down_weight.reshape(EXP_DEV * FF, D))
        result = middle + move.group_scatter(terms)
        kept = (
            layer_value,
            normed,
            queries,
            keys_values,
            probs,
            attended,
            middle,
            mixed_group,
            gates,
            own_gates,
            gate_up,
            hidden,
        )
        return (result, kept)

    def backward_layer(layer, upstream, upstream_group, kept):
        query_weight, output_weight, gate_up_weight, down_weight = weights[layer]
        (
            layer_value,
            normed,
            queries,
            keys_values,
            probs,
            attended,
            middle,
            mixed_group,
            gates,
            own_gates,
            gate_up,
            hidden,
        ) = kept
        grad_hidden = dot_t(upstream_group, down_weight.reshape(EXP_DEV * FF, D))
        grad_gate_up = []
        grad_gates = []
        for e in range(EXP_DEV):
            gate_part = gate_up[e][:, :FF].astype(WIDE)
            up_part = gate_up[e][:, FF:].astype(WIDE)
            bare = grad_hidden[:, e * FF : (e + 1) * FF]
            logistic = jax.nn.sigmoid(gate_part)
            activated = gate_part * logistic
            grad_gates.append(jnp.sum(bare * activated * up_part, axis=1, keepdims=True))
            gated = bare * own_gates[:, e : e + 1]
            grad_gate = gated * up_part * logistic * (1.0 + gate_part * (1.0 - logistic))
            grad_gate_up.append(
                jnp.concatenate([grad_gate, gated * activated], axis=1).astype(LOW)
            )
        own_terms = own_gates * jnp.concatenate(grad_gates, axis=1)
        own_ids = EXP_DEV * cycle_place + jnp.arange(EXP_DEV, dtype=jnp.int32)
        placed = jnp.sum(
            jnp.where(own_ids[None, :, None] == expert_ids[None, None, :], own_terms[:, :, None], 0.0),
            axis=1,
        )
        grad_logits = (placed - jnp.sum(own_terms, axis=1, keepdims=True) * gates).astype(LOW)
        terms = dot_t(grad_gate_up[0], gate_up_weight[0]) + dot_t(
            grad_gate_up[1], gate_up_weight[1]
        )
        terms = terms + dot_t(grad_logits, router_all[layer])
        grad_mixed = move.group_scatter(terms)
        grad_router = t_dot(mixed_group, grad_logits)
        grad_gate_up_weight = jnp.stack(
            [t_dot(mixed_group, grad_gate_up[e]).astype(LOW) for e in range(EXP_DEV)]
        )
        grad_down_weight = t_dot(hidden, upstream_group).astype(LOW).reshape(EXP_DEV, FF, D)
        expert_grads = (
            move.expert_scatter(grad_gate_up_weight),
            move.expert_scatter(grad_down_weight),
        )

        grad_middle, grad_second_gain = norm_backward(
            middle, gains_all[layer, :, 1], grad_mixed
        )
        grad_middle = grad_middle + upstream
        grad_middle_low = grad_middle.astype(LOW)
        grad_output_weight = move.dense_scatter(t_dot(attended.astype(LOW), grad_middle_low))
        grad_attended = dot_t(grad_middle_low, output_weight).astype(LOW)
        grad_heads = heads_first(grad_attended)
        delta = jnp.sum(grad_heads.astype(WIDE) * heads_first(attended), axis=-1, keepdims=True)
        key_heads = keys_values[:, :KVW].reshape(group_rows, KV_HEADS, HEAD)
        value_heads = keys_values[:, KVW:].reshape(group_rows, KV_HEADS, HEAD)
        grad_probs = jnp.einsum(
            "kqh,nkh->kqn", grad_heads, value_heads, preferred_element_type=WIDE
        )
        grad_scores = (probs.astype(WIDE) * (grad_probs - delta) * score_scale).astype(LOW)
        grad_queries = jnp.einsum(
            "kqn,nkh->kqh", grad_scores, key_heads, preferred_element_type=WIDE
        )
        grad_keys = jnp.einsum(
            "kqn,kqh->nkh", grad_scores, queries, preferred_element_type=WIDE
        )
        grad_values = jnp.einsum(
            "kqn,kqh->nkh", probs, grad_heads, preferred_element_type=WIDE
        )
        grad_keys_values = move.group_scatter(
            jnp.concatenate(
                [grad_keys.reshape(group_rows, KVW), grad_values.reshape(group_rows, KVW)], axis=1
            )
        )
        grad_queries = rotate(
            heads_last(grad_queries).reshape(row_count, HEADS, HEAD), cosine, -sine_table
        ).reshape(row_count, HQ)
        grad_keys = rotate(
            grad_keys_values[:, :KVW].reshape(row_count, KV_HEADS, HEAD), cosine, -sine_table
        ).reshape(row_count, KVW)
        grad_joined = jnp.concatenate(
            [grad_queries, grad_keys, grad_keys_values[:, KVW:]], axis=1
        ).astype(LOW)
        grad_query_weight = t_dot(grad_joined, normed)
        grad_normed = dot(grad_joined, query_weight)
        grad_input, grad_first_gain = norm_backward(
            layer_value, gains_all[layer, :, 0], grad_normed
        )
        grad_input = grad_input + grad_middle
        small_terms = jnp.concatenate(
            [grad_router, grad_first_gain[:, None], grad_second_gain[:, None]], axis=1
        )
        return (grad_input, grad_query_weight, grad_output_weight, expert_grads, small_terms)

    layer_value = tokens.astype(WIDE)
    stored = []
    for layer in range(LAYERS):
        layer_value, kept = forward_layer(layer, layer_value)
        stored.append(kept)
    upstream = cotangent.astype(WIDE)
    upstream_group = cotangent_group
    query_grads, output_grads, expert_grads, small_terms = ([None] * LAYERS for _ in range(4))
    for layer in reversed(range(LAYERS)):
        if layer < LAYERS - 1:
            upstream_group = move.group_gather(upstream.astype(LOW))
        upstream, query_terms, output_grads[layer], expert_grads[layer], small_terms[layer] = (
            backward_layer(layer, upstream, upstream_group, stored[layer])
        )
        if layer > 0:
            query_grads[layer] = move.dense_scatter(query_terms)
    small_grads = jnp.stack(small_terms).reshape(LAYERS, device_count, part_rows, small_width)
    small_grads = small_grads.transpose(1, 0, 2, 3).reshape(device_count, -1)
    small_size = small_grads.shape[1]
    extra_rows = -(-small_size // (8 * D)) * 8
    small_grads = jnp.pad(small_grads, ((0, 0), (0, extra_rows * D - small_size)))
    query_rows = query_terms.shape[0] // device_count
    last_terms = jnp.concatenate(
        [
            query_terms.astype(LOW).reshape(device_count, query_rows, D),
            small_grads.astype(LOW).reshape(device_count, extra_rows, D),
        ],
        axis=1,
    )
    last_grads = move.dense_scatter(last_terms.reshape(-1, D))
    query_grads[0] = last_grads[:query_rows]
    small_grads = last_grads[query_rows:].reshape(-1)[:small_size]
    small_grads = small_grads.reshape(LAYERS, part_rows, small_width)
    return (
        layer_value,
        upstream,
        jnp.stack(query_grads),
        jnp.stack(output_grads),
        small_grads[:, :, :expert_count],
        small_grads[:, :, expert_count:],
        jnp.stack([pair[0] for pair in expert_grads]),
        jnp.stack([pair[1] for pair in expert_grads]),
    )


def solution(mesh):
    return jax.shard_map(
        shards,
        mesh=mesh,
        in_specs=(
            P(("dp", "cp"), None),
            P(("dp", "cp"), None),
            P("dp", None),
            P(None, ("dp", "cp"), None),
            P(None, ("dp", "cp"), None),
            P(None, ("dp", "cp"), None),
            P(None, ("dp", "cp"), None),
            P(None, ("dp", "cp"), None),
            P(None, "cp", "dp", None),
            P(None, "cp", "dp", None),
        ),
        out_specs=(
            P(("dp", "cp"), None),
            P(("dp", "cp"), None),
            P(None, ("dp", "cp"), None),
            P(None, ("dp", "cp"), None),
            P(None, ("dp", "cp"), None),
            P(None, ("dp", "cp"), None),
            P(None, "cp", "dp", None),
            P(None, "cp", "dp", None),
        ),
        check_vma=False,
    )
```

```python
import jax
import jax.numpy as jnp
from jax import lax
from jax.experimental import pallas as pl
from jax.experimental.pallas import tpu as pltpu
from jax.sharding import PartitionSpec as P

D = 1536
HEADS = 12
KV_HEADS = 2
HEAD = 128
FF = 768
TOP = 4
EXP_DEV = 2
LAYERS = 2
DOCS = 4
HQ = 1536
KVW = 256
QKV = 2048
Q_PER_KV = 6

EPSILON = 1e-06
MASKED = -1e30
LOW = jnp.bfloat16
WIDE = jnp.float32


def inverse_rms(values):
    return lax.rsqrt(jnp.mean(values * values, axis=-1, keepdims=True) + EPSILON)


def norm_backward(values, gain, upstream):
    scale_rows = inverse_rms(values)
    weighted = gain * upstream
    inner_mean = jnp.mean(values * weighted, axis=-1, keepdims=True)
    grad_values = scale_rows * weighted - values * scale_rows * scale_rows * scale_rows * inner_mean
    grad_gain = jnp.sum(values * scale_rows * upstream, axis=0)
    return (grad_values, grad_gain)


def doc_places(token_index, lengths_row):
    starts = jnp.cumsum(lengths_row) - lengths_row
    segment = jnp.sum((token_index[:, None] >= starts[None, 1:]).astype(jnp.int32), axis=1)
    picked = segment[:, None] == jnp.arange(DOCS, dtype=jnp.int32)[None, :]
    offset = jnp.sum(jnp.where(picked, starts[None, :], 0), axis=1)
    return (segment, token_index - offset)


def rope_tables(positions):
    half_width = HEAD // 2
    frequency = jnp.exp(-jnp.log(10000.0) * 2.0 * jnp.arange(half_width, dtype=WIDE) / HEAD)
    angles = positions.astype(WIDE)[:, None] * frequency[None, :]
    return (jnp.cos(angles)[:, None, :], jnp.sin(angles)[:, None, :])


def rotate(values, cosine, sine_table):
    half_width = values.shape[-1] // 2
    former = values[..., :half_width]
    latter = values[..., half_width:]
    return jnp.concatenate(
        [former * cosine - latter * sine_table, latter * cosine + former * sine_table], axis=-1
    )


def heads_first(values):
    token_rows = values.shape[0]
    shaped = values.reshape(token_rows, KV_HEADS, Q_PER_KV, HEAD).transpose(1, 2, 0, 3)
    return shaped.reshape(KV_HEADS, Q_PER_KV * token_rows, HEAD)


def heads_last(values):
    token_rows = values.shape[1] // Q_PER_KV
    shaped = values.reshape(KV_HEADS, Q_PER_KV, token_rows, HEAD).transpose(2, 0, 1, 3)
    return shaped.reshape(token_rows, HQ)


def dot(left, right):
    return jnp.dot(left, right, preferred_element_type=WIDE)


def dot_t(left, right):
    return lax.dot_general(left, right, (((1,), (1,)), ((), ())), preferred_element_type=WIDE)


def t_dot(left, right):
    return lax.dot_general(left, right, (((0,), (0,)), ((), ())), preferred_element_type=WIDE)


def after(value, *earlier):
    return lax.optimization_barrier((value, *earlier))[0]


ROWS = 128
LINE = 4
GROUP = 2 * LINE * ROWS
HALF = GROUP // 2
QROWS = QKV // 32
OROWS = HQ // 32
GROWS = D // 4
FROWS = FF // 4
SMALL = 16
EXPERTS = 2 * LINE * EXP_DEV


def cost(microseconds):
    return pl.CostEstimate(flops=0, bytes_accessed=int(microseconds * 0.4e6), transcendentals=0)


LIMIT = 60 * 1024 * 1024
SCALE = HEAD**-0.5


def spec(shape, index=None):
    if index is None:
        index = lambda *unused: (0,) * len(shape)
    return pl.BlockSpec(shape, index)


ANYWHERE = pl.BlockSpec(memory_space=pl.ANY)
SCALARS = pl.BlockSpec(memory_space=pltpu.SMEM)


def place_scalars():
    dp, cp = lax.axis_index("dp"), lax.axis_index("cp")
    return jnp.stack([dp, cp % 2, cp, cp // 2]).astype(jnp.int32)


def call(body, name, grid, arguments, in_specs, outs, out_specs, scratch, microseconds):
    return pl.pallas_call(
        body,
        grid=grid,
        out_shape=outs,
        in_specs=in_specs,
        out_specs=out_specs,
        scratch_shapes=scratch,
        name=name,
        compiler_params=pltpu.CompilerParams(vmem_limit_bytes=LIMIT),
        cost_estimate=cost(microseconds),
    )(*arguments)


def shape(dims, dtype):
    return jax.ShapeDtypeStruct(dims, dtype)


class Dense:
    def __init__(self, pieces, first_row, rows):
        self.pieces = pieces
        self.rows = rows
        self.first_row = first_row

    def arrays(self):
        return [piece[0] for piece in self.pieces]

    def copies(self, refs, places, scratch, sems):
        made = []
        for number, (ref, piece) in enumerate(zip(refs, self.pieces)):
            unused, part, flip, other, chip, chips = piece
            rows = pl.ds(self.first_row, self.rows)
            source = ref.at[:, rows] if part is None else ref.at[:, part, rows]
            target = scratch.at[places[0] ^ flip, pl.ds(chip, chips), places[1] ^ other]
            made.append(pltpu.make_async_copy(source, target, sems.at[number]))
        return made

    def scratch(self):
        return [
            pltpu.VMEM((4, LINE, 2, self.rows, D), LOW),
            pltpu.SemaphoreType.DMA((len(self.pieces),)),
        ]


def expert_copies(refs, places, gate_up, down, sems):
    made = []
    for expert in range(EXP_DEV):
        for flip in range(4):
            part = places[0] ^ flip
            first = pl.multiple_of(part * GROWS, GROWS)
            target = gate_up.at[expert, pl.ds(first, GROWS)]
            made.append((refs[4 * expert + flip], target))
            source = refs[8 + flip].at[expert] if flip < 3 else refs[11 + expert]
            first = pl.multiple_of(part * FROWS, FROWS)
            made.append((source, down.at[expert, pl.ds(first, FROWS)]))
    return [
        pltpu.make_async_copy(source, target, sems.at[number])
        for number, (source, target) in enumerate(made)
    ]


EXPERT_SCRATCH = [
    pltpu.VMEM((EXP_DEV, D, 2 * FF), LOW),
    pltpu.VMEM((EXP_DEV, FF, D), LOW),
    pltpu.SemaphoreType.DMA((16,)),
]


def logistic_of(values):
    return 0.5 * jnp.tanh(0.5 * values) + 0.5


def norm_rows(values, gain):
    return (values * inverse_rms(values) * gain).astype(LOW)


def turn(values, cosine, sine):
    return values * cosine + pltpu.roll(values, HEAD // 2, 1) * sine


def small_call(pieces):
    count = len(pieces.pieces)

    def body(places, *rest):
        refs, (out, sems) = rest[:count], rest[count:]
        copies = pieces.copies(refs, places, out, sems)
        for copy in copies:
            copy.start()
        for copy in copies:
            copy.wait()

    out = shape((4, LINE, 2, SMALL, D), LOW)
    return call(
        body,
        "small",
        (),
        [place_scalars(), *pieces.arrays()],
        [SCALARS] + [ANYWHERE] * count,
        out,
        spec(out.shape),
        [pltpu.SemaphoreType.DMA((count,))],
        3,
    )


def project_call(value, gain, query, tables):
    count = len(query.pieces)

    def body(places, value_ref, gain_ref, tables_ref, *rest):
        refs, (normed_ref, heads_ref, kv_ref, weight, sems, joined) = rest[:count], rest[count:]
        copies = query.copies(refs, places, weight, sems)
        for copy in copies:
            copy.start()
        normed = norm_rows(value_ref[...], gain_ref[...])
        normed_ref[...] = normed
        for copy in copies:
            copy.wait()
        for part in range(4):
            joined[part] = dot_t(normed, weight[part].reshape(8 * QROWS, D))
        cosine, sine = tables_ref[0], tables_ref[1]
        for head in range(HEADS + 2 * KV_HEADS):
            at = pl.ds(head % 4 * HEAD, HEAD)
            values = joined[head // 4, :, at]
            if head < HEADS:
                heads_ref[head] = turn(values, cosine, sine).astype(LOW)
            else:
                if head < HEADS + KV_HEADS:
                    values = turn(values, cosine, sine)
                kv_ref[:, pl.ds((head - HEADS) * HEAD, HEAD)] = values.astype(LOW)

    outs = [shape((ROWS, D), LOW), shape((HEADS, ROWS, HEAD), LOW), shape((ROWS, 2 * KVW), LOW)]
    arguments = [place_scalars(), value, gain, tables, *query.arrays()]
    return call(
        body,
        "project",
        (),
        arguments,
        [SCALARS, spec((ROWS, D)), spec((1, D)), spec((2, ROWS, HEAD))] + [ANYWHERE] * count,
        outs,
        [spec(o.shape) for o in outs],
        [*query.scratch(), pltpu.VMEM((4, ROWS, 8 * QROWS), WIDE)],
        7,
    )


def attend_call(value, heads, keys_values, query_meta, key_meta, output, gain):
    count = len(output.pieces)

    def body(places, value_ref, heads_ref, kv_own, kv_other, qmeta, kmeta, gain_ref, *rest):
        refs, (low_ref, probs_ref, middle_ref, mixed_ref, weight, sems, joined, kv_ref) = (
            rest[:count],
            rest[count:],
        )
        copies = output.copies(refs, places, weight, sems)
        for copy in copies:
            copy.start()
        kv_ref[pl.ds(0, HALF)] = kv_own[...]
        kv_ref[pl.ds(HALF, HALF)] = kv_other[...]
        allowed = (qmeta[:, 1:2] == kmeta[1:2, :]) & (kmeta[0:1, :] <= qmeta[:, 0:1])
        for head in range(HEADS):
            kv = head // Q_PER_KV
            keys = kv_ref[:, pl.ds(kv * HEAD, HEAD)]
            vals = kv_ref[:, pl.ds(KVW + kv * HEAD, HEAD)]
            scores = dot_t(heads_ref[head], keys) * SCALE
            scores = jnp.where(allowed, scores, MASKED)
            shares = jnp.exp(scores - jnp.max(scores, axis=1, keepdims=True))
            probs = (shares * (1.0 / jnp.sum(shares, axis=1, keepdims=True))).astype(LOW)
            probs_ref[head] = probs
            joined[:, pl.ds(head * HEAD, HEAD)] = dot(probs, vals).astype(LOW)
        low = joined[...]
        low_ref[...] = low
        for copy in copies:
            copy.wait()
        middle = value_ref[...] + dot(low, weight[...].reshape(HQ, D))
        middle_ref[...] = middle
        mixed_ref[...] = norm_rows(middle, gain_ref[...])

    outs = [
        shape((ROWS, HQ), LOW),
        shape((HEADS, ROWS, GROUP), LOW),
        shape((ROWS, D), WIDE),
        shape((ROWS, D), LOW),
    ]
    arguments = [
        place_scalars(),
        value,
        heads,
        *keys_values,
        query_meta,
        key_meta,
        gain,
        *output.arrays(),
    ]
    return call(
        body,
        "attend",
        (),
        arguments,
        [
            SCALARS,
            spec((ROWS, D)),
            spec((HEADS, ROWS, HEAD)),
            spec((HALF, 2 * KVW)),
            spec((HALF, 2 * KVW)),
            spec((ROWS, 2)),
            spec((2, GROUP)),
            spec((1, D)),
        ]
        + [ANYWHERE] * count,
        outs,
        [spec(o.shape) for o in outs],
        [*output.scratch(), pltpu.VMEM((ROWS, HQ), LOW), pltpu.VMEM((GROUP, 2 * KVW), LOW)],
        9,
    )


BLOCK = 256
STEPS = GROUP // BLOCK


def own_half(step):
    return (jnp.minimum(step, STEPS // 2 - 1), 0)


def other_half(step):
    return (jnp.maximum(step - STEPS // 2, 0), 0)


def rows_at(step):
    return (step, 0)


def take_half(step, own_ref, other_ref):
    return jnp.where(step < STEPS // 2, own_ref[...], other_ref[...])


def put_halves(step, own_ref, other_ref, values):
    @pl.when(step < STEPS // 2)
    def own():
        own_ref[...] = values

    @pl.when(step >= STEPS // 2)
    def other():
        other_ref[...] = values


def own_gate(gates, places, expert):
    ids = lax.broadcasted_iota(jnp.int32, gates.shape, 1)
    return jnp.sum(
        jnp.where(ids == EXP_DEV * places[2] + expert, gates, 0.0), axis=1, keepdims=True
    )


def experts_call(mixed, routes, router, pieces):
    def body(places, mixed_own, mixed_other, routes_ref, router_ref, *rest):
        refs, (own_ref, other_ref, gu_ref, hidden_ref, gates_ref, gate_up, down, sems) = (
            rest[:13],
            rest[13:],
        )
        step = pl.program_id(0)
        copies = expert_copies(refs, places, gate_up, down, sems)

        @pl.when(step == 0)
        def begin():
            for copy in copies:
                copy.start()
            for copy in copies:
                copy.wait()

        mixed_rows = take_half(step, mixed_own, mixed_other)
        logits = dot(mixed_rows, router_ref[...])
        ids = lax.broadcasted_iota(jnp.int32, (BLOCK, EXPERTS), 1)
        chosen = routes_ref[:, 0:1] == ids
        for k in range(1, TOP):
            chosen = chosen | (routes_ref[:, k : k + 1] == ids)
        logits = jnp.where(chosen, logits, MASKED)
        shares = jnp.where(chosen, jnp.exp(logits - jnp.max(logits, axis=1, keepdims=True)), 0.0)
        gates = shares / jnp.sum(shares, axis=1, keepdims=True)
        gates_ref[...] = gates

        terms = None
        for expert in range(EXP_DEV):
            gu = dot(mixed_rows, gate_up[expert])
            gu_ref[:, pl.ds(expert * 2 * FF, 2 * FF)] = gu.astype(LOW)
            gate_part = gu[:, :FF]
            hidden = gate_part * logistic_of(gate_part) * gu[:, FF:]
            hidden = (hidden * own_gate(gates, places, expert)).astype(LOW)
            hidden_ref[:, pl.ds(expert * FF, FF)] = hidden
            product = dot(hidden, down[expert])
            terms = product if terms is None else terms + product
        put_halves(step, own_ref, other_ref, terms.astype(LOW))

    outs = [
        shape((HALF, D), LOW),
        shape((HALF, D), LOW),
        shape((GROUP, EXP_DEV * 2 * FF), LOW),
        shape((GROUP, EXP_DEV * FF), LOW),
        shape((GROUP, EXPERTS), WIDE),
    ]
    return call(
        body,
        "experts",
        (STEPS,),
        [place_scalars(), *mixed, routes, router, *pieces],
        [
            SCALARS,
            spec((BLOCK, D), own_half),
            spec((BLOCK, D), other_half),
            spec((BLOCK, TOP), rows_at),
            spec((D, EXPERTS)),
        ]
        + [ANYWHERE] * 13,
        outs,
        [
            spec((BLOCK, D), own_half),
            spec((BLOCK, D), other_half),
            spec((BLOCK, EXP_DEV * 2 * FF), rows_at),
            spec((BLOCK, EXP_DEV * FF), rows_at),
            spec((BLOCK, EXPERTS), rows_at),
        ],
        EXPERT_SCRATCH,
        26,
    )


def experts_back_call(upstream, gate_up_kept, gates, router, pieces):
    def body(places, up_own, up_other, gu_ref, gates_ref, router_ref, *rest):
        refs, (own_ref, other_ref, grad_ref, logits_ref, gate_up, down, sems) = (
            rest[:13],
            rest[13:],
        )
        step = pl.program_id(0)
        copies = expert_copies(refs, places, gate_up, down, sems)

        @pl.when(step == 0)
        def begin():
            for copy in copies:
                copy.start()
            for copy in copies:
                copy.wait()

        upstream_rows = take_half(step, up_own, up_other)
        gates = gates_ref[...]
        ids = lax.broadcasted_iota(jnp.int32, (BLOCK, EXPERTS), 1)
        grad_logits = jnp.zeros((BLOCK, EXPERTS), WIDE)
        terms = None
        for expert in range(EXP_DEV):
            bare = dot_t(upstream_rows, down[expert])
            gate_part = gu_ref[:, pl.ds(expert * 2 * FF, FF)].astype(WIDE)
            up_part = gu_ref[:, pl.ds(expert * 2 * FF + FF, FF)].astype(WIDE)
            gate = own_gate(gates, places, expert)
            logistic = logistic_of(gate_part)
            activated = gate_part * logistic
            share = gate * jnp.sum(bare * activated * up_part, axis=1, keepdims=True)
            mine = jnp.where(ids == EXP_DEV * places[2] + expert, 1.0, 0.0)
            grad_logits = grad_logits + share * (mine - gates)
            gated = bare * gate
            grad_gate = gated * up_part * logistic * (1.0 + gate_part * (1.0 - logistic))
            grad_gate = grad_gate.astype(LOW)
            grad_up = (gated * activated).astype(LOW)
            grad_ref[:, pl.ds(expert * 2 * FF, FF)] = grad_gate
            grad_ref[:, pl.ds(expert * 2 * FF + FF, FF)] = grad_up
            grad_both = jnp.concatenate([grad_gate, grad_up], axis=1)
            product = dot_t(grad_both, gate_up[expert])
            terms = product if terms is None else terms + product
        grad_logits = grad_logits.astype(LOW)
        terms = terms + dot(grad_logits, router_ref[...])
        put_halves(step, own_ref, other_ref, terms.astype(LOW))
        logits_ref[...] = grad_logits

    outs = [
        shape((HALF, D), LOW),
        shape((HALF, D), LOW),
        shape((GROUP, EXP_DEV * 2 * FF), LOW),
        shape((GROUP, EXPERTS), LOW),
    ]
    return call(
        body,
        "experts_back",
        (STEPS,),
        [place_scalars(), *upstream, gate_up_kept, gates, router, *pieces],
        [
            SCALARS,
            spec((BLOCK, D), own_half),
            spec((BLOCK, D), other_half),
            spec((BLOCK, EXP_DEV * 2 * FF), rows_at),
            spec((BLOCK, EXPERTS), rows_at),
            spec((EXPERTS, D)),
        ]
        + [ANYWHERE] * 13,
        outs,
        [
            spec((BLOCK, D), own_half),
            spec((BLOCK, D), other_half),
            spec((BLOCK, EXP_DEV * 2 * FF), rows_at),
            spec((BLOCK, EXPERTS), rows_at),
        ],
        EXPERT_SCRATCH,
        26,
    )


def expert_grads_call(
    flips, mixed, grad_gate_up, hidden, upstream, received=(), layer=None, results=None
):
    last = layer is not None
    apart = len(flips) == 1 and not last
    kept = () if results is None else tuple(results)
    count = len(flips)

    def body(places, *rest):
        mixed_refs, rest = rest[: 2 * count], rest[2 * count :]
        hidden_refs, rest = rest[: 2 * count], rest[2 * count :]
        grad_ref, up_own, up_other = rest[:3]
        sums, outs = rest[3 : 3 + len(received)], rest[3 + len(received) + len(kept) :]
        expert = pl.program_id(0)
        for number, flip in enumerate(flips):
            gate_up = t_dot(mixed_refs[2 * number][...], grad_ref[pl.ds(0, HALF)])
            gate_up = gate_up + t_dot(mixed_refs[2 * number + 1][...], grad_ref[pl.ds(HALF, HALF)])
            both = jnp.concatenate([hidden_refs[2 * number][...], hidden_refs[2 * number + 1][...]], axis=1)
            down = t_dot(both[:HALF], up_own[...]) + t_dot(both[HALF:], up_other[...])
            part = places[0] ^ flip
            down = jnp.where(part % 2 == 0, down[:FROWS], down[2 * HEAD - FROWS :])
            for ref, (unused, whose, only) in zip(sums, received):
                if whose != number:
                    continue
                held = (ref[...] if only is not None else ref[0]).astype(WIDE)
                if only is not None:
                    held = jnp.where(expert == only, held, 0.0)
                gate_up = gate_up + held[:GROWS]
                down = down + held[GROWS:]
            if last:
                outs[0][0, 0] = gate_up
                outs[1][0, 0] = down
                continue
            gate_up = gate_up.astype(LOW)
            down = down.astype(LOW)
            if apart:
                for own in range(EXP_DEV):

                    @pl.when(expert == own)
                    def put():
                        outs[own][pl.ds(0, GROWS)] = gate_up
                        outs[own][pl.ds(GROWS, FROWS)] = down

            else:
                outs[number][0, pl.ds(0, GROWS)] = gate_up
                outs[number][0, pl.ds(GROWS, FROWS)] = down

    each = lambda e, places: (e, 0, 0)
    whole = lambda e, places: (0, 0)
    if last:
        at_layer = lambda e, places: (layer, e, 0, 0)
        outs = [shape((LAYERS, EXP_DEV, GROWS, D), WIDE), shape((LAYERS, EXP_DEV, FROWS, D), WIDE)]
        out_specs = [
            pl.BlockSpec((1, 1, GROWS, D), at_layer),
            pl.BlockSpec((1, 1, FROWS, D), at_layer),
        ]
    elif apart:
        outs = [shape((GROWS + FROWS, D), LOW)] * EXP_DEV
        out_specs = [pl.BlockSpec((GROWS + FROWS, D), whole)] * EXP_DEV
    else:
        outs = [shape((EXP_DEV, GROWS + FROWS, D), LOW)] * count
        out_specs = [pl.BlockSpec((1, GROWS + FROWS, D), each)] * count
    in_specs = []
    for flip in flips:
        in_specs += [pl.BlockSpec((HALF, GROWS), lambda e, places, flip=flip: (0, places[0] ^ flip))] * 2
    for flip in flips:
        for side in range(2):
            in_specs.append(
                pl.BlockSpec(
                    (GROUP, HEAD),
                    lambda e, places, flip=flip, side=side: (
                        0,
                        e * (FF // HEAD) + (places[0] ^ flip) * 3 // 2 + side,
                    ),
                )
            )
    in_specs += [
        pl.BlockSpec((GROUP, 2 * FF), lambda e, places: (0, e)),
        pl.BlockSpec((HALF, D), whole),
        pl.BlockSpec((HALF, D), whole),
    ]
    for unused, whose, only in received:
        in_specs.append(
            pl.BlockSpec((1, GROWS + FROWS, D), each)
            if only is None
            else pl.BlockSpec((GROWS + FROWS, D), whole)
        )
    in_specs += [ANYWHERE] * len(kept)
    first_kept = 1 + 4 * count + 3 + len(received)
    return pl.pallas_call(
        body,
        out_shape=outs,
        input_output_aliases={first_kept + i: i for i in range(len(kept))},
        grid_spec=pltpu.PrefetchScalarGridSpec(
            num_scalar_prefetch=1, grid=(EXP_DEV,), in_specs=in_specs, out_specs=out_specs
        ),
        name="expert_grads",
        compiler_params=pltpu.CompilerParams(vmem_limit_bytes=LIMIT),
        cost_estimate=cost(15 if count > 1 else 11),
    )(
        place_scalars(),
        *(list(mixed) * count),
        *([hidden] * (2 * count)),
        grad_gate_up,
        *upstream,
        *(array for array, unused, only in received),
        *kept,
    )


def norm_back(values, gain, upstream):
    scale_rows = inverse_rms(values)
    weighted = gain * upstream
    inner_mean = jnp.mean(values * weighted, axis=1, keepdims=True)
    grads = scale_rows * (weighted - values * (scale_rows * scale_rows * inner_mean))
    return (grads, jnp.sum(values * scale_rows * upstream, axis=0, keepdims=True))


def attend_back_call(grad_mixed, middle, gain, upstream, output, low, probs, heads, keys_values):
    count = len(output.pieces)

    def body(
        places, gm_ref, middle_ref, gain_ref, up_ref, low_in, probs_ref, heads_ref, kv_own, kv_other, *rest
    ):
        refs, (grad_ref, error_ref, gq_ref, own_ref, other_ref, gg_ref, weight, sems, kvs, kv_ref) = (
            rest[:count],
            rest[count:],
        )
        copies = output.copies(refs, places, weight, sems)
        for copy in copies:
            copy.start()
        kv_ref[pl.ds(0, HALF)] = kv_own[...]
        kv_ref[pl.ds(HALF, HALF)] = kv_other[...]
        grads, gain_grad = norm_back(middle_ref[...], gain_ref[...], gm_ref[...])
        gg_ref[...] = gain_grad
        grads = grads + up_ref[...]
        grad_ref[...] = grads
        error = grads.astype(LOW)
        error_ref[...] = error
        for copy in copies:
            copy.wait()
        grad_attended = dot_t(error, weight[...].reshape(HQ, D)).astype(LOW)
        for head in range(HEADS):
            kv = head // Q_PER_KV
            at = pl.ds(kv * HEAD, HEAD)
            at_values = pl.ds(KVW + kv * HEAD, HEAD)
            grad_head = grad_attended[:, head * HEAD : (head + 1) * HEAD]
            delta = jnp.sum(
                grad_head.astype(WIDE) * low_in[:, pl.ds(head * HEAD, HEAD)].astype(WIDE),
                axis=1,
                keepdims=True,
            )
            shares = probs_ref[head]
            grad_scores = dot_t(grad_head, kv_ref[:, at_values]) - delta
            grad_scores = (shares.astype(WIDE) * grad_scores * SCALE).astype(LOW)
            gq_ref[head] = dot(grad_scores, kv_ref[:, at])
            grad_keys = t_dot(grad_scores, heads_ref[head])
            grad_values = t_dot(shares, grad_head)
            if head % Q_PER_KV == 0:
                kvs[:, at] = grad_keys
                kvs[:, at_values] = grad_values
            else:
                kvs[:, at] += grad_keys
                kvs[:, at_values] += grad_values
        own_ref[...] = kvs[pl.ds(0, HALF)].astype(LOW)
        other_ref[...] = kvs[pl.ds(HALF, HALF)].astype(LOW)

    outs = [
        shape((ROWS, D), WIDE),
        shape((ROWS, D), LOW),
        shape((HEADS, ROWS, HEAD), WIDE),
        shape((HALF, 2 * KVW), LOW),
        shape((HALF, 2 * KVW), LOW),
        shape((1, D), WIDE),
    ]
    arguments = [
        place_scalars(),
        grad_mixed,
        middle,
        gain,
        upstream,
        low,
        probs,
        heads,
        *keys_values,
        *output.arrays(),
    ]
    return call(
        body,
        "attend_back",
        (),
        arguments,
        [SCALARS] + [spec(a.shape) for a in arguments[1:10]] + [ANYWHERE] * count,
        outs,
        [spec(o.shape) for o in outs],
        [*output.scratch(), pltpu.VMEM((GROUP, 2 * KVW), WIDE), pltpu.VMEM((GROUP, 2 * KVW), LOW)],
        12,
    )


def project_back_call(grad_heads, grad_kv, tables, query, value, gain, grad_middle):
    count = len(query.pieces)

    def body(places, gq_ref, gkv_ref, tables_ref, value_ref, gain_ref, gm_ref, *rest):
        refs, (joined_ref, grad_ref, low_ref, gg_ref, weight, sems) = rest[:count], rest[count:]
        copies = query.copies(refs, places, weight, sems)
        for copy in copies:
            copy.start()
        cosine, sine = tables_ref[0], -tables_ref[1]
        for head in range(HEADS + 2 * KV_HEADS):
            if head < HEADS:
                values = turn(gq_ref[head], cosine, sine)
            else:
                values = gkv_ref[:, pl.ds((head - HEADS) * HEAD, HEAD)]
                if head < HEADS + KV_HEADS:
                    values = turn(values, cosine, sine)
            joined_ref[:, pl.ds(head * HEAD, HEAD)] = values.astype(LOW)
        for copy in copies:
            copy.wait()
        grad_normed = dot(joined_ref[...], weight[...].reshape(QKV, D))
        grads, gain_grad = norm_back(value_ref[...], gain_ref[...], grad_normed)
        gg_ref[...] = gain_grad
        grads = grads + gm_ref[...]
        grad_ref[...] = grads
        low_ref[...] = grads.astype(LOW)

    outs = [
        shape((ROWS, QKV), LOW),
        shape((ROWS, D), WIDE),
        shape((ROWS, D), LOW),
        shape((1, D), WIDE),
    ]
    arguments = [
        place_scalars(),
        grad_heads,
        grad_kv,
        tables,
        value,
        gain,
        grad_middle,
        *query.arrays(),
    ]
    return call(
        body,
        "project_back",
        (),
        arguments,
        [SCALARS] + [spec(a.shape) for a in arguments[1:7]] + [ANYWHERE] * count,
        outs,
        [spec(o.shape) for o in outs],
        query.scratch(),
        7,
    )


def dense_grads_call(joined, normed, low, error, small):
    rows = QROWS + OROWS + (SMALL if small is not None else 0)

    def body(places, joined_ref, normed_ref, low_ref, error_ref, *rest):
        mine_ref, other_ref = rest[-2:]
        query = t_dot(joined_ref[...], normed_ref[...]).astype(LOW).reshape(LINE, 2, QROWS, D)
        outs = t_dot(low_ref[...], error_ref[...]).astype(LOW).reshape(LINE, 2, OROWS, D)
        for core in range(2):

            def put(ref):
                ref[0, :, pl.ds(0, QROWS)] = query[:, core]
                ref[0, :, pl.ds(QROWS, OROWS)] = outs[:, core]
                if small is not None:
                    ref[0, :, pl.ds(QROWS + OROWS, SMALL)] = rest[0][0, :, core]

            @pl.when(places[1] == core)
            def mine():
                put(mine_ref)

            @pl.when(places[1] != core)
            def other():
                put(other_ref)

    out = shape((4, LINE, rows, D), LOW)
    part = lambda flip, places: (0, places[0] ^ flip)
    whole = lambda flip, places: (0, 0)
    in_specs = [
        pl.BlockSpec((ROWS, QKV // 4), part),
        pl.BlockSpec((ROWS, D), whole),
        pl.BlockSpec((ROWS, HQ // 4), part),
        pl.BlockSpec((ROWS, D), whole),
    ]
    arguments = [joined, normed, low, error]
    if small is not None:
        in_specs.append(
            pl.BlockSpec((1, LINE, 2, SMALL, D), lambda flip, places: (places[0] ^ flip, 0, 0, 0, 0))
        )
        arguments.append(small)
    out_spec = pl.BlockSpec((1, LINE, rows, D), lambda flip, places: (flip, 0, 0, 0))
    return pl.pallas_call(
        body,
        out_shape=[out, out],
        grid_spec=pltpu.PrefetchScalarGridSpec(
            num_scalar_prefetch=1, grid=(4,), in_specs=in_specs, out_specs=[out_spec, out_spec]
        ),
        name="dense_grads",
        compiler_params=pltpu.CompilerParams(vmem_limit_bytes=LIMIT),
        cost_estimate=cost(9),
    )(place_scalars(), *arguments)


def swap_core(value):
    return lax.ppermute(value, "cp", [(i, i ^ 1) for i in range(2 * LINE)])


def hop(value, upward, sources):
    step = 1 if upward else -1
    pairs = [(2 * z + core, 2 * (z + step) + core) for z in sources for core in range(2)]
    return lax.ppermute(value, "cp", pairs)


def leap(value, distance):
    pairs = [(i, i + 2 * distance) for i in range(2 * LINE) if 0 <= i + 2 * distance < 2 * LINE]
    return lax.ppermute(value, "cp", pairs)


def across(value, flip):
    return lax.ppermute(value, "dp", [(i, i ^ flip) for i in range(4)])


def line_gather(value, *stages):
    place = lax.axis_index("cp") // 2
    rising, falling = value, value
    risen, fallen = [], []
    for step in range(1, LINE):
        if step <= len(stages):
            rising = after(rising, *stages[step - 1])
            falling = after(falling, *stages[step - 1])
        rising = hop(rising, True, range(step - 1, LINE - 1))
        falling = hop(falling, False, range(1, LINE - step + 1))
        risen.insert(0, rising)
        fallen.append(falling)
    every = jnp.stack(risen + [value] + fallen)
    return lax.dynamic_slice_in_dim(every, LINE - 1 - place, LINE, 0)


def leap_gather(value):
    place = lax.axis_index("cp") // 2
    every = [leap(value, LINE - 1 - i) if i != LINE - 1 else value for i in range(2 * LINE - 1)]
    return lax.dynamic_slice_in_dim(jnp.stack(every), LINE - 1 - place, LINE, 0)


def line_scatter(parts, *stages):
    place = lax.axis_index("cp") // 2

    def pick(index):
        return lax.dynamic_index_in_dim(parts, jnp.clip(index, 0, LINE - 1), 0, keepdims=False)

    rising = falling = None
    for step in range(1, LINE):
        up = pick(LINE + place - step)
        down = pick(place - LINE + step)
        if step > 1:
            up = (up.astype(WIDE) + rising.astype(WIDE)).astype(LOW)
            down = (down.astype(WIDE) + falling.astype(WIDE)).astype(LOW)
        if step <= len(stages):
            up = after(up, *stages[step - 1])
            down = after(down, *stages[step - 1])
        rising = hop(up, True, range(step))
        falling = hop(down, False, range(LINE - step, LINE))
    return pick(place).astype(WIDE) + rising.astype(WIDE) + falling.astype(WIDE)


def group_gather(value, *stages):
    mine = line_gather(value, *stages[: LINE - 1])
    for stage in stages[LINE - 1 :]:
        mine = after(mine, *stage)
    other = swap_core(mine)
    return (mine.reshape(HALF, -1), other.reshape(HALF, -1))


def group_scatter(own, other, first=(), *stages):
    both = (own.astype(WIDE) + swap_core(after(other, *first)).astype(WIDE)).astype(LOW)
    return line_scatter(both.reshape(LINE, ROWS, -1), *stages)


def earlier_gather(value):
    mine = jnp.stack([leap(value, 3), leap(value, 2), leap(value, 1), value])
    other = swap_core(mine)
    return (mine.reshape(HALF, -1), other.reshape(HALF, -1))


def earlier_scatter(own, other):
    both = (own.astype(WIDE) + swap_core(other).astype(WIDE)).astype(LOW).reshape(LINE, ROWS, -1)
    total = both[LINE - 1].astype(WIDE)
    for distance in range(1, LINE):
        total = total + leap(both[LINE - 1 - distance], -distance).astype(WIDE)
    return total


def square_step(value):
    return (across(value, 1), across(value, 2))


def square_far(by_x, by_y):
    half = by_x.shape[0] // 2
    return (across(by_x[:half], 2), across(by_y[half:], 1))


def dense_pieces(line, by_x, by_y, far):
    held = [
        (line, 0, 0, LINE),
        (by_x, 1, 0, LINE),
        (by_y, 2, 0, LINE),
        (far[0], 3, 0, LINE // 2),
        (far[1], 3, LINE // 2, LINE // 2),
    ]
    pieces = []
    for array, flip, chip, chips in held:
        pieces.append((array, None, flip, 0, chip, chips))
        pieces.append((swap_core(array), None, flip, 1, chip, chips))
    return pieces


def dense_square_scatter(mine, received, *earlier):
    def piece(flip):
        return mine[flip].astype(WIDE) + received[flip].astype(WIDE)

    half = LINE // 2
    far = after(piece(3).astype(LOW), *earlier)
    from_x = across(far[:half], 1)
    from_y = across(far[half:], 2)
    to_x, to_y = piece(1), piece(2)
    to_x = jnp.concatenate([to_x[:half], to_x[half:] + from_y.astype(WIDE)], axis=0).astype(LOW)
    to_y = jnp.concatenate([to_y[:half] + from_x.astype(WIDE), to_y[half:]], axis=0).astype(LOW)
    got_x = across(to_x, 1)
    got_y = across(to_y, 2)
    plane = piece(0) + got_x.astype(WIDE) + got_y.astype(WIDE)
    return ((from_x, from_y), (got_x, got_y), plane.astype(LOW))


def square_line_shards(
    tokens, cotangent, doc_lengths, routes, w_qkv, w_out, router, gains, w_gate_up, w_down
):
    dp_place = lax.axis_index("dp")
    cp_place = lax.axis_index("cp")
    core = cp_place % 2
    chip = cp_place // 2
    lengths_row = doc_lengths[0]
    row_ids = jnp.arange(ROWS, dtype=jnp.int32)
    my_index = cp_place * ROWS + row_ids
    my_segment, my_position = doc_places(my_index, lengths_row)
    query_meta = jnp.stack([my_index, my_segment], axis=1)
    back = jnp.arange(LINE, dtype=jnp.int32) - (LINE - 1) + chip
    blocks = jnp.concatenate([2 * back + core, 2 * back + 1 - core])
    blocks = jnp.where(jnp.concatenate([back, back]) < 0, 4 * LINE, blocks)
    key_index = (blocks[:, None] * ROWS + row_ids[None, :]).reshape(-1)
    key_segment, unused_position = doc_places(key_index, lengths_row)
    key_meta = jnp.stack([key_index, key_segment])
    cosine, sine = rope_tables(my_position)
    cosine, sine = cosine[:, 0], sine[:, 0]
    tables = jnp.stack(
        [jnp.concatenate([cosine, cosine], axis=1), jnp.concatenate([-sine, sine], axis=1)]
    )

    small_lines = LAYERS * (EXPERTS + 2)
    own_rows = router.shape[1]
    small = jnp.concatenate([router, gains], axis=2).transpose(0, 2, 1).reshape(-1)
    small_size = small.shape[0]
    small_rows = -(-small_size // D)
    small = jnp.pad(small, (0, small_rows * D - small_size)).reshape(small_rows, D)
    route_numbers = routes.reshape(-1).astype(LOW)
    route_size = route_numbers.shape[0]
    route_numbers = jnp.pad(route_numbers, (0, D - route_size)).reshape(1, D)
    small = jnp.concatenate([small, route_numbers], axis=0)
    small = jnp.pad(small, ((0, SMALL - small_rows - 1), (0, 0)))

    gate_x, gate_y = square_step(w_gate_up[0, 0])
    first = line_gather(jnp.concatenate([w_qkv[0], w_out[0], small], axis=0))
    second = jnp.concatenate([w_qkv[1], w_out[1], cotangent], axis=0)
    second = line_gather(after(second, first))
    dense_rows = QROWS + OROWS
    upstream_line = second[:, dense_rows:]
    second = second[:, :dense_rows]
    first_x, first_y = square_step(after(first, gate_x, gate_y))
    first_far = square_far(first_x, first_y)
    pieces = dense_pieces(first, first_x, first_y, first_far)
    query, output = Dense(pieces, 0, QROWS), Dense(pieces, QROWS, OROWS)
    small = small_call(Dense(pieces, dense_rows, SMALL))

    def expert_weights(layer, first, more, down, far):
        gate_ups = [w_gate_up[layer, 0], *first, far[0], w_gate_up[layer, 1], *more, far[1]]
        return gate_ups + [w_down[layer], *down, far[2], far[3]]

    def experts_far(first, more, down):
        return (
            across(after(first[0], *down), 2),
            across(after(more[1], *down), 1),
            across(down[0][0], 2),
            across(down[1][1], 1),
        )

    gate_ups = [[(gate_x, gate_y)], []]
    gate_ups[0].append(square_step(after(w_gate_up[0, 1], *first_far)))
    downs = [square_step(after(w_down[0], *gate_ups[0][1]))]
    fars = [experts_far(*gate_ups[0], downs[0])]
    weights = [(query, output, expert_weights(0, *gate_ups[0], downs[0], fars[0]))]
    second_near = square_step(after(second, *fars[0]))
    second_far = square_far(*second_near)
    pieces = dense_pieces(second, *second_near, second_far)
    query, output = Dense(pieces, 0, QROWS), Dense(pieces, QROWS, OROWS)
    gate_ups[1].append(square_step(after(w_gate_up[1, 0], *second_far)))
    gate_ups[1].append(square_step(after(w_gate_up[1, 1], *gate_ups[1][0])))
    downs.append(square_step(after(w_down[1], *gate_ups[1][1])))
    fars.append(experts_far(*gate_ups[1], downs[1]))
    weights.append((query, output, expert_weights(1, *gate_ups[1], downs[1], fars[1])))

    shared = small.reshape(-1, SMALL, D)
    lines = shared[:, :small_rows].reshape(-1, small_rows * D)[:, :small_size]
    lines = lines.reshape(-1, small_lines, own_rows).transpose(1, 0, 2).reshape(small_lines, D)
    lines = lines.reshape(LAYERS, EXPERTS + 2, D)
    routers = lines[:, :EXPERTS]
    gain_rows = lines[:, EXPERTS:].astype(WIDE)[:, :, None]
    numbers = lax.dynamic_index_in_dim(small, dp_place, 0, keepdims=False)
    numbers = numbers[:, :, small_rows, :route_size]
    numbers = jnp.where(core == 0, numbers, numbers[:, ::-1]).astype(jnp.int32)
    numbers = numbers.reshape(LINE, 2, LAYERS, ROWS, TOP).transpose(2, 1, 0, 3, 4)
    group_routes = numbers.reshape(LAYERS, GROUP, TOP)

    value = after(tokens, second).astype(WIDE)
    stored = []
    for layer in range(LAYERS):
        query, output, pieces = weights[layer]
        normed, heads, kv = project_call(value, gain_rows[layer, 0], query, tables)
        keys_values = earlier_gather(kv)
        if layer == 0:
            keys_values = (after(keys_values[0], *gate_ups[0][1], routers, group_routes), keys_values[1])
        low, probs, middle, mixed = attend_call(
            value, heads, keys_values, query_meta, key_meta, output, gain_rows[layer, 1]
        )
        if layer == 0:
            mixed = group_gather(mixed, (), downs[0])
        else:
            mixed = group_gather(mixed, gate_ups[1][1], (), downs[1])
        own, other, gate_up, hidden, gates = experts_call(
            mixed, group_routes[layer], routers[layer].T, pieces
        )
        stored.append((value, normed, heads, keys_values, low, probs, middle, mixed, gate_up, hidden, gates))
        if layer == 0:
            value = middle + group_scatter(own, other, second_near, (), second_far, ())
            value = after(value, *gate_ups[1][0])
    last_sums = (own, other)

    upstream_group = (upstream_line.reshape(HALF, D), swap_core(upstream_line).reshape(HALF, D))
    upstream = cotangent.astype(WIDE)
    expert_grads = None
    dense_grads, router_grads, gain_grads = ([None] * LAYERS for _ in range(3))
    for layer in reversed(range(LAYERS)):
        query, output, pieces = weights[layer]
        value, normed, heads, keys_values, low, probs, middle, mixed, gate_up, hidden, gates = stored[layer]
        own, other, grad_gate_up, grad_logits = experts_back_call(
            upstream_group, gate_up, gates, routers[layer], pieces
        )
        router_grads[layer] = t_dot(grad_logits[:HALF], mixed[0]) + t_dot(grad_logits[HALF:], mixed[1])
        terms = (mixed, grad_gate_up, hidden, upstream_group)
        far = expert_grads_call((3,), *terms)
        from_x = across(far[0], 1)
        from_y = across(far[1], 2)
        if layer < LAYERS - 1:
            far = [after(part, *dense_sums[1]) for part in far]
        grad_mixed = group_scatter(own, other, far)
        to_x, to_y = expert_grads_call(
            (1, 2), *terms, received=[(from_y, 0, 1), (from_x, 1, 0)]
        )
        grad_mixed = after(grad_mixed, to_x, to_y)
        got_x = across(to_x, 1)
        got_y = across(to_y, 2)
        expert_sums = (got_x, got_y)
        expert_grads = expert_grads_call(
            (0,),
            *terms,
            received=[(got_x, 0, None), (got_y, 0, None)],
            layer=layer,
            results=expert_grads,
        )
        grad_middle, error, grad_heads, own, other, second_gain = attend_back_call(
            grad_mixed, middle, gain_rows[layer, 1], upstream, output, low, probs, heads, keys_values
        )
        grad_kv = earlier_scatter(own, other)
        joined, upstream, upstream_low, first_gain = project_back_call(
            grad_heads, grad_kv, tables, query, value, gain_rows[layer, 0], grad_middle
        )
        gain_grads[layer] = jnp.concatenate([first_gain, second_gain], axis=0)
        small = None
        if layer == 0:
            small = jnp.concatenate(
                [jnp.concatenate([router_grads[l], gain_grads[l]], axis=0) for l in range(LAYERS)], axis=0
            ).astype(LOW)
            small = small.reshape(small_lines, -1, own_rows).transpose(1, 0, 2).reshape(-1, small_size)
            small = jnp.pad(small, ((0, 0), (0, SMALL * D - small_size)))
            small = small.reshape(4, LINE, 2, SMALL, D)
        mine, other = dense_grads_call(joined, normed, low, error, small)
        if layer > 0:
            received = swap_core(other)
            dense_sums = dense_square_scatter(mine, received, got_x, got_y)
            upstream_group = group_gather(upstream_low, (mine, other), (), (got_x, got_y), dense_sums[0])
            dense_grads[layer] = line_scatter(dense_sums[2])
        else:
            dense_grads[0] = line_scatter(dense_square_scatter(mine, swap_core(other))[2])
    result = stored[-1][6] + group_scatter(after(last_sums[0], joined), last_sums[1])
    small = dense_grads[0][QROWS + OROWS :].reshape(-1)[:small_size]
    small = small.reshape(LAYERS, EXPERTS + 2, own_rows).transpose(0, 2, 1)
    return (
        result,
        upstream,
        jnp.stack([grads[:QROWS] for grads in dense_grads]),
        jnp.stack([grads[QROWS : QROWS + OROWS] for grads in dense_grads]),
        small[:, :, :EXPERTS],
        small[:, :, EXPERTS:],
        *expert_grads,
    )


class AnyMesh:
    def order(self, rows):
        return jnp.arange(lax.axis_size("cp") * rows, dtype=jnp.int32)

    def group_gather(self, value):
        return lax.all_gather(value, "cp", axis=0, tiled=True)

    def group_scatter(self, terms):
        return lax.psum_scatter(
            terms.astype(LOW), "cp", scatter_dimension=0, tiled=True
        ).astype(WIDE)

    def expert_gather(self, block):
        return lax.all_gather(block, "dp", axis=1, tiled=True)

    def expert_scatter(self, terms):
        return lax.psum_scatter(terms, "dp", scatter_dimension=1, tiled=True).astype(WIDE)

    def dense_gather(self, block):
        return lax.all_gather(block, ("dp", "cp"), axis=0, tiled=True)

    def dense_scatter(self, terms):
        return lax.psum_scatter(
            terms.astype(LOW), ("dp", "cp"), scatter_dimension=0, tiled=True
        ).astype(WIDE)


def any_mesh_shards(tokens, cotangent, doc_lengths, routes, w_qkv, w_out, router, gains, w_gate_up, w_down):
    dp_size = lax.axis_size("dp")
    cp_size = lax.axis_size("cp")
    device_count = dp_size * cp_size
    move = AnyMesh()
    row_count = tokens.shape[0]
    group_rows = row_count * cp_size
    cycle_place = lax.axis_index("cp")
    expert_count = EXP_DEV * cp_size
    lengths_row = doc_lengths[0]
    my_index = cycle_place * row_count + jnp.arange(row_count, dtype=jnp.int32)
    my_segment, my_position = doc_places(my_index, lengths_row)
    cosine, sine_table = rope_tables(my_position)
    score_scale = HEAD ** (-0.5)
    key_index = move.order(row_count)
    key_segment, unused_position = doc_places(key_index, lengths_row)
    allowed = (my_segment[:, None] == key_segment[None, :]) & (
        key_index[None, :] <= my_index[:, None]
    )
    allowed = jnp.tile(allowed, (Q_PER_KV, 1))[None]

    part_rows = router.shape[1]
    small_width = expert_count + 2
    small = jnp.concatenate([router, gains], axis=2).reshape(-1)
    small_size = small.shape[0]
    small = jnp.pad(small, (0, -small_size % 2048)).reshape(-1, 128)
    small = lax.all_gather(small, ("dp", "cp"), axis=0, tiled=False).reshape(device_count, -1)
    small = small[:, :small_size].reshape(device_count, LAYERS, part_rows, small_width)
    small = small.transpose(1, 0, 2, 3).reshape(LAYERS, D, small_width)
    router_all = small[:, :, :expert_count]
    gains_all = small[:, :, expert_count:].astype(WIDE)
    route_block = routes.reshape(-1, 128)
    route_blocks = lax.all_gather(route_block, "cp", axis=0, tiled=False)
    route_blocks = route_blocks.reshape(cp_size, LAYERS, row_count, TOP)
    route_rows = route_blocks.transpose(1, 0, 2, 3).reshape(LAYERS, group_rows, TOP)
    expert_ids = jnp.arange(expert_count, dtype=jnp.int32)

    weights = []
    for layer in range(LAYERS):
        query_weight = move.dense_gather(w_qkv[layer])
        output_weight = move.dense_gather(w_out[layer])
        gate_up_weight = move.expert_gather(w_gate_up[layer])
        down_weight = move.expert_gather(w_down[layer])
        weights.append((query_weight, output_weight, gate_up_weight, down_weight))
    cotangent_group = move.group_gather(cotangent)

    def forward_layer(layer, layer_value):
        query_weight, output_weight, gate_up_weight, down_weight = weights[layer]
        normed = norm_rows(layer_value, gains_all[layer, :, 0])
        joined = dot_t(normed, query_weight)
        queries = rotate(joined[:, :HQ].reshape(row_count, HEADS, HEAD), cosine, sine_table)
        keys = rotate(
            joined[:, HQ : HQ + KVW].reshape(row_count, KV_HEADS, HEAD), cosine, sine_table
        )
        queries = heads_first(queries.reshape(row_count, HQ).astype(LOW))
        keys_values = jnp.concatenate(
            [keys.reshape(row_count, KVW), joined[:, HQ + KVW :]], axis=1
        ).astype(LOW)
        keys_values = move.group_gather(keys_values)
        key_heads = keys_values[:, :KVW].reshape(group_rows, KV_HEADS, HEAD)
        value_heads = keys_values[:, KVW:].reshape(group_rows, KV_HEADS, HEAD)
        scores = (
            jnp.einsum("kqh,nkh->kqn", queries, key_heads, preferred_element_type=WIDE)
            * score_scale
        )
        scores = jnp.where(allowed, scores, MASKED)
        top_score = jnp.max(scores, axis=-1, keepdims=True)
        shares = jnp.exp(scores - top_score)
        total = jnp.sum(shares, axis=-1, keepdims=True)
        probs = (shares / total).astype(LOW)
        attended = jnp.einsum("kqn,nkh->kqh", probs, value_heads, preferred_element_type=WIDE)
        attended = heads_last(attended)
        attended_low = attended.astype(LOW)
        middle = layer_value + dot(attended_low, output_weight)
        mixed = norm_rows(middle, gains_all[layer, :, 1])
        mixed_group = move.group_gather(mixed)
        route_group = jnp.take(
            route_rows[layer].reshape(cp_size, row_count, TOP),
            key_index[::row_count] // row_count,
            axis=0,
        ).reshape(group_rows, TOP)
        chosen = jnp.any(route_group[:, :, None] == expert_ids[None, None, :], axis=1)
        logits = jnp.where(chosen, dot(mixed_group, router_all[layer]), MASKED)
        gates = jax.nn.softmax(logits, axis=-1)
        own_gates = lax.dynamic_slice_in_dim(gates, EXP_DEV * cycle_place, EXP_DEV, 1)
        gate_up = [dot(mixed_group, gate_up_weight[e]).astype(LOW) for e in range(EXP_DEV)]
        hidden = []
        for e in range(EXP_DEV):
            gate_part = gate_up[e][:, :FF].astype(WIDE)
            up_part = gate_up[e][:, FF:].astype(WIDE)
            hidden.append(jax.nn.silu(gate_part) * up_part * own_gates[:, e : e + 1])
        hidden = jnp.concatenate(hidden, axis=1).astype(LOW)
        terms = dot(hidden, down_weight.reshape(EXP_DEV * FF, D))
        result = middle + move.group_scatter(terms)
        kept = (
            layer_value,
            normed,
            queries,
            keys_values,
            probs,
            attended,
            middle,
            mixed_group,
            gates,
            own_gates,
            gate_up,
            hidden,
        )
        return (result, kept)

    def backward_layer(layer, upstream, upstream_group, kept):
        query_weight, output_weight, gate_up_weight, down_weight = weights[layer]
        (
            layer_value,
            normed,
            queries,
            keys_values,
            probs,
            attended,
            middle,
            mixed_group,
            gates,
            own_gates,
            gate_up,
            hidden,
        ) = kept
        grad_hidden = dot_t(upstream_group, down_weight.reshape(EXP_DEV * FF, D))
        grad_gate_up = []
        grad_gates = []
        for e in range(EXP_DEV):
            gate_part = gate_up[e][:, :FF].astype(WIDE)
            up_part = gate_up[e][:, FF:].astype(WIDE)
            bare = grad_hidden[:, e * FF : (e + 1) * FF]
            logistic = jax.nn.sigmoid(gate_part)
            activated = gate_part * logistic
            grad_gates.append(jnp.sum(bare * activated * up_part, axis=1, keepdims=True))
            gated = bare * own_gates[:, e : e + 1]
            grad_gate = gated * up_part * logistic * (1.0 + gate_part * (1.0 - logistic))
            grad_gate_up.append(
                jnp.concatenate([grad_gate, gated * activated], axis=1).astype(LOW)
            )
        own_terms = own_gates * jnp.concatenate(grad_gates, axis=1)
        own_ids = EXP_DEV * cycle_place + jnp.arange(EXP_DEV, dtype=jnp.int32)
        placed = jnp.sum(
            jnp.where(own_ids[None, :, None] == expert_ids[None, None, :], own_terms[:, :, None], 0.0),
            axis=1,
        )
        grad_logits = (placed - jnp.sum(own_terms, axis=1, keepdims=True) * gates).astype(LOW)
        terms = dot_t(grad_gate_up[0], gate_up_weight[0]) + dot_t(
            grad_gate_up[1], gate_up_weight[1]
        )
        terms = terms + dot_t(grad_logits, router_all[layer])
        grad_mixed = move.group_scatter(terms)
        grad_router = t_dot(mixed_group, grad_logits)
        grad_gate_up_weight = jnp.stack(
            [t_dot(mixed_group, grad_gate_up[e]).astype(LOW) for e in range(EXP_DEV)]
        )
        grad_down_weight = t_dot(hidden, upstream_group).astype(LOW).reshape(EXP_DEV, FF, D)
        expert_grads = (
            move.expert_scatter(grad_gate_up_weight),
            move.expert_scatter(grad_down_weight),
        )

        grad_middle, grad_second_gain = norm_backward(
            middle, gains_all[layer, :, 1], grad_mixed
        )
        grad_middle = grad_middle + upstream
        grad_middle_low = grad_middle.astype(LOW)
        grad_output_weight = move.dense_scatter(t_dot(attended.astype(LOW), grad_middle_low))
        grad_attended = dot_t(grad_middle_low, output_weight).astype(LOW)
        grad_heads = heads_first(grad_attended)
        delta = jnp.sum(grad_heads.astype(WIDE) * heads_first(attended), axis=-1, keepdims=True)
        key_heads = keys_values[:, :KVW].reshape(group_rows, KV_HEADS, HEAD)
        value_heads = keys_values[:, KVW:].reshape(group_rows, KV_HEADS, HEAD)
        grad_probs = jnp.einsum(
            "kqh,nkh->kqn", grad_heads, value_heads, preferred_element_type=WIDE
        )
        grad_scores = (probs.astype(WIDE) * (grad_probs - delta) * score_scale).astype(LOW)
        grad_queries = jnp.einsum(
            "kqn,nkh->kqh", grad_scores, key_heads, preferred_element_type=WIDE
        )
        grad_keys = jnp.einsum(
            "kqn,kqh->nkh", grad_scores, queries, preferred_element_type=WIDE
        )
        grad_values = jnp.einsum(
            "kqn,kqh->nkh", probs, grad_heads, preferred_element_type=WIDE
        )
        grad_keys_values = move.group_scatter(
            jnp.concatenate(
                [grad_keys.reshape(group_rows, KVW), grad_values.reshape(group_rows, KVW)], axis=1
            )
        )
        grad_queries = rotate(
            heads_last(grad_queries).reshape(row_count, HEADS, HEAD), cosine, -sine_table
        ).reshape(row_count, HQ)
        grad_keys = rotate(
            grad_keys_values[:, :KVW].reshape(row_count, KV_HEADS, HEAD), cosine, -sine_table
        ).reshape(row_count, KVW)
        grad_joined = jnp.concatenate(
            [grad_queries, grad_keys, grad_keys_values[:, KVW:]], axis=1
        ).astype(LOW)
        grad_query_weight = t_dot(grad_joined, normed)
        grad_normed = dot(grad_joined, query_weight)
        grad_input, grad_first_gain = norm_backward(
            layer_value, gains_all[layer, :, 0], grad_normed
        )
        grad_input = grad_input + grad_middle
        small_terms = jnp.concatenate(
            [grad_router, grad_first_gain[:, None], grad_second_gain[:, None]], axis=1
        )
        return (grad_input, grad_query_weight, grad_output_weight, expert_grads, small_terms)

    layer_value = tokens.astype(WIDE)
    stored = []
    for layer in range(LAYERS):
        layer_value, kept = forward_layer(layer, layer_value)
        stored.append(kept)
    upstream = cotangent.astype(WIDE)
    upstream_group = cotangent_group
    query_grads, output_grads, expert_grads, small_terms = ([None] * LAYERS for _ in range(4))
    for layer in reversed(range(LAYERS)):
        if layer < LAYERS - 1:
            upstream_group = move.group_gather(upstream.astype(LOW))
        upstream, query_terms, output_grads[layer], expert_grads[layer], small_terms[layer] = (
            backward_layer(layer, upstream, upstream_group, stored[layer])
        )
        if layer > 0:
            query_grads[layer] = move.dense_scatter(query_terms)
    small_grads = jnp.stack(small_terms).reshape(LAYERS, device_count, part_rows, small_width)
    small_grads = small_grads.transpose(1, 0, 2, 3).reshape(device_count, -1)
    small_size = small_grads.shape[1]
    extra_rows = -(-small_size // (8 * D)) * 8
    small_grads = jnp.pad(small_grads, ((0, 0), (0, extra_rows * D - small_size)))
    query_rows = query_terms.shape[0] // device_count
    last_terms = jnp.concatenate(
        [
            query_terms.astype(LOW).reshape(device_count, query_rows, D),
            small_grads.astype(LOW).reshape(device_count, extra_rows, D),
        ],
        axis=1,
    )
    last_grads = move.dense_scatter(last_terms.reshape(-1, D))
    query_grads[0] = last_grads[:query_rows]
    small_grads = last_grads[query_rows:].reshape(-1)[:small_size]
    small_grads = small_grads.reshape(LAYERS, part_rows, small_width)
    return (
        layer_value,
        upstream,
        jnp.stack(query_grads),
        jnp.stack(output_grads),
        small_grads[:, :, :expert_count],
        small_grads[:, :, expert_count:],
        jnp.stack([pair[0] for pair in expert_grads]),
        jnp.stack([pair[1] for pair in expert_grads]),
    )


def solution(mesh):
    sizes = dict(mesh.shape)
    square_line = (sizes["dp"], sizes["cp"]) == (4, 2 * LINE)
    return jax.shard_map(
        square_line_shards if square_line else any_mesh_shards,
        mesh=mesh,
        in_specs=(
            P(("dp", "cp"), None),
            P(("dp", "cp"), None),
            P("dp", None),
            P(None, ("dp", "cp"), None),
            P(None, ("dp", "cp"), None),
            P(None, ("dp", "cp"), None),
            P(None, ("dp", "cp"), None),
            P(None, ("dp", "cp"), None),
            P(None, "cp", "dp", None),
            P(None, "cp", "dp", None),
        ),
        out_specs=(
            P(("dp", "cp"), None),
            P(("dp", "cp"), None),
            P(None, ("dp", "cp"), None),
            P(None, ("dp", "cp"), None),
            P(None, ("dp", "cp"), None),
            P(None, ("dp", "cp"), None),
            P(None, "cp", "dp", None),
            P(None, "cp", "dp", None),
        ),
        check_vma=False,
    )
```

```python
import jax
import jax.numpy as jnp
from jax import lax
from jax.experimental import pallas as pl
from jax.experimental.pallas import tpu as pltpu
from jax.sharding import PartitionSpec as P

D = 1536
HEADS = 12
KV_HEADS = 2
HEAD = 128
FF = 768
TOP = 4
EXP_DEV = 2
LAYERS = 2
DOCS = 4
HQ = 1536
KVW = 256
QKV = 2048
Q_PER_KV = 6

EPSILON = 1e-06
MASKED = -1e30
LOW = jnp.bfloat16
WIDE = jnp.float32


def inverse_rms(values):
    return lax.rsqrt(jnp.mean(values * values, axis=-1, keepdims=True) + EPSILON)


def norm_backward(values, gain, upstream):
    scale_rows = inverse_rms(values)
    weighted = gain * upstream
    inner_mean = jnp.mean(values * weighted, axis=-1, keepdims=True)
    grad_values = scale_rows * weighted - values * scale_rows * scale_rows * scale_rows * inner_mean
    grad_gain = jnp.sum(values * scale_rows * upstream, axis=0)
    return (grad_values, grad_gain)


def doc_places(token_index, lengths_row):
    starts = jnp.cumsum(lengths_row) - lengths_row
    segment = jnp.sum((token_index[:, None] >= starts[None, 1:]).astype(jnp.int32), axis=1)
    picked = segment[:, None] == jnp.arange(DOCS, dtype=jnp.int32)[None, :]
    offset = jnp.sum(jnp.where(picked, starts[None, :], 0), axis=1)
    return (segment, token_index - offset)


def rope_tables(positions):
    half_width = HEAD // 2
    frequency = jnp.exp(-jnp.log(10000.0) * 2.0 * jnp.arange(half_width, dtype=WIDE) / HEAD)
    angles = positions.astype(WIDE)[:, None] * frequency[None, :]
    return (jnp.cos(angles)[:, None, :], jnp.sin(angles)[:, None, :])


def rotate(values, cosine, sine_table):
    half_width = values.shape[-1] // 2
    former = values[..., :half_width]
    latter = values[..., half_width:]
    return jnp.concatenate(
        [former * cosine - latter * sine_table, latter * cosine + former * sine_table], axis=-1
    )


def heads_first(values):
    token_rows = values.shape[0]
    shaped = values.reshape(token_rows, KV_HEADS, Q_PER_KV, HEAD).transpose(1, 2, 0, 3)
    return shaped.reshape(KV_HEADS, Q_PER_KV * token_rows, HEAD)


def heads_last(values):
    token_rows = values.shape[1] // Q_PER_KV
    shaped = values.reshape(KV_HEADS, Q_PER_KV, token_rows, HEAD).transpose(2, 0, 1, 3)
    return shaped.reshape(token_rows, HQ)


def dot(left, right):
    return jnp.dot(left, right, preferred_element_type=WIDE)


def dot_t(left, right):
    return lax.dot_general(left, right, (((1,), (1,)), ((), ())), preferred_element_type=WIDE)


def t_dot(left, right):
    return lax.dot_general(left, right, (((0,), (0,)), ((), ())), preferred_element_type=WIDE)


ROWS = 128
LINE = 4
GROUP = 2 * LINE * ROWS
HALF = GROUP // 2
QROWS = QKV // 32
OROWS = HQ // 32
GROWS = D // 4
FROWS = FF // 4
SMALL = 16
EXPERTS = 2 * LINE * EXP_DEV


def cost(microseconds):
    return pl.CostEstimate(flops=0, bytes_accessed=int(microseconds * 3.7e6), transcendentals=0)


LIMIT = 60 * 1024 * 1024
SCALE = HEAD**-0.5


def shape(dims, dtype):
    return jax.ShapeDtypeStruct(dims, dtype)


def spec(shape, index=None):
    if index is None:
        index = lambda *unused: (0,) * len(shape)
    return pl.BlockSpec(shape, index)


ANYWHERE = pl.BlockSpec(memory_space=pl.ANY)
SCALARS = pl.BlockSpec(memory_space=pltpu.SMEM)


def after(values, *earlier):
    several = isinstance(values, (tuple, list))
    group = list(values) if several else [values]
    result = pl.pallas_call(
        lambda *refs: None,
        out_shape=[shape(v.shape, v.dtype) for v in group],
        in_specs=[ANYWHERE] * (len(group) + len(earlier)),
        out_specs=[ANYWHERE] * len(group),
        input_output_aliases={i: i for i in range(len(group))},
        name="after",
        cost_estimate=cost(0),
    )(*group, *earlier)
    return result if several else result[0]


def place_scalars():
    dp, cp = lax.axis_index("dp"), lax.axis_index("cp")
    return jnp.stack([dp, cp % 2, cp, cp // 2]).astype(jnp.int32)


def call(body, name, grid, arguments, in_specs, outs, out_specs, scratch, microseconds, earlier=()):
    count = len(arguments)
    arguments = [*arguments, *earlier]
    in_specs = [*in_specs, *[ANYWHERE] * len(earlier)]

    def whole(*refs):
        body(*refs[:count], *refs[len(arguments) :])

    return pl.pallas_call(
        whole,
        grid=grid,
        out_shape=outs,
        in_specs=in_specs,
        out_specs=out_specs,
        scratch_shapes=scratch,
        name=name,
        compiler_params=pltpu.CompilerParams(vmem_limit_bytes=LIMIT),
        cost_estimate=cost(microseconds),
    )(*arguments)


class Dense:
    def __init__(self, pieces, first_row, rows):
        self.pieces = pieces
        self.rows = rows
        self.first_row = first_row

    def arrays(self):
        return [piece[0] for piece in self.pieces]

    def copies(self, refs, places, scratch, sems):
        made = []
        for number, (ref, piece) in enumerate(zip(refs, self.pieces)):
            unused, part, flip, other, chip, chips = piece
            rows = pl.ds(self.first_row, self.rows)
            source = ref.at[:, rows] if part is None else ref.at[:, part, rows]
            target = scratch.at[places[0] ^ flip, pl.ds(chip, chips), places[1] ^ other]
            made.append(pltpu.make_async_copy(source, target, sems.at[number]))
        return made

    def scratch(self):
        return [
            pltpu.VMEM((4, LINE, 2, self.rows, D), LOW),
            pltpu.SemaphoreType.DMA((len(self.pieces),)),
        ]


def expert_copies(refs, places, gate_up, down, sems):
    made = []
    for expert in range(EXP_DEV):
        for flip in range(4):
            part = places[0] ^ flip
            far = refs[9 + expert]
            first = pl.multiple_of(part * GROWS, GROWS)
            source = refs[3 * expert + flip] if flip < 3 else far.at[pl.ds(0, GROWS)]
            made.append((source, gate_up.at[expert, pl.ds(first, GROWS)]))
            first = pl.multiple_of(part * FROWS, FROWS)
            source = refs[6 + flip].at[expert] if flip < 3 else far.at[pl.ds(GROWS, FROWS)]
            made.append((source, down.at[expert, pl.ds(first, FROWS)]))
    return [
        pltpu.make_async_copy(source, target, sems.at[number])
        for number, (source, target) in enumerate(made)
    ]


EXPERT_SCRATCH = [
    pltpu.VMEM((EXP_DEV, D, 2 * FF), LOW),
    pltpu.VMEM((EXP_DEV, FF, D), LOW),
    pltpu.SemaphoreType.DMA((16,)),
]


def logistic_of(values):
    return 0.5 * jnp.tanh(0.5 * values) + 0.5


def norm_rows(values, gain):
    return (values * inverse_rms(values) * gain).astype(LOW)


def turn(values, cosine, sine):
    return values * cosine + pltpu.roll(values, HEAD // 2, 1) * sine


def small_call(pieces):
    count = len(pieces.pieces)

    def body(places, *rest):
        refs, (out, sems) = rest[:count], rest[count:]
        copies = pieces.copies(refs, places, out, sems)
        for copy in copies:
            copy.start()
        for copy in copies:
            copy.wait()

    out = shape((4, LINE, 2, SMALL, D), LOW)
    return call(
        body,
        "small",
        (),
        [place_scalars(), *pieces.arrays()],
        [SCALARS] + [ANYWHERE] * count,
        out,
        spec(out.shape),
        [pltpu.SemaphoreType.DMA((count,))],
        0,
    )


def project_call(value, gain, query, tables, earlier=()):
    count = len(query.pieces)

    def body(places, value_ref, gain_ref, tables_ref, *rest):
        refs, (normed_ref, heads_ref, kv_ref, weight, sems, joined) = rest[:count], rest[count:]
        copies = query.copies(refs, places, weight, sems)
        for copy in copies:
            copy.start()
        normed = norm_rows(value_ref[...], gain_ref[...])
        normed_ref[...] = normed
        for copy in copies:
            copy.wait()
        for part in range(4):
            joined[part] = dot_t(normed, weight[part].reshape(8 * QROWS, D))
        cosine, sine = tables_ref[0], tables_ref[1]
        for head in range(HEADS + 2 * KV_HEADS):
            at = pl.ds(head % 4 * HEAD, HEAD)
            values = joined[head // 4, :, at]
            if head < HEADS:
                heads_ref[head] = turn(values, cosine, sine).astype(LOW)
            else:
                if head < HEADS + KV_HEADS:
                    values = turn(values, cosine, sine)
                kv_ref[:, pl.ds((head - HEADS) * HEAD, HEAD)] = values.astype(LOW)

    outs = [shape((ROWS, D), LOW), shape((HEADS, ROWS, HEAD), LOW), shape((ROWS, 2 * KVW), LOW)]
    arguments = [place_scalars(), value, gain, tables, *query.arrays()]
    return call(
        body,
        "project",
        (),
        arguments,
        [SCALARS, spec((ROWS, D)), spec((1, D)), spec((2, ROWS, HEAD))] + [ANYWHERE] * count,
        outs,
        [spec(o.shape) for o in outs],
        [*query.scratch(), pltpu.VMEM((4, ROWS, 8 * QROWS), WIDE)],
        0,
        earlier,
    )


def attend_call(value, heads, keys_values, query_meta, key_meta, output, gain, earlier=()):
    count = len(output.pieces)

    def body(places, value_ref, heads_ref, kv_own, kv_other, qmeta, kmeta, gain_ref, *rest):
        refs, (low_ref, probs_ref, middle_ref, mixed_ref, weight, sems, joined, kv_ref) = (
            rest[:count],
            rest[count:],
        )
        copies = output.copies(refs, places, weight, sems)
        for copy in copies:
            copy.start()
        kv_ref[pl.ds(0, HALF)] = kv_own[...]
        kv_ref[pl.ds(HALF, HALF)] = kv_other[...]
        allowed = (qmeta[:, 1:2] == kmeta[1:2, :]) & (kmeta[0:1, :] <= qmeta[:, 0:1])
        for head in range(HEADS):
            kv = head // Q_PER_KV
            keys = kv_ref[:, pl.ds(kv * HEAD, HEAD)]
            vals = kv_ref[:, pl.ds(KVW + kv * HEAD, HEAD)]
            scores = dot_t(heads_ref[head], keys) * SCALE
            scores = jnp.where(allowed, scores, MASKED)
            shares = jnp.exp(scores - jnp.max(scores, axis=1, keepdims=True))
            probs = (shares * (1.0 / jnp.sum(shares, axis=1, keepdims=True))).astype(LOW)
            probs_ref[head] = probs
            joined[:, pl.ds(head * HEAD, HEAD)] = dot(probs, vals).astype(LOW)
        low = joined[...]
        low_ref[...] = low
        for copy in copies:
            copy.wait()
        middle = value_ref[...] + dot(low, weight[...].reshape(HQ, D))
        middle_ref[...] = middle
        mixed_ref[...] = norm_rows(middle, gain_ref[...])

    outs = [
        shape((ROWS, HQ), LOW),
        shape((HEADS, ROWS, GROUP), LOW),
        shape((ROWS, D), WIDE),
        shape((ROWS, D), LOW),
    ]
    arguments = [
        place_scalars(),
        value,
        heads,
        *keys_values,
        query_meta,
        key_meta,
        gain,
        *output.arrays(),
    ]
    return call(
        body,
        "attend",
        (),
        arguments,
        [
            SCALARS,
            spec((ROWS, D)),
            spec((HEADS, ROWS, HEAD)),
            spec((HALF, 2 * KVW)),
            spec((HALF, 2 * KVW)),
            spec((ROWS, 2)),
            spec((2, GROUP)),
            spec((1, D)),
        ]
        + [ANYWHERE] * count,
        outs,
        [spec(o.shape) for o in outs],
        [*output.scratch(), pltpu.VMEM((ROWS, HQ), LOW), pltpu.VMEM((GROUP, 2 * KVW), LOW)],
        0,
        earlier,
    )


BLOCK = 256
STEPS = GROUP // BLOCK


def own_half(step):
    return (jnp.minimum(step, STEPS // 2 - 1), 0)


def other_half(step):
    return (jnp.maximum(step - STEPS // 2, 0), 0)


def rows_at(step):
    return (step, 0)


def take_half(step, own_ref, other_ref):
    return jnp.where(step < STEPS // 2, own_ref[...], other_ref[...])


def put_halves(step, own_ref, other_refs, values):
    @pl.when(step < STEPS // 2)
    def own():
        own_ref[...] = values

    for number, ref in enumerate(other_refs):

        @pl.when(step == STEPS // 2 + number)
        def other():
            ref[...] = values


def own_gate(gates, places, expert):
    ids = lax.broadcasted_iota(jnp.int32, gates.shape, 1)
    return jnp.sum(
        jnp.where(ids == EXP_DEV * places[2] + expert, gates, 0.0), axis=1, keepdims=True
    )


def experts_call(mixed, routes, router, pieces, earlier=()):
    def body(places, mixed_own, mixed_other, routes_ref, router_ref, *rest):
        refs, (own_ref, *other_refs, gu_ref, hidden_ref, gates_ref, gate_up, down, sems) = (
            rest[:11],
            rest[11:],
        )
        step = pl.program_id(0)
        copies = expert_copies(refs, places, gate_up, down, sems)

        @pl.when(step == 0)
        def begin():
            for copy in copies:
                copy.start()
            for copy in copies:
                copy.wait()

        mixed_rows = take_half(step, mixed_own, mixed_other)
        logits = dot(mixed_rows, router_ref[...])
        ids = lax.broadcasted_iota(jnp.int32, (BLOCK, EXPERTS), 1)
        chosen = routes_ref[:, 0:1] == ids
        for k in range(1, TOP):
            chosen = chosen | (routes_ref[:, k : k + 1] == ids)
        logits = jnp.where(chosen, logits, MASKED)
        shares = jnp.where(chosen, jnp.exp(logits - jnp.max(logits, axis=1, keepdims=True)), 0.0)
        gates = shares / jnp.sum(shares, axis=1, keepdims=True)
        gates_ref[...] = gates

        terms = None
        for expert in range(EXP_DEV):
            gu = dot(mixed_rows, gate_up[expert])
            gu_ref[:, pl.ds(expert * 2 * FF, 2 * FF)] = gu.astype(LOW)
            gate_part = gu[:, :FF]
            hidden = gate_part * logistic_of(gate_part) * gu[:, FF:]
            hidden = (hidden * own_gate(gates, places, expert)).astype(LOW)
            hidden_ref[:, pl.ds(expert * FF, FF)] = hidden
            product = dot(hidden, down[expert])
            terms = product if terms is None else terms + product
        put_halves(step, own_ref, other_refs, terms.astype(LOW))

    outs = [
        shape((HALF, D), LOW),
        shape((BLOCK, D), LOW),
        shape((BLOCK, D), LOW),
        shape((GROUP, EXP_DEV * 2 * FF), LOW),
        shape((GROUP, EXP_DEV * FF), LOW),
        shape((GROUP, EXPERTS), WIDE),
    ]
    return call(
        body,
        "experts",
        (STEPS,),
        [place_scalars(), *mixed, routes, router, *pieces],
        [
            SCALARS,
            spec((BLOCK, D), own_half),
            spec((BLOCK, D), other_half),
            spec((BLOCK, TOP), rows_at),
            spec((D, EXPERTS)),
        ]
        + [ANYWHERE] * 11,
        outs,
        [
            spec((BLOCK, D), own_half),
            spec((BLOCK, D)),
            spec((BLOCK, D)),
            spec((BLOCK, EXP_DEV * 2 * FF), rows_at),
            spec((BLOCK, EXP_DEV * FF), rows_at),
            spec((BLOCK, EXPERTS), rows_at),
        ],
        EXPERT_SCRATCH,
        8,
        earlier,
    )


def experts_back_call(upstream, gate_up_kept, gates, router, pieces, earlier=()):
    def body(places, up_own, up_other, gu_ref, gates_ref, router_ref, *rest):
        refs, (own_ref, *other_refs, grad_ref, logits_ref, gate_up, down, sems) = (
            rest[:11],
            rest[11:],
        )
        step = pl.program_id(0)
        copies = expert_copies(refs, places, gate_up, down, sems)

        @pl.when(step == 0)
        def begin():
            for copy in copies:
                copy.start()
            for copy in copies:
                copy.wait()

        upstream_rows = take_half(step, up_own, up_other)
        gates = gates_ref[...]
        ids = lax.broadcasted_iota(jnp.int32, (BLOCK, EXPERTS), 1)
        grad_logits = jnp.zeros((BLOCK, EXPERTS), WIDE)
        terms = None
        for expert in range(EXP_DEV):
            bare = dot_t(upstream_rows, down[expert])
            gate_part = gu_ref[:, pl.ds(expert * 2 * FF, FF)].astype(WIDE)
            up_part = gu_ref[:, pl.ds(expert * 2 * FF + FF, FF)].astype(WIDE)
            gate = own_gate(gates, places, expert)
            logistic = logistic_of(gate_part)
            activated = gate_part * logistic
            share = gate * jnp.sum(bare * activated * up_part, axis=1, keepdims=True)
            mine = jnp.where(ids == EXP_DEV * places[2] + expert, 1.0, 0.0)
            grad_logits = grad_logits + share * (mine - gates)
            gated = bare * gate
            grad_gate = gated * up_part * logistic * (1.0 + gate_part * (1.0 - logistic))
            grad_gate = grad_gate.astype(LOW)
            grad_up = (gated * activated).astype(LOW)
            grad_ref[:, pl.ds(expert * 2 * FF, FF)] = grad_gate
            grad_ref[:, pl.ds(expert * 2 * FF + FF, FF)] = grad_up
            grad_both = jnp.concatenate([grad_gate, grad_up], axis=1)
            product = dot_t(grad_both, gate_up[expert])
            terms = product if terms is None else terms + product
        grad_logits = grad_logits.astype(LOW)
        terms = terms + dot(grad_logits, router_ref[...])
        put_halves(step, own_ref, other_refs, terms.astype(LOW))
        logits_ref[...] = grad_logits

    outs = [
        shape((HALF, D), LOW),
        shape((BLOCK, D), LOW),
        shape((BLOCK, D), LOW),
        shape((GROUP, EXP_DEV * 2 * FF), LOW),
        shape((GROUP, EXPERTS), LOW),
    ]
    return call(
        body,
        "experts_back",
        (STEPS,),
        [place_scalars(), *upstream, gate_up_kept, gates, router, *pieces],
        [
            SCALARS,
            spec((BLOCK, D), own_half),
            spec((BLOCK, D), other_half),
            spec((BLOCK, EXP_DEV * 2 * FF), rows_at),
            spec((BLOCK, EXPERTS), rows_at),
            spec((EXPERTS, D)),
        ]
        + [ANYWHERE] * 11,
        outs,
        [
            spec((BLOCK, D), own_half),
            spec((BLOCK, D)),
            spec((BLOCK, D)),
            spec((BLOCK, EXP_DEV * 2 * FF), rows_at),
            spec((BLOCK, EXPERTS), rows_at),
        ],
        EXPERT_SCRATCH,
        8,
        earlier,
    )


def expert_grads_call(
    flips, mixed, grad_gate_up, hidden, upstream, received=(), layer=None, results=None, earlier=()
):
    last = layer is not None
    kept = () if results is None else tuple(results)
    count = len(flips)

    def body(places, *rest):
        mixed_refs, rest = rest[: 2 * count], rest[2 * count :]
        hidden_refs, rest = rest[: 2 * count], rest[2 * count :]
        grad_ref, up_own, up_other = rest[:3]
        sums, outs = rest[3 : 3 + len(received)], rest[3 + len(received) + len(kept) + len(earlier) :]
        expert = pl.program_id(0)
        for number, flip in enumerate(flips):
            gate_up = t_dot(mixed_refs[2 * number][...], grad_ref[pl.ds(0, HALF)])
            gate_up = gate_up + t_dot(mixed_refs[2 * number + 1][...], grad_ref[pl.ds(HALF, HALF)])
            both = jnp.concatenate([hidden_refs[2 * number][...], hidden_refs[2 * number + 1][...]], axis=1)
            down = t_dot(both[:HALF], up_own[...]) + t_dot(both[HALF:], up_other[...])
            part = places[0] ^ flip
            down = jnp.where(part % 2 == 0, down[:FROWS], down[2 * HEAD - FROWS :])
            for ref, (unused, whose, only) in zip(sums, received):
                if whose != number:
                    continue
                held = jnp.where(expert == only, ref[...].astype(WIDE), 0.0)
                gate_up = gate_up + held[:GROWS]
                down = down + held[GROWS:]
            if last:
                outs[0][0, 0] = gate_up
                outs[1][0, 0] = down
                continue
            gate_up = gate_up.astype(LOW)
            down = down.astype(LOW)
            for own in range(EXP_DEV):

                @pl.when(expert == own)
                def put():
                    outs[EXP_DEV * number + own][pl.ds(0, GROWS)] = gate_up
                    outs[EXP_DEV * number + own][pl.ds(GROWS, FROWS)] = down

    whole = lambda e, places: (0, 0)
    if last:
        at_layer = lambda e, places: (layer, e, 0, 0)
        outs = [shape((LAYERS, EXP_DEV, GROWS, D), WIDE), shape((LAYERS, EXP_DEV, FROWS, D), WIDE)]
        out_specs = [
            pl.BlockSpec((1, 1, GROWS, D), at_layer),
            pl.BlockSpec((1, 1, FROWS, D), at_layer),
        ]
    else:
        outs = [shape((GROWS + FROWS, D), LOW)] * (count * EXP_DEV)
        out_specs = [pl.BlockSpec((GROWS + FROWS, D), whole)] * (count * EXP_DEV)
    in_specs = []
    for flip in flips:
        in_specs += [pl.BlockSpec((HALF, GROWS), lambda e, places, flip=flip: (0, places[0] ^ flip))] * 2
    for flip in flips:
        for side in range(2):
            in_specs.append(
                pl.BlockSpec(
                    (GROUP, HEAD),
                    lambda e, places, flip=flip, side=side: (
                        0,
                        e * (FF // HEAD) + (places[0] ^ flip) * 3 // 2 + side,
                    ),
                )
            )
    in_specs += [
        pl.BlockSpec((GROUP, 2 * FF), lambda e, places: (0, e)),
        pl.BlockSpec((HALF, D), whole),
        pl.BlockSpec((HALF, D), whole),
    ]
    in_specs += [pl.BlockSpec((GROWS + FROWS, D), whole)] * len(received)
    in_specs += [ANYWHERE] * (len(kept) + len(earlier))
    first_kept = 1 + 4 * count + 3 + len(received)
    return pl.pallas_call(
        body,
        out_shape=outs,
        input_output_aliases={first_kept + i: i for i in range(len(kept))},
        grid_spec=pltpu.PrefetchScalarGridSpec(
            num_scalar_prefetch=1, grid=(EXP_DEV,), in_specs=in_specs, out_specs=out_specs
        ),
        name="expert_grads",
        compiler_params=pltpu.CompilerParams(vmem_limit_bytes=LIMIT),
        cost_estimate=cost(4 if last else 0),
    )(
        place_scalars(),
        *(list(mixed) * count),
        *([hidden] * (2 * count)),
        grad_gate_up,
        *upstream,
        *(array for array, unused, only in received),
        *kept,
        *earlier,
    )


def norm_back(values, gain, upstream):
    scale_rows = inverse_rms(values)
    weighted = gain * upstream
    inner_mean = jnp.mean(values * weighted, axis=1, keepdims=True)
    grads = scale_rows * (weighted - values * (scale_rows * scale_rows * inner_mean))
    return (grads, jnp.sum(values * scale_rows * upstream, axis=0, keepdims=True))


def attend_back_call(
    grad_mixed, middle, gain, upstream, output, low, probs, heads, keys_values, earlier=()
):
    count = len(output.pieces)

    def body(
        places, gm_ref, middle_ref, gain_ref, up_ref, low_in, probs_ref, heads_ref, kv_own, kv_other, *rest
    ):
        refs, (grad_ref, error_ref, gq_ref, own_ref, other_ref, gg_ref, weight, sems, kvs, kv_ref) = (
            rest[:count],
            rest[count:],
        )
        copies = output.copies(refs, places, weight, sems)
        for copy in copies:
            copy.start()
        kv_ref[pl.ds(0, HALF)] = kv_own[...]
        kv_ref[pl.ds(HALF, HALF)] = kv_other[...]
        grads, gain_grad = norm_back(middle_ref[...], gain_ref[...], gm_ref[...])
        gg_ref[...] = gain_grad
        grads = grads + up_ref[...]
        grad_ref[...] = grads
        error = grads.astype(LOW)
        error_ref[...] = error
        for copy in copies:
            copy.wait()
        grad_attended = dot_t(error, weight[...].reshape(HQ, D)).astype(LOW)
        for head in range(HEADS):
            kv = head // Q_PER_KV
            at = pl.ds(kv * HEAD, HEAD)
            at_values = pl.ds(KVW + kv * HEAD, HEAD)
            grad_head = grad_attended[:, head * HEAD : (head + 1) * HEAD]
            delta = jnp.sum(
                grad_head.astype(WIDE) * low_in[:, pl.ds(head * HEAD, HEAD)].astype(WIDE),
                axis=1,
                keepdims=True,
            )
            shares = probs_ref[head]
            grad_scores = dot_t(grad_head, kv_ref[:, at_values]) - delta
            grad_scores = (shares.astype(WIDE) * grad_scores * SCALE).astype(LOW)
            gq_ref[head] = dot(grad_scores, kv_ref[:, at])
            grad_keys = t_dot(grad_scores, heads_ref[head])
            grad_values = t_dot(shares, grad_head)
            if head % Q_PER_KV == 0:
                kvs[:, at] = grad_keys
                kvs[:, at_values] = grad_values
            else:
                kvs[:, at] += grad_keys
                kvs[:, at_values] += grad_values
        own_ref[...] = kvs[pl.ds(0, HALF)].astype(LOW)
        other_ref[...] = kvs[pl.ds(HALF, HALF)].astype(LOW)

    outs = [
        shape((ROWS, D), WIDE),
        shape((ROWS, D), LOW),
        shape((HEADS, ROWS, HEAD), WIDE),
        shape((HALF, 2 * KVW), LOW),
        shape((HALF, 2 * KVW), LOW),
        shape((1, D), WIDE),
    ]
    arguments = [
        place_scalars(),
        grad_mixed,
        middle,
        gain,
        upstream,
        low,
        probs,
        heads,
        *keys_values,
        *output.arrays(),
    ]
    return call(
        body,
        "attend_back",
        (),
        arguments,
        [SCALARS] + [spec(a.shape) for a in arguments[1:10]] + [ANYWHERE] * count,
        outs,
        [spec(o.shape) for o in outs],
        [*output.scratch(), pltpu.VMEM((GROUP, 2 * KVW), WIDE), pltpu.VMEM((GROUP, 2 * KVW), LOW)],
        0,
        earlier,
    )


def project_back_call(grad_heads, grad_kv, tables, query, value, gain, grad_middle, earlier=()):
    count = len(query.pieces)

    def body(places, gq_ref, gkv_ref, tables_ref, value_ref, gain_ref, gm_ref, *rest):
        refs, (joined_ref, grad_ref, low_ref, gg_ref, weight, sems) = rest[:count], rest[count:]
        copies = query.copies(refs, places, weight, sems)
        for copy in copies:
            copy.start()
        cosine, sine = tables_ref[0], -tables_ref[1]
        for head in range(HEADS + 2 * KV_HEADS):
            if head < HEADS:
                values = turn(gq_ref[head], cosine, sine)
            else:
                values = gkv_ref[:, pl.ds((head - HEADS) * HEAD, HEAD)]
                if head < HEADS + KV_HEADS:
                    values = turn(values, cosine, sine)
            joined_ref[:, pl.ds(head * HEAD, HEAD)] = values.astype(LOW)
        for copy in copies:
            copy.wait()
        grad_normed = dot(joined_ref[...], weight[...].reshape(QKV, D))
        grads, gain_grad = norm_back(value_ref[...], gain_ref[...], grad_normed)
        gg_ref[...] = gain_grad
        grads = grads + gm_ref[...]
        grad_ref[...] = grads
        low_ref[...] = grads.astype(LOW)

    outs = [
        shape((ROWS, QKV), LOW),
        shape((ROWS, D), WIDE),
        shape((ROWS, D), LOW),
        shape((1, D), WIDE),
    ]
    arguments = [
        place_scalars(),
        grad_heads,
        grad_kv,
        tables,
        value,
        gain,
        grad_middle,
        *query.arrays(),
    ]
    return call(
        body,
        "project_back",
        (),
        arguments,
        [SCALARS] + [spec(a.shape) for a in arguments[1:7]] + [ANYWHERE] * count,
        outs,
        [spec(o.shape) for o in outs],
        query.scratch(),
        0,
        earlier,
    )


def dense_grads_call(joined, normed, low, error, small, earlier=()):
    rows = QROWS + OROWS + (SMALL if small is not None else 0)

    def body(places, joined_ref, normed_ref, low_ref, error_ref, *rest):
        mine_refs, other_refs = rest[-8:-4], rest[-4:]
        flip = pl.program_id(0)
        query = t_dot(joined_ref[...], normed_ref[...]).astype(LOW).reshape(LINE, 2, QROWS, D)
        outs = t_dot(low_ref[...], error_ref[...]).astype(LOW).reshape(LINE, 2, OROWS, D)
        for core in range(2):

            def put(ref):
                ref[:, pl.ds(0, QROWS)] = query[:, core]
                ref[:, pl.ds(QROWS, OROWS)] = outs[:, core]
                if small is not None:
                    ref[:, pl.ds(QROWS + OROWS, SMALL)] = rest[0][0, :, core]

            for at in range(4):

                @pl.when((flip == at) & (places[1] == core))
                def mine():
                    put(mine_refs[at])

                @pl.when((flip == at) & (places[1] != core))
                def other():
                    put(other_refs[at])

    out = shape((LINE, rows, D), LOW)
    count = len(earlier)
    part = lambda flip, places: (0, places[0] ^ flip)
    whole = lambda flip, places: (0, 0)
    in_specs = [
        pl.BlockSpec((ROWS, QKV // 4), part),
        pl.BlockSpec((ROWS, D), whole),
        pl.BlockSpec((ROWS, HQ // 4), part),
        pl.BlockSpec((ROWS, D), whole),
    ]
    arguments = [joined, normed, low, error]
    if small is not None:
        in_specs.append(
            pl.BlockSpec((1, LINE, 2, SMALL, D), lambda flip, places: (places[0] ^ flip, 0, 0, 0, 0))
        )
        arguments.append(small)
    in_specs += [ANYWHERE] * count
    out_spec = pl.BlockSpec((LINE, rows, D), lambda flip, places: (0, 0, 0))
    grads = pl.pallas_call(
        body,
        out_shape=[out] * 8,
        grid_spec=pltpu.PrefetchScalarGridSpec(
            num_scalar_prefetch=1, grid=(4,), in_specs=in_specs, out_specs=[out_spec] * 8
        ),
        name="dense_grads",
        compiler_params=pltpu.CompilerParams(vmem_limit_bytes=LIMIT),
        cost_estimate=cost(0),
    )(place_scalars(), *arguments, *earlier)
    return (grads[:4], grads[4:])


def swap_core(value):
    return lax.ppermute(value, "cp", [(i, i ^ 1) for i in range(2 * LINE)])


def hop(value, upward, sources):
    step = 1 if upward else -1
    pairs = [(2 * z + core, 2 * (z + step) + core) for z in sources for core in range(2)]
    return lax.ppermute(value, "cp", pairs)


def leap(value, distance):
    pairs = [(i, i + 2 * distance) for i in range(2 * LINE) if 0 <= i + 2 * distance < 2 * LINE]
    return lax.ppermute(value, "cp", pairs)


def across(value, flip):
    return lax.ppermute(value, "dp", [(i, i ^ flip) for i in range(4)])


def line_gather(value):
    place = lax.axis_index("cp") // 2
    rising, falling = value, value
    risen, fallen = [], []
    for step in range(1, LINE):
        rising = hop(rising, True, range(step - 1, LINE - 1))
        falling = hop(falling, False, range(1, LINE - step + 1))
        risen.insert(0, rising)
        fallen.append(falling)
    every = jnp.stack(risen + [value] + fallen)
    return lax.dynamic_slice_in_dim(every, LINE - 1 - place, LINE, 0)


def leap_gather(value):
    place = lax.axis_index("cp") // 2
    every = [leap(value, LINE - 1 - i) if i != LINE - 1 else value for i in range(2 * LINE - 1)]
    return lax.dynamic_slice_in_dim(jnp.stack(every), LINE - 1 - place, LINE, 0)


def line_scatter(parts, *stages):
    place = lax.axis_index("cp") // 2

    def pick(index):
        return lax.dynamic_index_in_dim(parts, jnp.clip(index, 0, LINE - 1), 0, keepdims=False)

    rising = falling = None
    for step in range(1, LINE):
        up = pick(LINE + place - step)
        down = pick(place - LINE + step)
        if step > 1:
            up = (up.astype(WIDE) + rising.astype(WIDE)).astype(LOW)
            down = (down.astype(WIDE) + falling.astype(WIDE)).astype(LOW)
        if step <= len(stages) and stages[step - 1]:
            up, down = after((up, down), *stages[step - 1])
        rising = hop(up, True, range(step))
        falling = hop(down, False, range(LINE - step, LINE))
    return pick(place).astype(WIDE) + rising.astype(WIDE) + falling.astype(WIDE)


def group_gather(value):
    mine = line_gather(value)
    other = swap_core(mine)
    return (mine.reshape(HALF, -1), other.reshape(HALF, -1))


def group_scatter(own, others, *stages):
    if stages and stages[0]:
        others = after(others, *stages[0])
    other = jnp.concatenate([swap_core(part) for part in others], axis=0)
    both = (own.astype(WIDE) + other.astype(WIDE)).astype(LOW)
    return line_scatter(both.reshape(LINE, ROWS, -1), *stages[1:])


def earlier_gather(value):
    mine = jnp.stack([leap(value, 3), leap(value, 2), leap(value, 1), value])
    other = swap_core(mine)
    return (mine.reshape(HALF, -1), other.reshape(HALF, -1))


def earlier_scatter(own, other):
    both = (own.astype(WIDE) + swap_core(other).astype(WIDE)).astype(LOW).reshape(LINE, ROWS, -1)
    total = both[LINE - 1].astype(WIDE)
    for distance in range(1, LINE):
        total = total + leap(both[LINE - 1 - distance], -distance).astype(WIDE)
    return total


def square_step(value):
    return (across(value, 1), across(value, 2))


def square_far(by_x, by_y):
    half = by_x.shape[0] // 2
    return (across(by_x[:half], 2), across(by_y[half:], 1))


def dense_pieces(line, by_x, by_y, far):
    held = [
        (line, 0, 0, LINE),
        (by_x, 1, 0, LINE),
        (by_y, 2, 0, LINE),
        (far[0], 3, 0, LINE // 2),
        (far[1], 3, LINE // 2, LINE // 2),
    ]
    pieces = []
    for array, flip, chip, chips in held:
        pieces.append((array, None, flip, 0, chip, chips))
        pieces.append((swap_core(array), None, flip, 1, chip, chips))
    return pieces


def dense_square_scatter(mine, others, *earlier):
    received = [swap_core(other) for other in others]

    def piece(flip):
        return mine[flip].astype(WIDE) + received[flip].astype(WIDE)

    half = LINE // 2
    far = after(piece(3).astype(LOW), *earlier)
    from_x = across(far[:half], 1)
    from_y = across(far[half:], 2)
    to_x, to_y = piece(1), piece(2)
    to_x = jnp.concatenate([to_x[:half], to_x[half:] + from_y.astype(WIDE)], axis=0).astype(LOW)
    to_y = jnp.concatenate([to_y[:half] + from_x.astype(WIDE), to_y[half:]], axis=0).astype(LOW)
    got_x = across(to_x, 1)
    got_y = across(to_y, 2)
    plane = piece(0) + got_x.astype(WIDE) + got_y.astype(WIDE)
    return ((from_x, from_y), (to_x, to_y), (got_x, got_y), plane.astype(LOW))


def in_order(own, other):
    own, other = (rows.reshape(LINE, 1, ROWS, -1) for rows in (own, other))
    first = lax.axis_index("cp") % 2 == 0
    rows = jnp.where(
        first, jnp.concatenate([own, other], axis=1), jnp.concatenate([other, own], axis=1)
    )
    return rows.reshape(GROUP, -1)


def square_line_shards(
    tokens, cotangent, doc_lengths, routes, w_qkv, w_out, router, gains, w_gate_up, w_down
):
    dp_place = lax.axis_index("dp")
    cp_place = lax.axis_index("cp")
    core = cp_place % 2
    chip = cp_place // 2
    lengths_row = doc_lengths[0]
    row_ids = jnp.arange(ROWS, dtype=jnp.int32)
    my_index = cp_place * ROWS + row_ids
    my_segment, my_position = doc_places(my_index, lengths_row)
    query_meta = jnp.stack([my_index, my_segment], axis=1)
    back = jnp.arange(LINE, dtype=jnp.int32) - (LINE - 1) + chip
    blocks = jnp.concatenate([2 * back + core, 2 * back + 1 - core])
    blocks = jnp.where(jnp.concatenate([back, back]) < 0, 4 * LINE, blocks)
    key_index = (blocks[:, None] * ROWS + row_ids[None, :]).reshape(-1)
    key_segment, unused_position = doc_places(key_index, lengths_row)
    key_meta = jnp.stack([key_index, key_segment])
    cosine, sine = rope_tables(my_position)
    cosine, sine = cosine[:, 0], sine[:, 0]
    tables = jnp.stack(
        [jnp.concatenate([cosine, cosine], axis=1), jnp.concatenate([-sine, sine], axis=1)]
    )

    small_lines = LAYERS * (EXPERTS + 2)
    own_rows = router.shape[1]
    small = jnp.concatenate([router, gains], axis=2).transpose(0, 2, 1).reshape(-1)
    small_size = small.shape[0]
    small_rows = -(-small_size // D)
    small = jnp.pad(small, (0, small_rows * D - small_size)).reshape(small_rows, D)
    route_numbers = routes.reshape(-1).astype(LOW)
    route_size = route_numbers.shape[0]
    route_numbers = jnp.pad(route_numbers, (0, D - route_size)).reshape(1, D)
    small = jnp.concatenate([small, route_numbers], axis=0)
    small = jnp.pad(small, ((0, SMALL - small_rows - 1), (0, 0)))

    own_gate_ups = [[w_gate_up[l, e] for e in range(EXP_DEV)] for l in range(LAYERS)]
    own_downs = [w_down[l] for l in range(LAYERS)]
    gate_ups = [[square_step(own_gate_ups[0][0])], []]
    first = line_gather(jnp.concatenate([w_qkv[0], w_out[0], small], axis=0))
    second = line_gather(after(jnp.concatenate([w_qkv[1], w_out[1], cotangent], axis=0), first))
    first = after(first, *gate_ups[0][0])
    dense_rows = QROWS + OROWS
    upstream_line = second[:, dense_rows:]
    second = second[:, :dense_rows]
    first_near = square_step(first)
    first_far = square_far(*first_near)
    pieces = dense_pieces(first, *first_near, first_far)
    query, output = Dense(pieces, 0, QROWS), Dense(pieces, QROWS, OROWS)
    small = small_call(Dense(pieces, dense_rows, SMALL))

    def expert_weights(layer, first, more, down, far):
        own = own_gate_ups[layer]
        return [own[0], *first, own[1], *more, own_downs[layer], *down, *far]

    def experts_far(first, more, down):
        by_x = jnp.concatenate([first[0], down[0][0]], axis=0)
        by_y = jnp.concatenate([more[1], down[1][1]], axis=0)
        by_x, by_y = after((by_x, by_y), *more, *down)
        return (across(by_x, 2), across(by_y, 1))

    own_gate_ups[0][1] = after(own_gate_ups[0][1], *first_far)
    gate_ups[0].append(square_step(own_gate_ups[0][1]))
    own_downs[0] = after(own_downs[0], *first_far)
    downs = [square_step(own_downs[0])]
    fars = [experts_far(*gate_ups[0], downs[0])]
    weights = [(query, output, expert_weights(0, *gate_ups[0], downs[0], fars[0]))]
    second = after(second, *fars[0])
    second_near = square_step(second)
    second_far = square_far(*second_near)
    pieces = dense_pieces(second, *second_near, second_far)
    query, output = Dense(pieces, 0, QROWS), Dense(pieces, QROWS, OROWS)
    own_gate_ups[1][0] = after(own_gate_ups[1][0], *second_far)
    gate_ups[1].append(square_step(own_gate_ups[1][0]))
    own_gate_ups[1][1] = after(own_gate_ups[1][1], *gate_ups[1][0])
    gate_ups[1].append(square_step(own_gate_ups[1][1]))
    own_downs[1] = after(own_downs[1], *gate_ups[1][0])
    downs.append(square_step(own_downs[1]))
    fars.append(experts_far(*gate_ups[1], downs[1]))
    weights.append((query, output, expert_weights(1, *gate_ups[1], downs[1], fars[1])))

    shared = small.reshape(-1, SMALL, D)
    lines = shared[:, :small_rows].reshape(-1, small_rows * D)[:, :small_size]
    lines = lines.reshape(-1, small_lines, own_rows).transpose(1, 0, 2).reshape(small_lines, D)
    lines = lines.reshape(LAYERS, EXPERTS + 2, D)
    routers = lines[:, :EXPERTS]
    gain_rows = lines[:, EXPERTS:].astype(WIDE)[:, :, None]
    numbers = lax.dynamic_index_in_dim(small, dp_place, 0, keepdims=False)
    numbers = numbers[:, :, small_rows, :route_size]
    numbers = jnp.where(core == 0, numbers, numbers[:, ::-1]).astype(jnp.int32)
    numbers = numbers.reshape(LINE, 2, LAYERS, ROWS, TOP).transpose(2, 1, 0, 3, 4)
    group_routes = numbers.reshape(LAYERS, GROUP, TOP)

    value = tokens.astype(WIDE)
    before_project = [(), gate_ups[1][0]]
    before_attend = [(upstream_line, routers, group_routes), ()]
    stored = []
    for layer in range(LAYERS):
        query, output, pieces = weights[layer]
        normed, heads, kv = project_call(
            value, gain_rows[layer, 0], query, tables, before_project[layer]
        )
        keys_values = earlier_gather(kv)
        low, probs, middle, mixed = attend_call(
            value,
            heads,
            keys_values,
            query_meta,
            key_meta,
            output,
            gain_rows[layer, 1],
            before_attend[layer],
        )
        mixed = group_gather(mixed)
        own, *others, gate_up, hidden, gates = experts_call(
            mixed, group_routes[layer], routers[layer].T, pieces
        )
        stored.append((value, normed, heads, keys_values, low, probs, middle, mixed, gate_up, hidden, gates))
        if layer == 0:
            value = middle + group_scatter(own, others, second_near, (), second_far)
    last_sums = (own, others)

    upstream_group = (upstream_line.reshape(HALF, D), swap_core(upstream_line).reshape(HALF, D))
    upstream = cotangent.astype(WIDE)
    router_grads, gain_grads = ([None] * LAYERS for _ in range(2))
    before_back = before_scatter = ()
    for layer in reversed(range(LAYERS)):
        query, output, pieces = weights[layer]
        value, normed, heads, keys_values, low, probs, middle, mixed, gate_up, hidden, gates = stored[layer]
        own, *others, grad_gate_up, grad_logits = experts_back_call(
            upstream_group, gate_up, gates, routers[layer], pieces, before_back
        )
        router_grads[layer] = t_dot(grad_logits[:HALF], mixed[0]) + t_dot(grad_logits[HALF:], mixed[1])
        terms = (mixed, grad_gate_up, hidden, upstream_group)
        far = expert_grads_call((3,), *terms)
        from_x = across(far[0], 1)
        from_y = across(far[1], 2)
        grad_mixed = group_scatter(own, others, before_scatter, far, (), (from_x, from_y))
        to_x0, to_x1, to_y0, to_y1 = expert_grads_call(
            (1, 2), *terms, received=[(from_y, 0, 1), (from_x, 1, 0)]
        )
        got = [(across(to_x0, 1), across(to_y0, 2)), (across(to_x1, 1), across(to_y1, 2))]
        last_part = dict(
            flips=(0,),
            mixed=mixed,
            grad_gate_up=grad_gate_up,
            hidden=hidden,
            upstream=upstream_group,
            received=[(got[e][k], 0, e) for e in range(EXP_DEV) for k in range(2)],
            layer=layer,
        )
        grad_middle, error, grad_heads, own, other, second_gain = attend_back_call(
            grad_mixed,
            middle,
            gain_rows[layer, 1],
            upstream,
            output,
            low,
            probs,
            heads,
            keys_values,
            (to_x0, to_x1, to_y0, to_y1),
        )
        grad_kv = earlier_scatter(own, other)
        joined, upstream, upstream_low, first_gain = project_back_call(
            grad_heads, grad_kv, tables, query, value, gain_rows[layer, 0], grad_middle
        )
        gain_grads[layer] = jnp.concatenate([first_gain, second_gain], axis=0)
        small = None
        if layer == 0:
            small = jnp.concatenate(
                [jnp.concatenate([router_grads[l], gain_grads[l]], axis=0) for l in range(LAYERS)], axis=0
            ).astype(LOW)
            small = small.reshape(small_lines, -1, own_rows).transpose(1, 0, 2).reshape(-1, small_size)
            small = jnp.pad(small, ((0, 0), (0, SMALL * D - small_size)))
            small = small.reshape(4, LINE, 2, SMALL, D)
        mine, others = dense_grads_call(joined, normed, low, error, small, got[0])
        if layer > 0:
            sums = dense_square_scatter(mine, others)
            upstream_group = group_gather(upstream_low)
            before_back = got[1]
            before_scatter = sums[2]
            dense_sums = sums
            second_part = last_part
    expert_grads = expert_grads_call(**second_part, earlier=mine)
    sums = dense_square_scatter(mine, others, *got[1], *expert_grads)
    expert_grads = expert_grads_call(**last_part, results=expert_grads, earlier=sums[1])
    dense_grads = [line_scatter(sums[3]), line_scatter(after(dense_sums[3], *mine))]
    last_sums = in_order(last_sums[0], jnp.concatenate(last_sums[1], axis=0))
    result = stored[-1][6] + lax.psum_scatter(
        last_sums, "cp", scatter_dimension=0, tiled=True
    ).astype(WIDE)
    small = dense_grads[0][QROWS + OROWS :].reshape(-1)[:small_size]
    small = small.reshape(LAYERS, EXPERTS + 2, own_rows).transpose(0, 2, 1)
    return (
        result,
        upstream,
        jnp.stack([grads[:QROWS] for grads in dense_grads]),
        jnp.stack([grads[QROWS : QROWS + OROWS] for grads in dense_grads]),
        small[:, :, :EXPERTS],
        small[:, :, EXPERTS:],
        *expert_grads,
    )


class AnyMesh:
    def order(self, rows):
        return jnp.arange(lax.axis_size("cp") * rows, dtype=jnp.int32)

    def group_gather(self, value):
        return lax.all_gather(value, "cp", axis=0, tiled=True)

    def group_scatter(self, terms):
        return lax.psum_scatter(
            terms.astype(LOW), "cp", scatter_dimension=0, tiled=True
        ).astype(WIDE)

    def expert_gather(self, block):
        return lax.all_gather(block, "dp", axis=1, tiled=True)

    def expert_scatter(self, terms):
        return lax.psum_scatter(terms, "dp", scatter_dimension=1, tiled=True).astype(WIDE)

    def dense_gather(self, block):
        return lax.all_gather(block, ("dp", "cp"), axis=0, tiled=True)

    def dense_scatter(self, terms):
        return lax.psum_scatter(
            terms.astype(LOW), ("dp", "cp"), scatter_dimension=0, tiled=True
        ).astype(WIDE)


def any_mesh_shards(tokens, cotangent, doc_lengths, routes, w_qkv, w_out, router, gains, w_gate_up, w_down):
    dp_size = lax.axis_size("dp")
    cp_size = lax.axis_size("cp")
    device_count = dp_size * cp_size
    move = AnyMesh()
    row_count = tokens.shape[0]
    group_rows = row_count * cp_size
    cycle_place = lax.axis_index("cp")
    expert_count = EXP_DEV * cp_size
    lengths_row = doc_lengths[0]
    my_index = cycle_place * row_count + jnp.arange(row_count, dtype=jnp.int32)
    my_segment, my_position = doc_places(my_index, lengths_row)
    cosine, sine_table = rope_tables(my_position)
    score_scale = HEAD ** (-0.5)
    key_index = move.order(row_count)
    key_segment, unused_position = doc_places(key_index, lengths_row)
    allowed = (my_segment[:, None] == key_segment[None, :]) & (
        key_index[None, :] <= my_index[:, None]
    )
    allowed = jnp.tile(allowed, (Q_PER_KV, 1))[None]

    part_rows = router.shape[1]
    small_width = expert_count + 2
    small = jnp.concatenate([router, gains], axis=2).reshape(-1)
    small_size = small.shape[0]
    small = jnp.pad(small, (0, -small_size % 2048)).reshape(-1, 128)
    small = lax.all_gather(small, ("dp", "cp"), axis=0, tiled=False).reshape(device_count, -1)
    small = small[:, :small_size].reshape(device_count, LAYERS, part_rows, small_width)
    small = small.transpose(1, 0, 2, 3).reshape(LAYERS, D, small_width)
    router_all = small[:, :, :expert_count]
    gains_all = small[:, :, expert_count:].astype(WIDE)
    route_block = routes.reshape(-1, 128)
    route_blocks = lax.all_gather(route_block, "cp", axis=0, tiled=False)
    route_blocks = route_blocks.reshape(cp_size, LAYERS, row_count, TOP)
    route_rows = route_blocks.transpose(1, 0, 2, 3).reshape(LAYERS, group_rows, TOP)
    expert_ids = jnp.arange(expert_count, dtype=jnp.int32)

    weights = []
    for layer in range(LAYERS):
        query_weight = move.dense_gather(w_qkv[layer])
        output_weight = move.dense_gather(w_out[layer])
        gate_up_weight = move.expert_gather(w_gate_up[layer])
        down_weight = move.expert_gather(w_down[layer])
        weights.append((query_weight, output_weight, gate_up_weight, down_weight))
    cotangent_group = move.group_gather(cotangent)

    def forward_layer(layer, layer_value):
        query_weight, output_weight, gate_up_weight, down_weight = weights[layer]
        normed = norm_rows(layer_value, gains_all[layer, :, 0])
        joined = dot_t(normed, query_weight)
        queries = rotate(joined[:, :HQ].reshape(row_count, HEADS, HEAD), cosine, sine_table)
        keys = rotate(
            joined[:, HQ : HQ + KVW].reshape(row_count, KV_HEADS, HEAD), cosine, sine_table
        )
        queries = heads_first(queries.reshape(row_count, HQ).astype(LOW))
        keys_values = jnp.concatenate(
            [keys.reshape(row_count, KVW), joined[:, HQ + KVW :]], axis=1
        ).astype(LOW)
        keys_values = move.group_gather(keys_values)
        key_heads = keys_values[:, :KVW].reshape(group_rows, KV_HEADS, HEAD)
        value_heads = keys_values[:, KVW:].reshape(group_rows, KV_HEADS, HEAD)
        scores = (
            jnp.einsum("kqh,nkh->kqn", queries, key_heads, preferred_element_type=WIDE)
            * score_scale
        )
        scores = jnp.where(allowed, scores, MASKED)
        top_score = jnp.max(scores, axis=-1, keepdims=True)
        shares = jnp.exp(scores - top_score)
        total = jnp.sum(shares, axis=-1, keepdims=True)
        probs = (shares / total).astype(LOW)
        attended = jnp.einsum("kqn,nkh->kqh", probs, value_heads, preferred_element_type=WIDE)
        attended = heads_last(attended)
        attended_low = attended.astype(LOW)
        middle = layer_value + dot(attended_low, output_weight)
        mixed = norm_rows(middle, gains_all[layer, :, 1])
        mixed_group = move.group_gather(mixed)
        route_group = jnp.take(
            route_rows[layer].reshape(cp_size, row_count, TOP),
            key_index[::row_count] // row_count,
            axis=0,
        ).reshape(group_rows, TOP)
        chosen = jnp.any(route_group[:, :, None] == expert_ids[None, None, :], axis=1)
        logits = jnp.where(chosen, dot(mixed_group, router_all[layer]), MASKED)
        gates = jax.nn.softmax(logits, axis=-1)
        own_gates = lax.dynamic_slice_in_dim(gates, EXP_DEV * cycle_place, EXP_DEV, 1)
        gate_up = [dot(mixed_group, gate_up_weight[e]).astype(LOW) for e in range(EXP_DEV)]
        hidden = []
        for e in range(EXP_DEV):
            gate_part = gate_up[e][:, :FF].astype(WIDE)
            up_part = gate_up[e][:, FF:].astype(WIDE)
            hidden.append(jax.nn.silu(gate_part) * up_part * own_gates[:, e : e + 1])
        hidden = jnp.concatenate(hidden, axis=1).astype(LOW)
        terms = dot(hidden, down_weight.reshape(EXP_DEV * FF, D))
        result = middle + move.group_scatter(terms)
        kept = (
            layer_value,
            normed,
            queries,
            keys_values,
            probs,
            attended,
            middle,
            mixed_group,
            gates,
            own_gates,
            gate_up,
            hidden,
        )
        return (result, kept)

    def backward_layer(layer, upstream, upstream_group, kept):
        query_weight, output_weight, gate_up_weight, down_weight = weights[layer]
        (
            layer_value,
            normed,
            queries,
            keys_values,
            probs,
            attended,
            middle,
            mixed_group,
            gates,
            own_gates,
            gate_up,
            hidden,
        ) = kept
        grad_hidden = dot_t(upstream_group, down_weight.reshape(EXP_DEV * FF, D))
        grad_gate_up = []
        grad_gates = []
        for e in range(EXP_DEV):
            gate_part = gate_up[e][:, :FF].astype(WIDE)
            up_part = gate_up[e][:, FF:].astype(WIDE)
            bare = grad_hidden[:, e * FF : (e + 1) * FF]
            logistic = jax.nn.sigmoid(gate_part)
            activated = gate_part * logistic
            grad_gates.append(jnp.sum(bare * activated * up_part, axis=1, keepdims=True))
            gated = bare * own_gates[:, e : e + 1]
            grad_gate = gated * up_part * logistic * (1.0 + gate_part * (1.0 - logistic))
            grad_gate_up.append(
                jnp.concatenate([grad_gate, gated * activated], axis=1).astype(LOW)
            )
        own_terms = own_gates * jnp.concatenate(grad_gates, axis=1)
        own_ids = EXP_DEV * cycle_place + jnp.arange(EXP_DEV, dtype=jnp.int32)
        placed = jnp.sum(
            jnp.where(own_ids[None, :, None] == expert_ids[None, None, :], own_terms[:, :, None], 0.0),
            axis=1,
        )
        grad_logits = (placed - jnp.sum(own_terms, axis=1, keepdims=True) * gates).astype(LOW)
        terms = dot_t(grad_gate_up[0], gate_up_weight[0]) + dot_t(
            grad_gate_up[1], gate_up_weight[1]
        )
        terms = terms + dot_t(grad_logits, router_all[layer])
        grad_mixed = move.group_scatter(terms)
        grad_router = t_dot(mixed_group, grad_logits)
        grad_gate_up_weight = jnp.stack(
            [t_dot(mixed_group, grad_gate_up[e]).astype(LOW) for e in range(EXP_DEV)]
        )
        grad_down_weight = t_dot(hidden, upstream_group).astype(LOW).reshape(EXP_DEV, FF, D)
        expert_grads = (
            move.expert_scatter(grad_gate_up_weight),
            move.expert_scatter(grad_down_weight),
        )

        grad_middle, grad_second_gain = norm_backward(
            middle, gains_all[layer, :, 1], grad_mixed
        )
        grad_middle = grad_middle + upstream
        grad_middle_low = grad_middle.astype(LOW)
        grad_output_weight = move.dense_scatter(t_dot(attended.astype(LOW), grad_middle_low))
        grad_attended = dot_t(grad_middle_low, output_weight).astype(LOW)
        grad_heads = heads_first(grad_attended)
        delta = jnp.sum(grad_heads.astype(WIDE) * heads_first(attended), axis=-1, keepdims=True)
        key_heads = keys_values[:, :KVW].reshape(group_rows, KV_HEADS, HEAD)
        value_heads = keys_values[:, KVW:].reshape(group_rows, KV_HEADS, HEAD)
        grad_probs = jnp.einsum(
            "kqh,nkh->kqn", grad_heads, value_heads, preferred_element_type=WIDE
        )
        grad_scores = (probs.astype(WIDE) * (grad_probs - delta) * score_scale).astype(LOW)
        grad_queries = jnp.einsum(
            "kqn,nkh->kqh", grad_scores, key_heads, preferred_element_type=WIDE
        )
        grad_keys = jnp.einsum(
            "kqn,kqh->nkh", grad_scores, queries, preferred_element_type=WIDE
        )
        grad_values = jnp.einsum(
            "kqn,kqh->nkh", probs, grad_heads, preferred_element_type=WIDE
        )
        grad_keys_values = move.group_scatter(
            jnp.concatenate(
                [grad_keys.reshape(group_rows, KVW), grad_values.reshape(group_rows, KVW)], axis=1
            )
        )
        grad_queries = rotate(
            heads_last(grad_queries).reshape(row_count, HEADS, HEAD), cosine, -sine_table
        ).reshape(row_count, HQ)
        grad_keys = rotate(
            grad_keys_values[:, :KVW].reshape(row_count, KV_HEADS, HEAD), cosine, -sine_table
        ).reshape(row_count, KVW)
        grad_joined = jnp.concatenate(
            [grad_queries, grad_keys, grad_keys_values[:, KVW:]], axis=1
        ).astype(LOW)
        grad_query_weight = t_dot(grad_joined, normed)
        grad_normed = dot(grad_joined, query_weight)
        grad_input, grad_first_gain = norm_backward(
            layer_value, gains_all[layer, :, 0], grad_normed
        )
        grad_input = grad_input + grad_middle
        small_terms = jnp.concatenate(
            [grad_router, grad_first_gain[:, None], grad_second_gain[:, None]], axis=1
        )
        return (grad_input, grad_query_weight, grad_output_weight, expert_grads, small_terms)

    layer_value = tokens.astype(WIDE)
    stored = []
    for layer in range(LAYERS):
        layer_value, kept = forward_layer(layer, layer_value)
        stored.append(kept)
    upstream = cotangent.astype(WIDE)
    upstream_group = cotangent_group
    query_grads, output_grads, expert_grads, small_terms = ([None] * LAYERS for _ in range(4))
    for layer in reversed(range(LAYERS)):
        if layer < LAYERS - 1:
            upstream_group = move.group_gather(upstream.astype(LOW))
        upstream, query_terms, output_grads[layer], expert_grads[layer], small_terms[layer] = (
            backward_layer(layer, upstream, upstream_group, stored[layer])
        )
        if layer > 0:
            query_grads[layer] = move.dense_scatter(query_terms)
    small_grads = jnp.stack(small_terms).reshape(LAYERS, device_count, part_rows, small_width)
    small_grads = small_grads.transpose(1, 0, 2, 3).reshape(device_count, -1)
    small_size = small_grads.shape[1]
    extra_rows = -(-small_size // (8 * D)) * 8
    small_grads = jnp.pad(small_grads, ((0, 0), (0, extra_rows * D - small_size)))
    query_rows = query_terms.shape[0] // device_count
    last_terms = jnp.concatenate(
        [
            query_terms.astype(LOW).reshape(device_count, query_rows, D),
            small_grads.astype(LOW).reshape(device_count, extra_rows, D),
        ],
        axis=1,
    )
    last_grads = move.dense_scatter(last_terms.reshape(-1, D))
    query_grads[0] = last_grads[:query_rows]
    small_grads = last_grads[query_rows:].reshape(-1)[:small_size]
    small_grads = small_grads.reshape(LAYERS, part_rows, small_width)
    return (
        layer_value,
        upstream,
        jnp.stack(query_grads),
        jnp.stack(output_grads),
        small_grads[:, :, :expert_count],
        small_grads[:, :, expert_count:],
        jnp.stack([pair[0] for pair in expert_grads]),
        jnp.stack([pair[1] for pair in expert_grads]),
    )


def solution(mesh):
    sizes = dict(mesh.shape)
    square_line = (sizes["dp"], sizes["cp"]) == (4, 2 * LINE)
    return jax.shard_map(
        square_line_shards if square_line else any_mesh_shards,
        mesh=mesh,
        in_specs=(
            P(("dp", "cp"), None),
            P(("dp", "cp"), None),
            P("dp", None),
            P(None, ("dp", "cp"), None),
            P(None, ("dp", "cp"), None),
            P(None, ("dp", "cp"), None),
            P(None, ("dp", "cp"), None),
            P(None, ("dp", "cp"), None),
            P(None, "cp", "dp", None),
            P(None, "cp", "dp", None),
        ),
        out_specs=(
            P(("dp", "cp"), None),
            P(("dp", "cp"), None),
            P(None, ("dp", "cp"), None),
            P(None, ("dp", "cp"), None),
            P(None, ("dp", "cp"), None),
            P(None, ("dp", "cp"), None),
            P(None, "cp", "dp", None),
            P(None, "cp", "dp", None),
        ),
        check_vma=False,
    )
```

```python
import jax
import jax.numpy as jnp
from jax import lax
from jax.experimental import pallas as pl
from jax.experimental.pallas import tpu as pltpu
from jax.sharding import PartitionSpec as P

D = 1536
HEADS = 12
KV_HEADS = 2
HEAD = 128
FF = 768
TOP = 4
EXP_DEV = 2
LAYERS = 2
DOCS = 4
HQ = 1536
KVW = 256
QKV = 2048
Q_PER_KV = 6

EPSILON = 1e-06
MASKED = -1e30
LOW = jnp.bfloat16
WIDE = jnp.float32


def inverse_rms(values):
    return lax.rsqrt(jnp.mean(values * values, axis=-1, keepdims=True) + EPSILON)


def norm_backward(values, gain, upstream):
    scale_rows = inverse_rms(values)
    weighted = gain * upstream
    inner_mean = jnp.mean(values * weighted, axis=-1, keepdims=True)
    grad_values = scale_rows * weighted - values * scale_rows * scale_rows * scale_rows * inner_mean
    grad_gain = jnp.sum(values * scale_rows * upstream, axis=0)
    return (grad_values, grad_gain)


def doc_places(token_index, lengths_row):
    starts = jnp.cumsum(lengths_row) - lengths_row
    segment = jnp.sum((token_index[:, None] >= starts[None, 1:]).astype(jnp.int32), axis=1)
    picked = segment[:, None] == jnp.arange(DOCS, dtype=jnp.int32)[None, :]
    offset = jnp.sum(jnp.where(picked, starts[None, :], 0), axis=1)
    return (segment, token_index - offset)


def rope_tables(positions):
    half_width = HEAD // 2
    frequency = jnp.exp(-jnp.log(10000.0) * 2.0 * jnp.arange(half_width, dtype=WIDE) / HEAD)
    angles = positions.astype(WIDE)[:, None] * frequency[None, :]
    return (jnp.cos(angles)[:, None, :], jnp.sin(angles)[:, None, :])


def rotate(values, cosine, sine_table):
    half_width = values.shape[-1] // 2
    former = values[..., :half_width]
    latter = values[..., half_width:]
    return jnp.concatenate(
        [former * cosine - latter * sine_table, latter * cosine + former * sine_table], axis=-1
    )


def heads_first(values):
    token_rows = values.shape[0]
    shaped = values.reshape(token_rows, KV_HEADS, Q_PER_KV, HEAD).transpose(1, 2, 0, 3)
    return shaped.reshape(KV_HEADS, Q_PER_KV * token_rows, HEAD)


def heads_last(values):
    token_rows = values.shape[1] // Q_PER_KV
    shaped = values.reshape(KV_HEADS, Q_PER_KV, token_rows, HEAD).transpose(2, 0, 1, 3)
    return shaped.reshape(token_rows, HQ)


def dot(left, right):
    return jnp.dot(left, right, preferred_element_type=WIDE)


def dot_t(left, right):
    return lax.dot_general(left, right, (((1,), (1,)), ((), ())), preferred_element_type=WIDE)


def t_dot(left, right):
    return lax.dot_general(left, right, (((0,), (0,)), ((), ())), preferred_element_type=WIDE)


ROWS = 128
LINE = 4
GROUP = 2 * LINE * ROWS
HALF = GROUP // 2
QROWS = QKV // 32
OROWS = HQ // 32
GROWS = D // 4
FROWS = FF // 4
SMALL = 16
EXPERTS = 2 * LINE * EXP_DEV


def cost(microseconds):
    return pl.CostEstimate(flops=0, bytes_accessed=int(microseconds * 3.7e6), transcendentals=0)


LIMIT = 60 * 1024 * 1024
SCALE = HEAD**-0.5


def shape(dims, dtype):
    return jax.ShapeDtypeStruct(dims, dtype)


def spec(shape, index=None):
    if index is None:
        index = lambda *unused: (0,) * len(shape)
    return pl.BlockSpec(shape, index)


ANYWHERE = pl.BlockSpec(memory_space=pl.ANY)
SCALARS = pl.BlockSpec(memory_space=pltpu.SMEM)


def after(values, *earlier):
    several = isinstance(values, (tuple, list))
    group = list(values) if several else [values]
    result = pl.pallas_call(
        lambda *refs: None,
        out_shape=[shape(v.shape, v.dtype) for v in group],
        in_specs=[ANYWHERE] * (len(group) + len(earlier)),
        out_specs=[ANYWHERE] * len(group),
        input_output_aliases={i: i for i in range(len(group))},
        name="after",
        cost_estimate=cost(0),
    )(*group, *earlier)
    return result if several else result[0]


def place_scalars():
    dp, cp = lax.axis_index("dp"), lax.axis_index("cp")
    return jnp.stack([dp, cp % 2, cp, cp // 2]).astype(jnp.int32)


def call(body, name, grid, arguments, in_specs, outs, out_specs, scratch, microseconds, earlier=()):
    count = len(arguments)
    arguments = [*arguments, *earlier]
    in_specs = [*in_specs, *[ANYWHERE] * len(earlier)]

    def whole(*refs):
        body(*refs[:count], *refs[len(arguments) :])

    return pl.pallas_call(
        whole,
        grid=grid,
        out_shape=outs,
        in_specs=in_specs,
        out_specs=out_specs,
        scratch_shapes=scratch,
        name=name,
        compiler_params=pltpu.CompilerParams(vmem_limit_bytes=LIMIT),
        cost_estimate=cost(microseconds),
    )(*arguments)


class Dense:
    def __init__(self, pieces, first_row, rows):
        self.pieces = pieces
        self.rows = rows
        self.first_row = first_row

    def arrays(self):
        return [piece[0] for piece in self.pieces]

    def copies(self, refs, places, scratch, sems):
        made = []
        for number, (ref, piece) in enumerate(zip(refs, self.pieces)):
            unused, part, flip, other, chip, chips = piece
            rows = pl.ds(self.first_row, self.rows)
            source = ref.at[:, rows] if part is None else ref.at[:, part, rows]
            target = scratch.at[places[0] ^ flip, pl.ds(chip, chips), places[1] ^ other]
            made.append(pltpu.make_async_copy(source, target, sems.at[number]))
        return made

    def scratch(self):
        return [
            pltpu.VMEM((4, LINE, 2, self.rows, D), LOW),
            pltpu.SemaphoreType.DMA((len(self.pieces),)),
        ]


def expert_copies(refs, places, gate_up, down, sems):
    made = []
    for expert in range(EXP_DEV):
        for flip in range(4):
            part = places[0] ^ flip
            far = refs[9 + expert]
            first = pl.multiple_of(part * GROWS, GROWS)
            source = refs[3 * expert + flip] if flip < 3 else far.at[pl.ds(0, GROWS)]
            made.append((source, gate_up.at[expert, pl.ds(first, GROWS)]))
            first = pl.multiple_of(part * FROWS, FROWS)
            source = refs[6 + flip].at[expert] if flip < 3 else far.at[pl.ds(GROWS, FROWS)]
            made.append((source, down.at[expert, pl.ds(first, FROWS)]))
    return [
        pltpu.make_async_copy(source, target, sems.at[number])
        for number, (source, target) in enumerate(made)
    ]


EXPERT_SCRATCH = [
    pltpu.VMEM((EXP_DEV, D, 2 * FF), LOW),
    pltpu.VMEM((EXP_DEV, FF, D), LOW),
    pltpu.SemaphoreType.DMA((16,)),
]


def logistic_of(values):
    return 0.5 * jnp.tanh(0.5 * values) + 0.5


def norm_rows(values, gain):
    return (values * inverse_rms(values) * gain).astype(LOW)


def turn(values, cosine, sine):
    return values * cosine + pltpu.roll(values, HEAD // 2, 1) * sine


def small_call(pieces):
    count = len(pieces.pieces)

    def body(places, *rest):
        refs, (out, sems) = rest[:count], rest[count:]
        copies = pieces.copies(refs, places, out, sems)
        for copy in copies:
            copy.start()
        for copy in copies:
            copy.wait()

    out = shape((4, LINE, 2, SMALL, D), LOW)
    return call(
        body,
        "small",
        (),
        [place_scalars(), *pieces.arrays()],
        [SCALARS] + [ANYWHERE] * count,
        out,
        spec(out.shape),
        [pltpu.SemaphoreType.DMA((count,))],
        0,
    )


def project_call(value, gain, query, tables, earlier=()):
    count = len(query.pieces)

    def body(places, value_ref, gain_ref, tables_ref, *rest):
        refs, (normed_ref, heads_ref, kv_ref, weight, sems, joined) = rest[:count], rest[count:]
        copies = query.copies(refs, places, weight, sems)
        for copy in copies:
            copy.start()
        normed = norm_rows(value_ref[...], gain_ref[...])
        normed_ref[...] = normed
        for copy in copies:
            copy.wait()
        for part in range(4):
            joined[part] = dot_t(normed, weight[part].reshape(8 * QROWS, D))
        cosine, sine = tables_ref[0], tables_ref[1]
        for head in range(HEADS + 2 * KV_HEADS):
            at = pl.ds(head % 4 * HEAD, HEAD)
            values = joined[head // 4, :, at]
            if head < HEADS:
                heads_ref[head] = turn(values, cosine, sine).astype(LOW)
            else:
                if head < HEADS + KV_HEADS:
                    values = turn(values, cosine, sine)
                kv_ref[:, pl.ds((head - HEADS) * HEAD, HEAD)] = values.astype(LOW)

    outs = [shape((ROWS, D), LOW), shape((HEADS, ROWS, HEAD), LOW), shape((ROWS, 2 * KVW), LOW)]
    arguments = [place_scalars(), value, gain, tables, *query.arrays()]
    return call(
        body,
        "project",
        (),
        arguments,
        [SCALARS, spec((ROWS, D)), spec((1, D)), spec((2, ROWS, HEAD))] + [ANYWHERE] * count,
        outs,
        [spec(o.shape) for o in outs],
        [*query.scratch(), pltpu.VMEM((4, ROWS, 8 * QROWS), WIDE)],
        0,
        earlier,
    )


def attend_call(value, heads, keys_values, query_meta, key_meta, output, gain, earlier=()):
    count = len(output.pieces)

    def body(places, value_ref, heads_ref, kv_own, kv_other, qmeta, kmeta, gain_ref, *rest):
        refs, (low_ref, probs_ref, middle_ref, mixed_ref, weight, sems, joined, kv_ref) = (
            rest[:count],
            rest[count:],
        )
        copies = output.copies(refs, places, weight, sems)
        for copy in copies:
            copy.start()
        kv_ref[pl.ds(0, HALF)] = kv_own[...]
        kv_ref[pl.ds(HALF, HALF)] = kv_other[...]
        allowed = (qmeta[:, 1:2] == kmeta[1:2, :]) & (kmeta[0:1, :] <= qmeta[:, 0:1])
        for head in range(HEADS):
            kv = head // Q_PER_KV
            keys = kv_ref[:, pl.ds(kv * HEAD, HEAD)]
            vals = kv_ref[:, pl.ds(KVW + kv * HEAD, HEAD)]
            scores = dot_t(heads_ref[head], keys) * SCALE
            scores = jnp.where(allowed, scores, MASKED)
            shares = jnp.exp(scores - jnp.max(scores, axis=1, keepdims=True))
            probs = (shares * (1.0 / jnp.sum(shares, axis=1, keepdims=True))).astype(LOW)
            probs_ref[head] = probs
            joined[:, pl.ds(head * HEAD, HEAD)] = dot(probs, vals).astype(LOW)
        low = joined[...]
        low_ref[...] = low
        for copy in copies:
            copy.wait()
        middle = value_ref[...] + dot(low, weight[...].reshape(HQ, D))
        middle_ref[...] = middle
        mixed_ref[...] = norm_rows(middle, gain_ref[...])

    outs = [
        shape((ROWS, HQ), LOW),
        shape((HEADS, ROWS, GROUP), LOW),
        shape((ROWS, D), WIDE),
        shape((ROWS, D), LOW),
    ]
    arguments = [
        place_scalars(),
        value,
        heads,
        *keys_values,
        query_meta,
        key_meta,
        gain,
        *output.arrays(),
    ]
    return call(
        body,
        "attend",
        (),
        arguments,
        [
            SCALARS,
            spec((ROWS, D)),
            spec((HEADS, ROWS, HEAD)),
            spec((HALF, 2 * KVW)),
            spec((HALF, 2 * KVW)),
            spec((ROWS, 2)),
            spec((2, GROUP)),
            spec((1, D)),
        ]
        + [ANYWHERE] * count,
        outs,
        [spec(o.shape) for o in outs],
        [*output.scratch(), pltpu.VMEM((ROWS, HQ), LOW), pltpu.VMEM((GROUP, 2 * KVW), LOW)],
        0,
        earlier,
    )


BLOCK = 256
STEPS = GROUP // BLOCK


def own_half(step):
    return (jnp.minimum(step, STEPS // 2 - 1), 0)


def other_half(step):
    return (jnp.maximum(step - STEPS // 2, 0), 0)


def rows_at(step):
    return (step, 0)


def take_half(step, own_ref, other_ref):
    return jnp.where(step < STEPS // 2, own_ref[...], other_ref[...])


def put_halves(step, own_ref, other_refs, values):
    @pl.when(step < STEPS // 2)
    def own():
        own_ref[...] = values

    for number, ref in enumerate(other_refs):

        @pl.when(step == STEPS // 2 + number)
        def other():
            ref[...] = values


def own_gate(gates, places, expert):
    ids = lax.broadcasted_iota(jnp.int32, gates.shape, 1)
    return jnp.sum(
        jnp.where(ids == EXP_DEV * places[2] + expert, gates, 0.0), axis=1, keepdims=True
    )


def experts_call(mixed, routes, router, pieces, earlier=()):
    def body(places, mixed_own, mixed_other, routes_ref, router_ref, *rest):
        refs, (own_ref, *other_refs, gu_ref, hidden_ref, gates_ref, gate_up, down, sems) = (
            rest[:11],
            rest[11:],
        )
        step = pl.program_id(0)
        copies = expert_copies(refs, places, gate_up, down, sems)

        @pl.when(step == 0)
        def begin():
            for copy in copies:
                copy.start()
            for copy in copies:
                copy.wait()

        mixed_rows = take_half(step, mixed_own, mixed_other)
        logits = dot(mixed_rows, router_ref[...])
        ids = lax.broadcasted_iota(jnp.int32, (BLOCK, EXPERTS), 1)
        chosen = routes_ref[:, 0:1] == ids
        for k in range(1, TOP):
            chosen = chosen | (routes_ref[:, k : k + 1] == ids)
        logits = jnp.where(chosen, logits, MASKED)
        shares = jnp.where(chosen, jnp.exp(logits - jnp.max(logits, axis=1, keepdims=True)), 0.0)
        gates = shares / jnp.sum(shares, axis=1, keepdims=True)
        gates_ref[...] = gates

        terms = None
        for expert in range(EXP_DEV):
            gu = dot(mixed_rows, gate_up[expert])
            gu_ref[:, pl.ds(expert * 2 * FF, 2 * FF)] = gu.astype(LOW)
            gate_part = gu[:, :FF]
            hidden = gate_part * logistic_of(gate_part) * gu[:, FF:]
            hidden = (hidden * own_gate(gates, places, expert)).astype(LOW)
            hidden_ref[:, pl.ds(expert * FF, FF)] = hidden
            product = dot(hidden, down[expert])
            terms = product if terms is None else terms + product
        put_halves(step, own_ref, other_refs, terms.astype(LOW))

    outs = [
        shape((HALF, D), LOW),
        shape((BLOCK, D), LOW),
        shape((BLOCK, D), LOW),
        shape((GROUP, EXP_DEV * 2 * FF), LOW),
        shape((GROUP, EXP_DEV * FF), LOW),
        shape((GROUP, EXPERTS), WIDE),
    ]
    return call(
        body,
        "experts",
        (STEPS,),
        [place_scalars(), *mixed, routes, router, *pieces],
        [
            SCALARS,
            spec((BLOCK, D), own_half),
            spec((BLOCK, D), other_half),
            spec((BLOCK, TOP), rows_at),
            spec((D, EXPERTS)),
        ]
        + [ANYWHERE] * 11,
        outs,
        [
            spec((BLOCK, D), own_half),
            spec((BLOCK, D)),
            spec((BLOCK, D)),
            spec((BLOCK, EXP_DEV * 2 * FF), rows_at),
            spec((BLOCK, EXP_DEV * FF), rows_at),
            spec((BLOCK, EXPERTS), rows_at),
        ],
        EXPERT_SCRATCH,
        8,
        earlier,
    )


def experts_back_call(upstream, gate_up_kept, gates, router, pieces, earlier=()):
    def body(places, up_own, up_other, gu_ref, gates_ref, router_ref, *rest):
        refs, (own_ref, *other_refs, grad_ref, logits_ref, gate_up, down, sems) = (
            rest[:11],
            rest[11:],
        )
        step = pl.program_id(0)
        copies = expert_copies(refs, places, gate_up, down, sems)

        @pl.when(step == 0)
        def begin():
            for copy in copies:
                copy.start()
            for copy in copies:
                copy.wait()

        upstream_rows = take_half(step, up_own, up_other)
        gates = gates_ref[...]
        ids = lax.broadcasted_iota(jnp.int32, (BLOCK, EXPERTS), 1)
        grad_logits = jnp.zeros((BLOCK, EXPERTS), WIDE)
        terms = None
        for expert in range(EXP_DEV):
            bare = dot_t(upstream_rows, down[expert])
            gate_part = gu_ref[:, pl.ds(expert * 2 * FF, FF)].astype(WIDE)
            up_part = gu_ref[:, pl.ds(expert * 2 * FF + FF, FF)].astype(WIDE)
            gate = own_gate(gates, places, expert)
            logistic = logistic_of(gate_part)
            activated = gate_part * logistic
            share = gate * jnp.sum(bare * activated * up_part, axis=1, keepdims=True)
            mine = jnp.where(ids == EXP_DEV * places[2] + expert, 1.0, 0.0)
            grad_logits = grad_logits + share * (mine - gates)
            gated = bare * gate
            grad_gate = gated * up_part * logistic * (1.0 + gate_part * (1.0 - logistic))
            grad_gate = grad_gate.astype(LOW)
            grad_up = (gated * activated).astype(LOW)
            grad_ref[:, pl.ds(expert * 2 * FF, FF)] = grad_gate
            grad_ref[:, pl.ds(expert * 2 * FF + FF, FF)] = grad_up
            grad_both = jnp.concatenate([grad_gate, grad_up], axis=1)
            product = dot_t(grad_both, gate_up[expert])
            terms = product if terms is None else terms + product
        grad_logits = grad_logits.astype(LOW)
        terms = terms + dot(grad_logits, router_ref[...])
        put_halves(step, own_ref, other_refs, terms.astype(LOW))
        logits_ref[...] = grad_logits

    outs = [
        shape((HALF, D), LOW),
        shape((BLOCK, D), LOW),
        shape((BLOCK, D), LOW),
        shape((GROUP, EXP_DEV * 2 * FF), LOW),
        shape((GROUP, EXPERTS), LOW),
    ]
    return call(
        body,
        "experts_back",
        (STEPS,),
        [place_scalars(), *upstream, gate_up_kept, gates, router, *pieces],
        [
            SCALARS,
            spec((BLOCK, D), own_half),
            spec((BLOCK, D), other_half),
            spec((BLOCK, EXP_DEV * 2 * FF), rows_at),
            spec((BLOCK, EXPERTS), rows_at),
            spec((EXPERTS, D)),
        ]
        + [ANYWHERE] * 11,
        outs,
        [
            spec((BLOCK, D), own_half),
            spec((BLOCK, D)),
            spec((BLOCK, D)),
            spec((BLOCK, EXP_DEV * 2 * FF), rows_at),
            spec((BLOCK, EXPERTS), rows_at),
        ],
        EXPERT_SCRATCH,
        8,
        earlier,
    )


def expert_grads_call(
    flips, mixed, grad_gate_up, hidden, upstream, received=(), layer=None, results=None, earlier=()
):
    last = layer is not None
    kept = () if results is None else tuple(results)
    count = len(flips)

    def body(places, *rest):
        mixed_refs, rest = rest[: 2 * count], rest[2 * count :]
        hidden_refs, rest = rest[: 2 * count], rest[2 * count :]
        grad_ref, up_own, up_other = rest[:3]
        sums, outs = rest[3 : 3 + len(received)], rest[3 + len(received) + len(kept) + len(earlier) :]
        expert = pl.program_id(0)
        for number, flip in enumerate(flips):
            gate_up = t_dot(mixed_refs[2 * number][...], grad_ref[pl.ds(0, HALF)])
            gate_up = gate_up + t_dot(mixed_refs[2 * number + 1][...], grad_ref[pl.ds(HALF, HALF)])
            both = jnp.concatenate([hidden_refs[2 * number][...], hidden_refs[2 * number + 1][...]], axis=1)
            down = t_dot(both[:HALF], up_own[...]) + t_dot(both[HALF:], up_other[...])
            part = places[0] ^ flip
            down = jnp.where(part % 2 == 0, down[:FROWS], down[2 * HEAD - FROWS :])
            for ref, (unused, whose, only) in zip(sums, received):
                if whose != number:
                    continue
                held = jnp.where(expert == only, ref[...].astype(WIDE), 0.0)
                gate_up = gate_up + held[:GROWS]
                down = down + held[GROWS:]
            if last:
                outs[0][0, 0] = gate_up
                outs[1][0, 0] = down
                continue
            gate_up = gate_up.astype(LOW)
            down = down.astype(LOW)
            for own in range(EXP_DEV):

                @pl.when(expert == own)
                def put():
                    outs[EXP_DEV * number + own][pl.ds(0, GROWS)] = gate_up
                    outs[EXP_DEV * number + own][pl.ds(GROWS, FROWS)] = down

    whole = lambda e, places: (0, 0)
    if last:
        at_layer = lambda e, places: (layer, e, 0, 0)
        outs = [shape((LAYERS, EXP_DEV, GROWS, D), WIDE), shape((LAYERS, EXP_DEV, FROWS, D), WIDE)]
        out_specs = [
            pl.BlockSpec((1, 1, GROWS, D), at_layer),
            pl.BlockSpec((1, 1, FROWS, D), at_layer),
        ]
    else:
        outs = [shape((GROWS + FROWS, D), LOW)] * (count * EXP_DEV)
        out_specs = [pl.BlockSpec((GROWS + FROWS, D), whole)] * (count * EXP_DEV)
    in_specs = []
    for flip in flips:
        in_specs += [pl.BlockSpec((HALF, GROWS), lambda e, places, flip=flip: (0, places[0] ^ flip))] * 2
    for flip in flips:
        for side in range(2):
            in_specs.append(
                pl.BlockSpec(
                    (GROUP, HEAD),
                    lambda e, places, flip=flip, side=side: (
                        0,
                        e * (FF // HEAD) + (places[0] ^ flip) * 3 // 2 + side,
                    ),
                )
            )
    in_specs += [
        pl.BlockSpec((GROUP, 2 * FF), lambda e, places: (0, e)),
        pl.BlockSpec((HALF, D), whole),
        pl.BlockSpec((HALF, D), whole),
    ]
    in_specs += [pl.BlockSpec((GROWS + FROWS, D), whole)] * len(received)
    in_specs += [ANYWHERE] * (len(kept) + len(earlier))
    first_kept = 1 + 4 * count + 3 + len(received)
    return pl.pallas_call(
        body,
        out_shape=outs,
        input_output_aliases={first_kept + i: i for i in range(len(kept))},
        grid_spec=pltpu.PrefetchScalarGridSpec(
            num_scalar_prefetch=1, grid=(EXP_DEV,), in_specs=in_specs, out_specs=out_specs
        ),
        name="expert_grads",
        compiler_params=pltpu.CompilerParams(vmem_limit_bytes=LIMIT),
        cost_estimate=cost(4 if last else 0),
    )(
        place_scalars(),
        *(list(mixed) * count),
        *([hidden] * (2 * count)),
        grad_gate_up,
        *upstream,
        *(array for array, unused, only in received),
        *kept,
        *earlier,
    )


def norm_back(values, gain, upstream):
    scale_rows = inverse_rms(values)
    weighted = gain * upstream
    inner_mean = jnp.mean(values * weighted, axis=1, keepdims=True)
    grads = scale_rows * (weighted - values * (scale_rows * scale_rows * inner_mean))
    return (grads, jnp.sum(values * scale_rows * upstream, axis=0, keepdims=True))


def attend_back_call(
    grad_mixed, middle, gain, upstream, output, low, probs, heads, keys_values, earlier=()
):
    count = len(output.pieces)

    def body(
        places, gm_ref, middle_ref, gain_ref, up_ref, low_in, probs_ref, heads_ref, kv_own, kv_other, *rest
    ):
        refs, (grad_ref, error_ref, gq_ref, own_ref, other_ref, gg_ref, weight, sems, kvs, kv_ref) = (
            rest[:count],
            rest[count:],
        )
        copies = output.copies(refs, places, weight, sems)
        for copy in copies:
            copy.start()
        kv_ref[pl.ds(0, HALF)] = kv_own[...]
        kv_ref[pl.ds(HALF, HALF)] = kv_other[...]
        grads, gain_grad = norm_back(middle_ref[...], gain_ref[...], gm_ref[...])
        gg_ref[...] = gain_grad
        grads = grads + up_ref[...]
        grad_ref[...] = grads
        error = grads.astype(LOW)
        error_ref[...] = error
        for copy in copies:
            copy.wait()
        grad_attended = dot_t(error, weight[...].reshape(HQ, D)).astype(LOW)
        for head in range(HEADS):
            kv = head // Q_PER_KV
            at = pl.ds(kv * HEAD, HEAD)
            at_values = pl.ds(KVW + kv * HEAD, HEAD)
            grad_head = grad_attended[:, head * HEAD : (head + 1) * HEAD]
            delta = jnp.sum(
                grad_head.astype(WIDE) * low_in[:, pl.ds(head * HEAD, HEAD)].astype(WIDE),
                axis=1,
                keepdims=True,
            )
            shares = probs_ref[head]
            grad_scores = dot_t(grad_head, kv_ref[:, at_values]) - delta
            grad_scores = (shares.astype(WIDE) * grad_scores * SCALE).astype(LOW)
            gq_ref[head] = dot(grad_scores, kv_ref[:, at])
            grad_keys = t_dot(grad_scores, heads_ref[head])
            grad_values = t_dot(shares, grad_head)
            if head % Q_PER_KV == 0:
                kvs[:, at] = grad_keys
                kvs[:, at_values] = grad_values
            else:
                kvs[:, at] += grad_keys
                kvs[:, at_values] += grad_values
        own_ref[...] = kvs[pl.ds(0, HALF)].astype(LOW)
        other_ref[...] = kvs[pl.ds(HALF, HALF)].astype(LOW)

    outs = [
        shape((ROWS, D), WIDE),
        shape((ROWS, D), LOW),
        shape((HEADS, ROWS, HEAD), WIDE),
        shape((HALF, 2 * KVW), LOW),
        shape((HALF, 2 * KVW), LOW),
        shape((1, D), WIDE),
    ]
    arguments = [
        place_scalars(),
        grad_mixed,
        middle,
        gain,
        upstream,
        low,
        probs,
        heads,
        *keys_values,
        *output.arrays(),
    ]
    return call(
        body,
        "attend_back",
        (),
        arguments,
        [SCALARS] + [spec(a.shape) for a in arguments[1:10]] + [ANYWHERE] * count,
        outs,
        [spec(o.shape) for o in outs],
        [*output.scratch(), pltpu.VMEM((GROUP, 2 * KVW), WIDE), pltpu.VMEM((GROUP, 2 * KVW), LOW)],
        0,
        earlier,
    )


def project_back_call(grad_heads, grad_kv, tables, query, value, gain, grad_middle, earlier=()):
    count = len(query.pieces)

    def body(places, gq_ref, gkv_ref, tables_ref, value_ref, gain_ref, gm_ref, *rest):
        refs, (joined_ref, grad_ref, low_ref, gg_ref, weight, sems) = rest[:count], rest[count:]
        copies = query.copies(refs, places, weight, sems)
        for copy in copies:
            copy.start()
        cosine, sine = tables_ref[0], -tables_ref[1]
        for head in range(HEADS + 2 * KV_HEADS):
            if head < HEADS:
                values = turn(gq_ref[head], cosine, sine)
            else:
                values = gkv_ref[:, pl.ds((head - HEADS) * HEAD, HEAD)]
                if head < HEADS + KV_HEADS:
                    values = turn(values, cosine, sine)
            joined_ref[:, pl.ds(head * HEAD, HEAD)] = values.astype(LOW)
        for copy in copies:
            copy.wait()
        grad_normed = dot(joined_ref[...], weight[...].reshape(QKV, D))
        grads, gain_grad = norm_back(value_ref[...], gain_ref[...], grad_normed)
        gg_ref[...] = gain_grad
        grads = grads + gm_ref[...]
        grad_ref[...] = grads
        low_ref[...] = grads.astype(LOW)

    outs = [
        shape((ROWS, QKV), LOW),
        shape((ROWS, D), WIDE),
        shape((ROWS, D), LOW),
        shape((1, D), WIDE),
    ]
    arguments = [
        place_scalars(),
        grad_heads,
        grad_kv,
        tables,
        value,
        gain,
        grad_middle,
        *query.arrays(),
    ]
    return call(
        body,
        "project_back",
        (),
        arguments,
        [SCALARS] + [spec(a.shape) for a in arguments[1:7]] + [ANYWHERE] * count,
        outs,
        [spec(o.shape) for o in outs],
        query.scratch(),
        0,
        earlier,
    )


def dense_grads_call(joined, normed, low, error, small, earlier=()):
    rows = QROWS + OROWS + (SMALL if small is not None else 0)

    def body(places, joined_ref, normed_ref, low_ref, error_ref, *rest):
        mine_refs, other_refs = rest[-8:-4], rest[-4:]
        flip = pl.program_id(0)
        query = t_dot(joined_ref[...], normed_ref[...]).astype(LOW).reshape(LINE, 2, QROWS, D)
        outs = t_dot(low_ref[...], error_ref[...]).astype(LOW).reshape(LINE, 2, OROWS, D)
        for core in range(2):

            def put(ref):
                ref[:, pl.ds(0, QROWS)] = query[:, core]
                ref[:, pl.ds(QROWS, OROWS)] = outs[:, core]
                if small is not None:
                    ref[:, pl.ds(QROWS + OROWS, SMALL)] = rest[0][0, :, core]

            for at in range(4):

                @pl.when((flip == at) & (places[1] == core))
                def mine():
                    put(mine_refs[at])

                @pl.when((flip == at) & (places[1] != core))
                def other():
                    put(other_refs[at])

    out = shape((LINE, rows, D), LOW)
    count = len(earlier)
    part = lambda flip, places: (0, places[0] ^ flip)
    whole = lambda flip, places: (0, 0)
    in_specs = [
        pl.BlockSpec((ROWS, QKV // 4), part),
        pl.BlockSpec((ROWS, D), whole),
        pl.BlockSpec((ROWS, HQ // 4), part),
        pl.BlockSpec((ROWS, D), whole),
    ]
    arguments = [joined, normed, low, error]
    if small is not None:
        in_specs.append(
            pl.BlockSpec((1, LINE, 2, SMALL, D), lambda flip, places: (places[0] ^ flip, 0, 0, 0, 0))
        )
        arguments.append(small)
    in_specs += [ANYWHERE] * count
    out_spec = pl.BlockSpec((LINE, rows, D), lambda flip, places: (0, 0, 0))
    grads = pl.pallas_call(
        body,
        out_shape=[out] * 8,
        grid_spec=pltpu.PrefetchScalarGridSpec(
            num_scalar_prefetch=1, grid=(4,), in_specs=in_specs, out_specs=[out_spec] * 8
        ),
        name="dense_grads",
        compiler_params=pltpu.CompilerParams(vmem_limit_bytes=LIMIT),
        cost_estimate=cost(0),
    )(place_scalars(), *arguments, *earlier)
    return (grads[:4], grads[4:])


def swap_core(value):
    return lax.ppermute(value, "cp", [(i, i ^ 1) for i in range(2 * LINE)])


def hop(value, upward, sources):
    step = 1 if upward else -1
    pairs = [(2 * z + core, 2 * (z + step) + core) for z in sources for core in range(2)]
    return lax.ppermute(value, "cp", pairs)


def leap(value, distance):
    pairs = [(i, i + 2 * distance) for i in range(2 * LINE) if 0 <= i + 2 * distance < 2 * LINE]
    return lax.ppermute(value, "cp", pairs)


def across(value, flip):
    return lax.ppermute(value, "dp", [(i, i ^ flip) for i in range(4)])


def line_gather(value, *earlier):
    place = lax.axis_index("cp") // 2
    rising, falling = value, value
    risen, fallen = [], []
    for step in range(1, LINE):
        if earlier and step == LINE - 1:
            rising, falling = after((rising, falling), *earlier)
        rising = hop(rising, True, range(step - 1, LINE - 1))
        falling = hop(falling, False, range(1, LINE - step + 1))
        risen.insert(0, rising)
        fallen.append(falling)
    every = jnp.stack(risen + [value] + fallen)
    return lax.dynamic_slice_in_dim(every, LINE - 1 - place, LINE, 0)


def leap_gather(value):
    place = lax.axis_index("cp") // 2
    every = [leap(value, LINE - 1 - i) if i != LINE - 1 else value for i in range(2 * LINE - 1)]
    return lax.dynamic_slice_in_dim(jnp.stack(every), LINE - 1 - place, LINE, 0)


def line_scatter(parts, *stages):
    place = lax.axis_index("cp") // 2

    def pick(index):
        return lax.dynamic_index_in_dim(parts, jnp.clip(index, 0, LINE - 1), 0, keepdims=False)

    rising = falling = None
    for step in range(1, LINE):
        up = pick(LINE + place - step)
        down = pick(place - LINE + step)
        if step > 1:
            up = (up.astype(WIDE) + rising.astype(WIDE)).astype(LOW)
            down = (down.astype(WIDE) + falling.astype(WIDE)).astype(LOW)
        if step <= len(stages) and stages[step - 1]:
            up, down = after((up, down), *stages[step - 1])
        rising = hop(up, True, range(step))
        falling = hop(down, False, range(LINE - step, LINE))
    return pick(place).astype(WIDE) + rising.astype(WIDE) + falling.astype(WIDE)


def group_gather(value, *earlier):
    mine = line_gather(value, *earlier)
    other = swap_core(mine)
    return (mine.reshape(HALF, -1), other.reshape(HALF, -1))


def group_scatter(own, others, *stages):
    if stages and stages[0]:
        others = after(others, *stages[0])
    other = jnp.concatenate([swap_core(part) for part in others], axis=0)
    both = (own.astype(WIDE) + other.astype(WIDE)).astype(LOW)
    return line_scatter(both.reshape(LINE, ROWS, -1), *stages[1:])


def earlier_gather(value):
    mine = jnp.stack([leap(value, 3), leap(value, 2), leap(value, 1), value])
    other = swap_core(mine)
    return (mine.reshape(HALF, -1), other.reshape(HALF, -1))


def earlier_scatter(own, other):
    both = (own.astype(WIDE) + swap_core(other).astype(WIDE)).astype(LOW).reshape(LINE, ROWS, -1)
    total = both[LINE - 1].astype(WIDE)
    for distance in range(1, LINE):
        total = total + leap(both[LINE - 1 - distance], -distance).astype(WIDE)
    return total


def square_step(value):
    return (across(value, 1), across(value, 2))


def square_far(by_x, by_y):
    half = by_x.shape[0] // 2
    return (across(by_x[:half], 2), across(by_y[half:], 1))


def dense_pieces(line, by_x, by_y, far):
    held = [
        (line, 0, 0, LINE),
        (by_x, 1, 0, LINE),
        (by_y, 2, 0, LINE),
        (far[0], 3, 0, LINE // 2),
        (far[1], 3, LINE // 2, LINE // 2),
    ]
    pieces = []
    for array, flip, chip, chips in held:
        pieces.append((array, None, flip, 0, chip, chips))
        pieces.append((swap_core(array), None, flip, 1, chip, chips))
    return pieces


def dense_square_scatter(mine, others, *earlier):
    received = [swap_core(other) for other in others]

    def piece(flip):
        return mine[flip].astype(WIDE) + received[flip].astype(WIDE)

    half = LINE // 2
    far = after(piece(3).astype(LOW), *earlier)
    from_x = across(far[:half], 1)
    from_y = across(far[half:], 2)
    to_x, to_y = piece(1), piece(2)
    to_x = jnp.concatenate([to_x[:half], to_x[half:] + from_y.astype(WIDE)], axis=0).astype(LOW)
    to_y = jnp.concatenate([to_y[:half] + from_x.astype(WIDE), to_y[half:]], axis=0).astype(LOW)
    got_x = across(to_x, 1)
    got_y = across(to_y, 2)
    plane = piece(0) + got_x.astype(WIDE) + got_y.astype(WIDE)
    return ((from_x, from_y), (to_x, to_y), (got_x, got_y), plane.astype(LOW))


def in_order(own, other):
    own, other = (rows.reshape(LINE, 1, ROWS, -1) for rows in (own, other))
    first = lax.axis_index("cp") % 2 == 0
    rows = jnp.where(
        first, jnp.concatenate([own, other], axis=1), jnp.concatenate([other, own], axis=1)
    )
    return rows.reshape(GROUP, -1)


def square_line_shards(
    tokens, cotangent, doc_lengths, routes, w_qkv, w_out, router, gains, w_gate_up, w_down
):
    dp_place = lax.axis_index("dp")
    cp_place = lax.axis_index("cp")
    core = cp_place % 2
    chip = cp_place // 2
    lengths_row = doc_lengths[0]
    row_ids = jnp.arange(ROWS, dtype=jnp.int32)
    my_index = cp_place * ROWS + row_ids
    my_segment, my_position = doc_places(my_index, lengths_row)
    query_meta = jnp.stack([my_index, my_segment], axis=1)
    back = jnp.arange(LINE, dtype=jnp.int32) - (LINE - 1) + chip
    blocks = jnp.concatenate([2 * back + core, 2 * back + 1 - core])
    blocks = jnp.where(jnp.concatenate([back, back]) < 0, 4 * LINE, blocks)
    key_index = (blocks[:, None] * ROWS + row_ids[None, :]).reshape(-1)
    key_segment, unused_position = doc_places(key_index, lengths_row)
    key_meta = jnp.stack([key_index, key_segment])
    cosine, sine = rope_tables(my_position)
    cosine, sine = cosine[:, 0], sine[:, 0]
    tables = jnp.stack(
        [jnp.concatenate([cosine, cosine], axis=1), jnp.concatenate([-sine, sine], axis=1)]
    )

    small_lines = LAYERS * (EXPERTS + 2)
    own_rows = router.shape[1]
    small = jnp.concatenate([router, gains], axis=2).transpose(0, 2, 1).reshape(-1)
    small_size = small.shape[0]
    small_rows = -(-small_size // D)
    small = jnp.pad(small, (0, small_rows * D - small_size)).reshape(small_rows, D)
    route_numbers = routes.reshape(-1).astype(LOW)
    route_size = route_numbers.shape[0]
    route_numbers = jnp.pad(route_numbers, (0, D - route_size)).reshape(1, D)
    small = jnp.concatenate([small, route_numbers], axis=0)
    small = jnp.pad(small, ((0, SMALL - small_rows - 1), (0, 0)))

    own_gate_ups = [[w_gate_up[l, e] for e in range(EXP_DEV)] for l in range(LAYERS)]
    own_downs = [w_down[l] for l in range(LAYERS)]
    gate_ups = [[square_step(own_gate_ups[0][0])], []]
    first = line_gather(jnp.concatenate([w_qkv[0], w_out[0], small], axis=0))
    second = line_gather(after(jnp.concatenate([w_qkv[1], w_out[1], cotangent], axis=0), first))
    first = after(first, *gate_ups[0][0])
    dense_rows = QROWS + OROWS
    upstream_line = second[:, dense_rows:]
    second = second[:, :dense_rows]
    first_near = square_step(first)
    first_far = square_far(*first_near)
    pieces = dense_pieces(first, *first_near, first_far)
    query, output = Dense(pieces, 0, QROWS), Dense(pieces, QROWS, OROWS)
    small = small_call(Dense(pieces, dense_rows, SMALL))

    def expert_weights(layer, first, more, down, far):
        own = own_gate_ups[layer]
        return [own[0], *first, own[1], *more, own_downs[layer], *down, *far]

    def experts_far(first, more, down):
        by_x = jnp.concatenate([first[0], down[0][0]], axis=0)
        by_y = jnp.concatenate([more[1], down[1][1]], axis=0)
        by_x, by_y = after((by_x, by_y), *more, *down)
        return (across(by_x, 2), across(by_y, 1))

    own_gate_ups[0][1] = after(own_gate_ups[0][1], *first_far)
    gate_ups[0].append(square_step(own_gate_ups[0][1]))
    own_downs[0] = after(own_downs[0], *first_far)
    downs = [square_step(own_downs[0])]
    fars = [experts_far(*gate_ups[0], downs[0])]
    weights = [(query, output, expert_weights(0, *gate_ups[0], downs[0], fars[0]))]
    second = after(second, *fars[0])
    second_near = square_step(second)
    second_far = square_far(*second_near)
    pieces = dense_pieces(second, *second_near, second_far)
    query, output = Dense(pieces, 0, QROWS), Dense(pieces, QROWS, OROWS)
    own_gate_ups[1][0] = after(own_gate_ups[1][0], *second_far)
    gate_ups[1].append(square_step(own_gate_ups[1][0]))
    own_gate_ups[1][1] = after(own_gate_ups[1][1], *gate_ups[1][0])
    gate_ups[1].append(square_step(own_gate_ups[1][1]))
    own_downs[1] = after(own_downs[1], *gate_ups[1][0])
    downs.append(square_step(own_downs[1]))
    fars.append(experts_far(*gate_ups[1], downs[1]))
    weights.append((query, output, expert_weights(1, *gate_ups[1], downs[1], fars[1])))

    shared = small.reshape(-1, SMALL, D)
    lines = shared[:, :small_rows].reshape(-1, small_rows * D)[:, :small_size]
    lines = lines.reshape(-1, small_lines, own_rows).transpose(1, 0, 2).reshape(small_lines, D)
    lines = lines.reshape(LAYERS, EXPERTS + 2, D)
    routers = lines[:, :EXPERTS]
    gain_rows = lines[:, EXPERTS:].astype(WIDE)[:, :, None]
    numbers = lax.dynamic_index_in_dim(small, dp_place, 0, keepdims=False)
    numbers = numbers[:, :, small_rows, :route_size]
    numbers = jnp.where(core == 0, numbers, numbers[:, ::-1]).astype(jnp.int32)
    numbers = numbers.reshape(LINE, 2, LAYERS, ROWS, TOP).transpose(2, 1, 0, 3, 4)
    group_routes = numbers.reshape(LAYERS, GROUP, TOP)

    value = tokens.astype(WIDE)
    before_project = [(), gate_ups[1][0]]
    before_attend = [(upstream_line, routers, group_routes), ()]
    stored = []
    for layer in range(LAYERS):
        query, output, pieces = weights[layer]
        normed, heads, kv = project_call(
            value, gain_rows[layer, 0], query, tables, before_project[layer]
        )
        keys_values = earlier_gather(kv)
        low, probs, middle, mixed = attend_call(
            value,
            heads,
            keys_values,
            query_meta,
            key_meta,
            output,
            gain_rows[layer, 1],
            before_attend[layer],
        )
        mixed = group_gather(mixed, *(fars[0] if layer == 0 else ()))
        own, *others, gate_up, hidden, gates = experts_call(
            mixed, group_routes[layer], routers[layer].T, pieces
        )
        stored.append((value, normed, heads, keys_values, low, probs, middle, mixed, gate_up, hidden, gates))
        if layer == 0:
            value = middle + group_scatter(own, others, second_near, (), second_far)
    last_sums = (own, others)

    upstream_group = (upstream_line.reshape(HALF, D), swap_core(upstream_line).reshape(HALF, D))
    upstream = cotangent.astype(WIDE)
    router_grads, gain_grads = ([None] * LAYERS for _ in range(2))
    before_back = before_scatter = ()
    for layer in reversed(range(LAYERS)):
        query, output, pieces = weights[layer]
        value, normed, heads, keys_values, low, probs, middle, mixed, gate_up, hidden, gates = stored[layer]
        own, *others, grad_gate_up, grad_logits = experts_back_call(
            upstream_group, gate_up, gates, routers[layer], pieces, before_back
        )
        router_grads[layer] = t_dot(grad_logits[:HALF], mixed[0]) + t_dot(grad_logits[HALF:], mixed[1])
        terms = (mixed, grad_gate_up, hidden, upstream_group)
        far = expert_grads_call((3,), *terms)
        from_x = across(far[0], 1)
        from_y = across(far[1], 2)
        grad_mixed = group_scatter(own, others, before_scatter, far, (), (from_x, from_y))
        to_x0, to_x1, to_y0, to_y1 = expert_grads_call(
            (1, 2), *terms, received=[(from_y, 0, 1), (from_x, 1, 0)]
        )
        got = [(across(to_x0, 1), across(to_y0, 2)), (across(to_x1, 1), across(to_y1, 2))]
        last_part = dict(
            flips=(0,),
            mixed=mixed,
            grad_gate_up=grad_gate_up,
            hidden=hidden,
            upstream=upstream_group,
            received=[(got[e][k], 0, e) for e in range(EXP_DEV) for k in range(2)],
            layer=layer,
        )
        grad_middle, error, grad_heads, own, other, second_gain = attend_back_call(
            grad_mixed,
            middle,
            gain_rows[layer, 1],
            upstream,
            output,
            low,
            probs,
            heads,
            keys_values,
            (to_x0, to_x1, to_y0, to_y1),
        )
        grad_kv = earlier_scatter(own, other)
        joined, upstream, upstream_low, first_gain = project_back_call(
            grad_heads, grad_kv, tables, query, value, gain_rows[layer, 0], grad_middle
        )
        gain_grads[layer] = jnp.concatenate([first_gain, second_gain], axis=0)
        small = None
        if layer == 0:
            small = jnp.concatenate(
                [jnp.concatenate([router_grads[l], gain_grads[l]], axis=0) for l in range(LAYERS)], axis=0
            ).astype(LOW)
            small = small.reshape(small_lines, -1, own_rows).transpose(1, 0, 2).reshape(-1, small_size)
            small = jnp.pad(small, ((0, 0), (0, SMALL * D - small_size)))
            small = small.reshape(4, LINE, 2, SMALL, D)
        mine, others = dense_grads_call(joined, normed, low, error, small, got[0])
        if layer > 0:
            sums = dense_square_scatter(mine, others)
            upstream_group = group_gather(upstream_low)
            before_back = got[1]
            before_scatter = sums[2]
            dense_sums = sums
            second_part = last_part
    sums = dense_square_scatter(mine, others)
    expert_grads = expert_grads_call(**second_part, earlier=sums[1])
    late_x, late_y = after((to_x1, to_y1), *sums[2])
    got = (across(late_x, 1), across(late_y, 2))
    last_part["received"] = last_part["received"][:2] + [(part, 0, 1) for part in got]
    plane = after(sums[3], *expert_grads)
    expert_grads = expert_grads_call(**last_part, results=expert_grads)
    dense_grads = [line_scatter(plane, (), (), got), line_scatter(after(dense_sums[3], *mine))]
    last_sums = in_order(last_sums[0], jnp.concatenate(last_sums[1], axis=0))
    result = stored[-1][6] + lax.psum_scatter(
        last_sums, "cp", scatter_dimension=0, tiled=True
    ).astype(WIDE)
    small = dense_grads[0][QROWS + OROWS :].reshape(-1)[:small_size]
    small = small.reshape(LAYERS, EXPERTS + 2, own_rows).transpose(0, 2, 1)
    return (
        result,
        upstream,
        jnp.stack([grads[:QROWS] for grads in dense_grads]),
        jnp.stack([grads[QROWS : QROWS + OROWS] for grads in dense_grads]),
        small[:, :, :EXPERTS],
        small[:, :, EXPERTS:],
        *expert_grads,
    )


class AnyMesh:
    def order(self, rows):
        return jnp.arange(lax.axis_size("cp") * rows, dtype=jnp.int32)

    def group_gather(self, value):
        return lax.all_gather(value, "cp", axis=0, tiled=True)

    def group_scatter(self, terms):
        return lax.psum_scatter(
            terms.astype(LOW), "cp", scatter_dimension=0, tiled=True
        ).astype(WIDE)

    def expert_gather(self, block):
        return lax.all_gather(block, "dp", axis=1, tiled=True)

    def expert_scatter(self, terms):
        return lax.psum_scatter(terms, "dp", scatter_dimension=1, tiled=True).astype(WIDE)

    def dense_gather(self, block):
        return lax.all_gather(block, ("dp", "cp"), axis=0, tiled=True)

    def dense_scatter(self, terms):
        return lax.psum_scatter(
            terms.astype(LOW), ("dp", "cp"), scatter_dimension=0, tiled=True
        ).astype(WIDE)


def any_mesh_shards(tokens, cotangent, doc_lengths, routes, w_qkv, w_out, router, gains, w_gate_up, w_down):
    dp_size = lax.axis_size("dp")
    cp_size = lax.axis_size("cp")
    device_count = dp_size * cp_size
    move = AnyMesh()
    row_count = tokens.shape[0]
    group_rows = row_count * cp_size
    cycle_place = lax.axis_index("cp")
    expert_count = EXP_DEV * cp_size
    lengths_row = doc_lengths[0]
    my_index = cycle_place * row_count + jnp.arange(row_count, dtype=jnp.int32)
    my_segment, my_position = doc_places(my_index, lengths_row)
    cosine, sine_table = rope_tables(my_position)
    score_scale = HEAD ** (-0.5)
    key_index = move.order(row_count)
    key_segment, unused_position = doc_places(key_index, lengths_row)
    allowed = (my_segment[:, None] == key_segment[None, :]) & (
        key_index[None, :] <= my_index[:, None]
    )
    allowed = jnp.tile(allowed, (Q_PER_KV, 1))[None]

    part_rows = router.shape[1]
    small_width = expert_count + 2
    small = jnp.concatenate([router, gains], axis=2).reshape(-1)
    small_size = small.shape[0]
    small = jnp.pad(small, (0, -small_size % 2048)).reshape(-1, 128)
    small = lax.all_gather(small, ("dp", "cp"), axis=0, tiled=False).reshape(device_count, -1)
    small = small[:, :small_size].reshape(device_count, LAYERS, part_rows, small_width)
    small = small.transpose(1, 0, 2, 3).reshape(LAYERS, D, small_width)
    router_all = small[:, :, :expert_count]
    gains_all = small[:, :, expert_count:].astype(WIDE)
    route_block = routes.reshape(-1, 128)
    route_blocks = lax.all_gather(route_block, "cp", axis=0, tiled=False)
    route_blocks = route_blocks.reshape(cp_size, LAYERS, row_count, TOP)
    route_rows = route_blocks.transpose(1, 0, 2, 3).reshape(LAYERS, group_rows, TOP)
    expert_ids = jnp.arange(expert_count, dtype=jnp.int32)

    weights = []
    for layer in range(LAYERS):
        query_weight = move.dense_gather(w_qkv[layer])
        output_weight = move.dense_gather(w_out[layer])
        gate_up_weight = move.expert_gather(w_gate_up[layer])
        down_weight = move.expert_gather(w_down[layer])
        weights.append((query_weight, output_weight, gate_up_weight, down_weight))
    cotangent_group = move.group_gather(cotangent)

    def forward_layer(layer, layer_value):
        query_weight, output_weight, gate_up_weight, down_weight = weights[layer]
        normed = norm_rows(layer_value, gains_all[layer, :, 0])
        joined = dot_t(normed, query_weight)
        queries = rotate(joined[:, :HQ].reshape(row_count, HEADS, HEAD), cosine, sine_table)
        keys = rotate(
            joined[:, HQ : HQ + KVW].reshape(row_count, KV_HEADS, HEAD), cosine, sine_table
        )
        queries = heads_first(queries.reshape(row_count, HQ).astype(LOW))
        keys_values = jnp.concatenate(
            [keys.reshape(row_count, KVW), joined[:, HQ + KVW :]], axis=1
        ).astype(LOW)
        keys_values = move.group_gather(keys_values)
        key_heads = keys_values[:, :KVW].reshape(group_rows, KV_HEADS, HEAD)
        value_heads = keys_values[:, KVW:].reshape(group_rows, KV_HEADS, HEAD)
        scores = (
            jnp.einsum("kqh,nkh->kqn", queries, key_heads, preferred_element_type=WIDE)
            * score_scale
        )
        scores = jnp.where(allowed, scores, MASKED)
        top_score = jnp.max(scores, axis=-1, keepdims=True)
        shares = jnp.exp(scores - top_score)
        total = jnp.sum(shares, axis=-1, keepdims=True)
        probs = (shares / total).astype(LOW)
        attended = jnp.einsum("kqn,nkh->kqh", probs, value_heads, preferred_element_type=WIDE)
        attended = heads_last(attended)
        attended_low = attended.astype(LOW)
        middle = layer_value + dot(attended_low, output_weight)
        mixed = norm_rows(middle, gains_all[layer, :, 1])
        mixed_group = move.group_gather(mixed)
        route_group = jnp.take(
            route_rows[layer].reshape(cp_size, row_count, TOP),
            key_index[::row_count] // row_count,
            axis=0,
        ).reshape(group_rows, TOP)
        chosen = jnp.any(route_group[:, :, None] == expert_ids[None, None, :], axis=1)
        logits = jnp.where(chosen, dot(mixed_group, router_all[layer]), MASKED)
        gates = jax.nn.softmax(logits, axis=-1)
        own_gates = lax.dynamic_slice_in_dim(gates, EXP_DEV * cycle_place, EXP_DEV, 1)
        gate_up = [dot(mixed_group, gate_up_weight[e]).astype(LOW) for e in range(EXP_DEV)]
        hidden = []
        for e in range(EXP_DEV):
            gate_part = gate_up[e][:, :FF].astype(WIDE)
            up_part = gate_up[e][:, FF:].astype(WIDE)
            hidden.append(jax.nn.silu(gate_part) * up_part * own_gates[:, e : e + 1])
        hidden = jnp.concatenate(hidden, axis=1).astype(LOW)
        terms = dot(hidden, down_weight.reshape(EXP_DEV * FF, D))
        result = middle + move.group_scatter(terms)
        kept = (
            layer_value,
            normed,
            queries,
            keys_values,
            probs,
            attended,
            middle,
            mixed_group,
            gates,
            own_gates,
            gate_up,
            hidden,
        )
        return (result, kept)

    def backward_layer(layer, upstream, upstream_group, kept):
        query_weight, output_weight, gate_up_weight, down_weight = weights[layer]
        (
            layer_value,
            normed,
            queries,
            keys_values,
            probs,
            attended,
            middle,
            mixed_group,
            gates,
            own_gates,
            gate_up,
            hidden,
        ) = kept
        grad_hidden = dot_t(upstream_group, down_weight.reshape(EXP_DEV * FF, D))
        grad_gate_up = []
        grad_gates = []
        for e in range(EXP_DEV):
            gate_part = gate_up[e][:, :FF].astype(WIDE)
            up_part = gate_up[e][:, FF:].astype(WIDE)
            bare = grad_hidden[:, e * FF : (e + 1) * FF]
            logistic = jax.nn.sigmoid(gate_part)
            activated = gate_part * logistic
            grad_gates.append(jnp.sum(bare * activated * up_part, axis=1, keepdims=True))
            gated = bare * own_gates[:, e : e + 1]
            grad_gate = gated * up_part * logistic * (1.0 + gate_part * (1.0 - logistic))
            grad_gate_up.append(
                jnp.concatenate([grad_gate, gated * activated], axis=1).astype(LOW)
            )
        own_terms = own_gates * jnp.concatenate(grad_gates, axis=1)
        own_ids = EXP_DEV * cycle_place + jnp.arange(EXP_DEV, dtype=jnp.int32)
        placed = jnp.sum(
            jnp.where(own_ids[None, :, None] == expert_ids[None, None, :], own_terms[:, :, None], 0.0),
            axis=1,
        )
        grad_logits = (placed - jnp.sum(own_terms, axis=1, keepdims=True) * gates).astype(LOW)
        terms = dot_t(grad_gate_up[0], gate_up_weight[0]) + dot_t(
            grad_gate_up[1], gate_up_weight[1]
        )
        terms = terms + dot_t(grad_logits, router_all[layer])
        grad_mixed = move.group_scatter(terms)
        grad_router = t_dot(mixed_group, grad_logits)
        grad_gate_up_weight = jnp.stack(
            [t_dot(mixed_group, grad_gate_up[e]).astype(LOW) for e in range(EXP_DEV)]
        )
        grad_down_weight = t_dot(hidden, upstream_group).astype(LOW).reshape(EXP_DEV, FF, D)
        expert_grads = (
            move.expert_scatter(grad_gate_up_weight),
            move.expert_scatter(grad_down_weight),
        )

        grad_middle, grad_second_gain = norm_backward(
            middle, gains_all[layer, :, 1], grad_mixed
        )
        grad_middle = grad_middle + upstream
        grad_middle_low = grad_middle.astype(LOW)
        grad_output_weight = move.dense_scatter(t_dot(attended.astype(LOW), grad_middle_low))
        grad_attended = dot_t(grad_middle_low, output_weight).astype(LOW)
        grad_heads = heads_first(grad_attended)
        delta = jnp.sum(grad_heads.astype(WIDE) * heads_first(attended), axis=-1, keepdims=True)
        key_heads = keys_values[:, :KVW].reshape(group_rows, KV_HEADS, HEAD)
        value_heads = keys_values[:, KVW:].reshape(group_rows, KV_HEADS, HEAD)
        grad_probs = jnp.einsum(
            "kqh,nkh->kqn", grad_heads, value_heads, preferred_element_type=WIDE
        )
        grad_scores = (probs.astype(WIDE) * (grad_probs - delta) * score_scale).astype(LOW)
        grad_queries = jnp.einsum(
            "kqn,nkh->kqh", grad_scores, key_heads, preferred_element_type=WIDE
        )
        grad_keys = jnp.einsum(
            "kqn,kqh->nkh", grad_scores, queries, preferred_element_type=WIDE
        )
        grad_values = jnp.einsum(
            "kqn,kqh->nkh", probs, grad_heads, preferred_element_type=WIDE
        )
        grad_keys_values = move.group_scatter(
            jnp.concatenate(
                [grad_keys.reshape(group_rows, KVW), grad_values.reshape(group_rows, KVW)], axis=1
            )
        )
        grad_queries = rotate(
            heads_last(grad_queries).reshape(row_count, HEADS, HEAD), cosine, -sine_table
        ).reshape(row_count, HQ)
        grad_keys = rotate(
            grad_keys_values[:, :KVW].reshape(row_count, KV_HEADS, HEAD), cosine, -sine_table
        ).reshape(row_count, KVW)
        grad_joined = jnp.concatenate(
            [grad_queries, grad_keys, grad_keys_values[:, KVW:]], axis=1
        ).astype(LOW)
        grad_query_weight = t_dot(grad_joined, normed)
        grad_normed = dot(grad_joined, query_weight)
        grad_input, grad_first_gain = norm_backward(
            layer_value, gains_all[layer, :, 0], grad_normed
        )
        grad_input = grad_input + grad_middle
        small_terms = jnp.concatenate(
            [grad_router, grad_first_gain[:, None], grad_second_gain[:, None]], axis=1
        )
        return (grad_input, grad_query_weight, grad_output_weight, expert_grads, small_terms)

    layer_value = tokens.astype(WIDE)
    stored = []
    for layer in range(LAYERS):
        layer_value, kept = forward_layer(layer, layer_value)
        stored.append(kept)
    upstream = cotangent.astype(WIDE)
    upstream_group = cotangent_group
    query_grads, output_grads, expert_grads, small_terms = ([None] * LAYERS for _ in range(4))
    for layer in reversed(range(LAYERS)):
        if layer < LAYERS - 1:
            upstream_group = move.group_gather(upstream.astype(LOW))
        upstream, query_terms, output_grads[layer], expert_grads[layer], small_terms[layer] = (
            backward_layer(layer, upstream, upstream_group, stored[layer])
        )
        if layer > 0:
            query_grads[layer] = move.dense_scatter(query_terms)
    small_grads = jnp.stack(small_terms).reshape(LAYERS, device_count, part_rows, small_width)
    small_grads = small_grads.transpose(1, 0, 2, 3).reshape(device_count, -1)
    small_size = small_grads.shape[1]
    extra_rows = -(-small_size // (8 * D)) * 8
    small_grads = jnp.pad(small_grads, ((0, 0), (0, extra_rows * D - small_size)))
    query_rows = query_terms.shape[0] // device_count
    last_terms = jnp.concatenate(
        [
            query_terms.astype(LOW).reshape(device_count, query_rows, D),
            small_grads.astype(LOW).reshape(device_count, extra_rows, D),
        ],
        axis=1,
    )
    last_grads = move.dense_scatter(last_terms.reshape(-1, D))
    query_grads[0] = last_grads[:query_rows]
    small_grads = last_grads[query_rows:].reshape(-1)[:small_size]
    small_grads = small_grads.reshape(LAYERS, part_rows, small_width)
    return (
        layer_value,
        upstream,
        jnp.stack(query_grads),
        jnp.stack(output_grads),
        small_grads[:, :, :expert_count],
        small_grads[:, :, expert_count:],
        jnp.stack([pair[0] for pair in expert_grads]),
        jnp.stack([pair[1] for pair in expert_grads]),
    )


def solution(mesh):
    sizes = dict(mesh.shape)
    square_line = (sizes["dp"], sizes["cp"]) == (4, 2 * LINE)
    return jax.shard_map(
        square_line_shards if square_line else any_mesh_shards,
        mesh=mesh,
        in_specs=(
            P(("dp", "cp"), None),
            P(("dp", "cp"), None),
            P("dp", None),
            P(None, ("dp", "cp"), None),
            P(None, ("dp", "cp"), None),
            P(None, ("dp", "cp"), None),
            P(None, ("dp", "cp"), None),
            P(None, ("dp", "cp"), None),
            P(None, "cp", "dp", None),
            P(None, "cp", "dp", None),
        ),
        out_specs=(
            P(("dp", "cp"), None),
            P(("dp", "cp"), None),
            P(None, ("dp", "cp"), None),
            P(None, ("dp", "cp"), None),
            P(None, ("dp", "cp"), None),
            P(None, ("dp", "cp"), None),
            P(None, "cp", "dp", None),
            P(None, "cp", "dp", None),
        ),
        check_vma=False,
    )
```
